32 devices in a mesh: row: 8 (over z, x), col: 4 (over y, core).
Axes of the slice: x: 2, y: 2, z: 4, core: 2. Of those that a mesh axis runs over, the one named last changes fastest.
Arguments:
- basis_now: float32 [8192, 128], P(('row', 'col')), may hold values from -6 to 6
- basis_prev: float32 [8192, 128], P(('row', 'col')), may hold values from -6 to 6
- coupling: float32 [128, 128], replicated, may hold values from -0.875 to 0.875
- tiles: bfloat16 [8, 4, 16, 128, 128], P('row', 'col'), may hold values from -0.1875 to 0.1875
- tile_rows: int32 [8, 4, 16], P('row', 'col'), may hold values from 0 to 15
- tile_cols: int32 [8, 4, 16], P('row', 'col'), may hold values from 0 to 7
- tile_counts: int32 [8, 4], P('row', 'col'), may hold values from 4 to 16, as said below
Outputs:
- basis: float32 [8192, 128], P(('row', 'col'))
- projection: float32 [128, 128], replicated
- rfactor: float32 [128, 128], replicated
The draws below stay inside these ranges and needn't reach their ends.
Inputs may be any that keep to these rules, and one draw needn't show every extreme that they name: Each device uses the first tile_counts of its 16 tile slots; some device uses all of them.
All inputs are finite; a program needn't handle non-finite values.
Results may differ from the reference program's by a relative error of at most 0.0033.
Values may be sent and summed in bfloat16 or wider, within the bound.
No kernel may reach another device: no remote copies, remote signals or barrier semaphores. Data moves between devices by JAX's collectives and lax.ppermute only.
A program may use at most 64 MiB of HBM per device.

```python
import jax
import jax.numpy as jnp
from jax import lax

B = 128
TILE = 128
NV = 256
TMAX = 16
NROWS = 8192
RTILES = 16
CTILES = 8
N_ROW = 8
N_COL = 4


def draw_tile_counts(key, part):
    key_counts, key_full = jax.random.split(key)
    counts = jax.random.randint(key_counts, (N_ROW * N_COL,), TMAX // 4, TMAX + 1)
    fullest = jax.random.randint(key_full, (), 0, N_ROW * N_COL)
    flattened = jnp.where(jnp.arange(N_ROW * N_COL) == fullest, TMAX, counts)
    return flattened.reshape(N_ROW, N_COL).astype(jnp.int32)


def place_ends(result, rng, low, top_value):
    dims = result.shape
    place = [jax.random.randint(jax.random.fold_in(rng, axis), (), 0, dims[axis]) for axis in range(len(dims))]
    result = result.at[tuple(place)].set(low)
    longest = dims.index(max(dims))
    place[longest] = (place[longest] + 1) % dims[longest]
    return result.at[tuple(place)].set(top_value)


def steps_of(rng, dims, pieces, least, top_value):
    def one(position, shards_of):
        draws = jax.random.uniform(jax.random.fold_in(jax.random.fold_in(rng, 6), position), (shards_of,), jnp.float32, least / len(pieces), top_value / len(pieces))
        return jnp.repeat(jnp.exp(draws), dims[position] // shards_of).reshape((-1,) + (1,) * (len(dims) - position - 1))

    level = one(*pieces[0])
    for cut in pieces[1:]:
        level = level * one(*cut)
    return level


def bell_draw(key, shape, spread, limit, cuts=(), kind=jnp.bfloat16):
    result = jax.random.normal(key, shape, jnp.float32) * spread
    if len(cuts) > 0:
        result = steps_of(key, shape, cuts, -0.22, 0.18) * result
    return jnp.clip(result, min=-limit, max=limit).astype(kind)


def setup_inputs(seed: int = 0) -> dict:
    key_of = jax.random.split(jax.random.key(seed), 8)
    basis_now = bell_draw(key_of[0], (NROWS, B), 1.0, 6.0, ((0, 32),), jnp.float32)
    basis_prev = bell_draw(key_of[1], (NROWS, B), 1.0, 6.0, ((0, 32),), jnp.float32)
    coupling = bell_draw(key_of[2], (B, B), (0.7 * B ** -0.5), 0.875, (), jnp.float32)
    tiles = bell_draw(key_of[3], (N_ROW, N_COL, TMAX, TILE, TILE), (TMAX * TILE * TILE // NV) ** -0.5, 0.1875, ((0, 8), (1, 4)))
    tile_rows = place_ends(jax.random.randint(key_of[4], (N_ROW, N_COL, TMAX), 0, RTILES), jax.random.fold_in(key_of[4], 1), 0, RTILES - 1).astype(jnp.int32)
    tile_cols = place_ends(jax.random.randint(key_of[5], (N_ROW, N_COL, TMAX), 0, CTILES), jax.random.fold_in(key_of[5], 1), 0, CTILES - 1).astype(jnp.int32)
    tile_counts = draw_tile_counts(jax.random.fold_in(key_of[7], 71), 0)
    return dict(basis_now=basis_now, basis_prev=basis_prev, coupling=coupling, tiles=tiles, tile_rows=tile_rows, tile_cols=tile_cols, tile_counts=tile_counts)


HIGHEST = lax.Precision.HIGHEST

def upper_cholesky(gram):
    return jnp.linalg.cholesky(gram).T

def lower_inverse(lower_part):
    identity = jnp.eye(lower_part.shape[0], dtype=lower_part.dtype)
    return jax.scipy.linalg.solve_triangular(lower_part, identity, lower=True)

def tile_product(tile_block, row_ids, col_ids, tile_total, column_basis):
    stacked = column_basis.reshape(-1, TILE, B)
    chosen = stacked[col_ids]
    products = jnp.einsum('tij,tjb->tib', tile_block.astype(jnp.float32), chosen.astype(jnp.float32))
    usable = jnp.arange(TMAX, dtype=jnp.int32) < tile_total
    selector = (row_ids[None, :] == jnp.arange(RTILES, dtype=jnp.int32)[:, None]) & usable[None, :]
    partial_value = jnp.einsum('rt,tib->rib', selector.astype(jnp.float32), products, precision=HIGHEST)
    return partial_value.reshape(RTILES * TILE, B)

def reference(basis_now, basis_prev, coupling, tiles, tile_rows, tile_cols, tile_counts):
    half_basis = basis_now.astype(jnp.bfloat16)
    column_blocks = half_basis.reshape(N_ROW, N_COL * NV, B)

    def column(col_index):

        def accumulate(running, row_index):
            partial_value = tile_product(tiles[row_index, col_index], tile_rows[row_index, col_index], tile_cols[row_index, col_index], tile_counts[row_index, col_index], column_blocks[row_index])
            return (running + partial_value, None)
        running, _ = lax.scan(accumulate, jnp.zeros((N_ROW * NV, B), jnp.float32), jnp.arange(N_ROW, dtype=jnp.int32))
        return running
    blocks = lax.map(column, jnp.arange(N_COL, dtype=jnp.int32))
    product = blocks.reshape(N_COL, N_ROW, NV, B).transpose(1, 0, 2, 3).reshape(NROWS, B)
    norm_scale = float(NROWS) ** (-0.5)
    projection = jnp.dot(basis_now.T, product, precision=HIGHEST) * norm_scale
    upper_part = jnp.triu(coupling)
    residual = product - jnp.dot(basis_now, projection, precision=HIGHEST) * norm_scale
    residual = residual - jnp.dot(basis_prev, upper_part.T, precision=HIGHEST)
    gram = jnp.dot(residual.T, residual, precision=HIGHEST) / float(NROWS)
    rfactor = upper_cholesky(gram)
    inverse = lower_inverse(rfactor.T)
    basis = jnp.dot(residual, inverse.T, precision=HIGHEST)
    return (basis, projection, rfactor)
```

```python
import functools

import jax
import jax.numpy as jnp
from jax import lax
from jax.experimental import pallas as pl
from jax.experimental.pallas import tpu as pltpu
from jax.sharding import PartitionSpec as P

HIGHEST = lax.Precision.HIGHEST
F32 = jnp.float32
BF16 = jnp.bfloat16


def dot(a, b):
    return jnp.dot(a, b, precision=HIGHEST, preferred_element_type=F32)


def dot_tn(a, b):
    return lax.dot_general(a, b, (((0,), (0,)), ((), ())), precision=HIGHEST, preferred_element_type=F32)


def dot_nt(a, b):
    return lax.dot_general(a, b, (((1,), (1,)), ((), ())), precision=HIGHEST, preferred_element_type=F32)


def upper_of(x):
    rows = lax.broadcasted_iota(jnp.int32, x.shape, 0)
    cols = lax.broadcasted_iota(jnp.int32, x.shape, 1)
    return jnp.where(rows <= cols, x, 0.0)


def tiles_kernel(rows_ref, cols_ref, count_ref, tiles_ref, basis_ref, out_ref, total_ref):
    slots, size, _ = tiles_ref.shape
    total_ref[...] = jnp.zeros_like(total_ref)
    used = count_ref[0]
    for slot in range(slots):
        start = pl.multiple_of(cols_ref[slot] * size, size)
        value = jnp.dot(tiles_ref[slot], basis_ref[pl.ds(start, size), :], preferred_element_type=F32)
        value = jnp.where(slot < used, value, 0.0)
        place = pl.ds(pl.multiple_of(rows_ref[slot] * size, size), size)
        total_ref[place, :] += value
    out_ref[...] = total_ref[...].astype(BF16)


def early_kernel(now_ref, prev_ref, coupling_ref, grams_ref, shift_ref):
    width = now_ref.shape[1]
    now, prev = now_ref[...], prev_ref[...]
    grams_ref[:width, :] = dot_tn(now, now)
    grams_ref[width:, :] = dot_tn(now, prev)
    shift_ref[...] = dot_nt(prev, upper_of(coupling_ref[...]))


def late_kernel(parts_ref, now_ref, shift_ref, shifted_ref, grams_ref):
    width = now_ref.shape[1]
    shifted = -shift_ref[...]
    for part in range(parts_ref.shape[0]):
        shifted = shifted + parts_ref[part].astype(F32)
    shifted_ref[...] = shifted
    grams_ref[:width, :] = dot_tn(now_ref[...], shifted)
    grams_ref[width:, :] = dot_tn(shifted, shifted)


def sum_kernel(parts_ref, out_ref):
    total = parts_ref[0]
    for part in range(1, parts_ref.shape[0]):
        total = total + parts_ref[part]
    out_ref[...] = total


def eliminate(gram):
    width = gram.shape[0]
    lanes = lax.broadcasted_iota(jnp.int32, (1, width), 1)
    block = 8
    strips = [gram[r : r + block, :] for r in range(0, width, block)]
    subs = lax.broadcasted_iota(jnp.int32, (block, 1), 0)
    for k in range(width):
        at, inside = divmod(k, block)
        row = strips[at][inside : inside + 1, :]
        pivot = row[:, k : k + 1]
        scaled = jnp.where(lanes == k, 1.0, row) * (1.0 / pivot)
        for s in range(at, len(strips)):
            factor = strips[s][:, k : k + 1]
            if s == at:
                factor = jnp.where(subs > inside, factor, 0.0)
                kept = jnp.where((lanes == k) & (subs > inside), 0.0, strips[s])
            else:
                kept = jnp.where(lanes == k, 0.0, strips[s])
            strips[s] = kept - factor * scaled
    return jnp.concatenate(strips, axis=0)


def final_kernel(total_rows, parts_ref, early_ref, coupling_ref, now_ref, shifted_ref, basis_ref, projection_ref, rfactor_ref):
    width = now_ref.shape[1]
    late = parts_ref[0]
    for part in range(1, parts_ref.shape[0]):
        late = late + parts_ref[part]
    cross, square = late[:width], late[width:]
    now_square, now_prev = early_ref[:width, :], early_ref[width:, :]
    norm_scale = total_rows**-0.5
    projection = (cross + dot_nt(now_prev, upper_of(coupling_ref[...]))) * norm_scale
    projection_ref[...] = projection
    scaled = projection * norm_scale
    mixed = dot_tn(scaled, cross - 0.5 * dot(now_square, scaled))
    gram = square - mixed - mixed.T
    reduced = eliminate(gram * (1.0 / total_rows))
    rows = lax.broadcasted_iota(jnp.int32, reduced.shape, 0)
    cols = lax.broadcasted_iota(jnp.int32, reduced.shape, 1)
    diagonal = jnp.sum(jnp.where(rows == cols, reduced, 0.0), axis=1, keepdims=True)
    root = lax.rsqrt(diagonal)
    rfactor_ref[...] = jnp.where(rows <= cols, reduced, 0.0) * root
    inverse = jnp.where(rows > cols, reduced, jnp.where(rows == cols, 1.0, 0.0)) * root
    residual = shifted_ref[...] - dot(now_ref[...], scaled)
    basis_ref[...] = dot_nt(residual, inverse)


def on_device(basis_now, basis_prev, coupling, tiles, tile_rows, tile_cols, tile_counts):
    rows_dev, width = basis_now.shape
    n_row, n_col = lax.axis_size("row"), lax.axis_size("col")
    tile_block = tiles[0, 0]
    total_rows = float(rows_dev * n_row * n_col)
    smem = pl.BlockSpec(memory_space=pltpu.SMEM)
    vmem = pl.BlockSpec(memory_space=pltpu.VMEM)
    params = pltpu.CompilerParams(vmem_limit_bytes=48 * 1024 * 1024)

    gathered = lax.all_gather(basis_now.astype(BF16), "col", axis=0, tiled=True)
    partial = pl.pallas_call(
        tiles_kernel,
        out_shape=jax.ShapeDtypeStruct((n_row * rows_dev, width), BF16),
        in_specs=[smem, smem, smem, vmem, vmem],
        out_specs=vmem,
        scratch_shapes=[pltpu.VMEM((n_row * rows_dev, width), F32)],
        compiler_params=params,
        name="tile_products",
    )(tile_rows.reshape(-1), tile_cols.reshape(-1), tile_counts.reshape(-1), tile_block, gathered)
    parts = lax.all_to_all(partial.reshape(n_row, rows_dev, width), "row", split_axis=0, concat_axis=0, tiled=True)

    early, shift = pl.pallas_call(
        early_kernel,
        out_shape=(
            jax.ShapeDtypeStruct((2 * width, width), F32),
            jax.ShapeDtypeStruct((rows_dev, width), F32),
        ),
        in_specs=[vmem] * 3,
        out_specs=(vmem, vmem),
        compiler_params=params,
        name="early_grams",
    )(basis_now, basis_prev, coupling)
    early = lax.psum(early, ("row", "col"))

    shifted, late = pl.pallas_call(
        late_kernel,
        out_shape=(
            jax.ShapeDtypeStruct((rows_dev, width), F32),
            jax.ShapeDtypeStruct((2 * width, width), F32),
        ),
        in_specs=[vmem] * 3,
        out_specs=(vmem, vmem),
        compiler_params=params,
        name="late_grams",
    )(parts, basis_now, shift)
    late = lax.all_gather(late, "col", axis=0)
    late = pl.pallas_call(
        sum_kernel,
        out_shape=jax.ShapeDtypeStruct((2 * width, width), F32),
        in_specs=[vmem],
        out_specs=vmem,
        compiler_params=params,
        name="column_sum",
    )(late)
    late = lax.all_gather(late, "row", axis=0)
    return pl.pallas_call(
        functools.partial(final_kernel, total_rows),
        out_shape=(
            jax.ShapeDtypeStruct((rows_dev, width), F32),
            jax.ShapeDtypeStruct((width, width), F32),
            jax.ShapeDtypeStruct((width, width), F32),
        ),
        in_specs=[vmem] * 5,
        out_specs=(vmem, vmem, vmem),
        compiler_params=params,
        name="factor_and_basis",
    )(late, early, coupling, basis_now, shifted)


def solution(mesh):
    placed = (
        P(("row", "col"), None),
        P(("row", "col"), None),
        P(),
        P("row", "col", None, None, None),
        P("row", "col", None),
        P("row", "col", None),
        P("row", "col"),
    )
    return jax.shard_map(
        on_device,
        mesh=mesh,
        in_specs=placed,
        out_specs=(P(("row", "col"), None), P(), P()),
        check_vma=False,
    )
```

```python
import functools

import jax
import jax.numpy as jnp
from jax import lax
from jax.experimental import pallas as pl
from jax.experimental.pallas import tpu as pltpu
from jax.sharding import PartitionSpec as P

HIGHEST = lax.Precision.HIGHEST
F32 = jnp.float32
BF16 = jnp.bfloat16


def dot(a, b):
    return jnp.dot(a, b, precision=HIGHEST, preferred_element_type=F32)


def dot_tn(a, b):
    return lax.dot_general(a, b, (((0,), (0,)), ((), ())), precision=HIGHEST, preferred_element_type=F32)


def dot_nt(a, b):
    return lax.dot_general(a, b, (((1,), (1,)), ((), ())), precision=HIGHEST, preferred_element_type=F32)


def upper_of(x):
    rows = lax.broadcasted_iota(jnp.int32, x.shape, 0)
    cols = lax.broadcasted_iota(jnp.int32, x.shape, 1)
    return jnp.where(rows <= cols, x, 0.0)


def tiles_kernel(rows_ref, cols_ref, count_ref, tiles_ref, basis_ref, out_ref, total_ref):
    slots, size, _ = tiles_ref.shape
    total_ref[...] = jnp.zeros_like(total_ref)
    used = count_ref[0]
    for slot in range(slots):
        start = pl.multiple_of(cols_ref[slot] * size, size)
        value = jnp.dot(tiles_ref[slot], basis_ref[pl.ds(start, size), :], preferred_element_type=F32)
        value = jnp.where(slot < used, value, 0.0)
        place = pl.ds(pl.multiple_of(rows_ref[slot] * size, size), size)
        total_ref[place, :] += value
    out_ref[...] = total_ref[...].astype(BF16)


def grams_kernel(parts_ref, now_ref, prev_ref, coupling_ref, shifted_ref, grams_ref):
    width = now_ref.shape[1]
    now, prev = now_ref[...], prev_ref[...]
    shifted = -dot_nt(prev, upper_of(coupling_ref[...]))
    for part in range(parts_ref.shape[0]):
        shifted = shifted + parts_ref[part].astype(F32)
    shifted_ref[...] = shifted
    grams_ref[:width, :] = dot_tn(now, shifted)
    grams_ref[width : 2 * width, :] = dot_tn(shifted, shifted)
    grams_ref[2 * width : 3 * width, :] = dot_tn(now, now)
    grams_ref[3 * width :, :] = dot_tn(now, prev)


def sum_kernel(parts_ref, out_ref):
    total = parts_ref[0]
    for part in range(1, parts_ref.shape[0]):
        total = total + parts_ref[part]
    out_ref[...] = total


def eliminate(gram):
    width = gram.shape[0]
    lanes = lax.broadcasted_iota(jnp.int32, (1, width), 1)
    block = 8
    strips = [gram[r : r + block, :] for r in range(0, width, block)]
    subs = lax.broadcasted_iota(jnp.int32, (block, 1), 0)
    for k in range(width):
        at, inside = divmod(k, block)
        row = strips[at][inside : inside + 1, :]
        pivot = row[:, k : k + 1]
        scaled = jnp.where(lanes == k, 1.0, row) * (1.0 / pivot)
        for s in range(at, len(strips)):
            factor = strips[s][:, k : k + 1]
            if s == at:
                factor = jnp.where(subs > inside, factor, 0.0)
                kept = jnp.where((lanes == k) & (subs > inside), 0.0, strips[s])
            else:
                kept = jnp.where(lanes == k, 0.0, strips[s])
            strips[s] = kept - factor * scaled
    return jnp.concatenate(strips, axis=0)


def final_kernel(total_rows, grams_ref, coupling_ref, now_ref, shifted_ref, basis_ref, projection_ref, rfactor_ref):
    width = now_ref.shape[1]
    cross, square, now_square, now_prev = [grams_ref[k * width : (k + 1) * width, :] for k in range(4)]
    norm_scale = total_rows**-0.5
    projection = (cross + dot_nt(now_prev, upper_of(coupling_ref[...]))) * norm_scale
    projection_ref[...] = projection
    scaled = projection * norm_scale
    mixed = dot_tn(scaled, cross - 0.5 * dot(now_square, scaled))
    gram = square - mixed - mixed.T
    reduced = eliminate(gram * (1.0 / total_rows))
    rows = lax.broadcasted_iota(jnp.int32, reduced.shape, 0)
    cols = lax.broadcasted_iota(jnp.int32, reduced.shape, 1)
    diagonal = jnp.sum(jnp.where(rows == cols, reduced, 0.0), axis=1, keepdims=True)
    root = lax.rsqrt(diagonal)
    rfactor_ref[...] = jnp.where(rows <= cols, reduced, 0.0) * root
    inverse = jnp.where(rows > cols, reduced, jnp.where(rows == cols, 1.0, 0.0)) * root
    residual = shifted_ref[...] - dot(now_ref[...], scaled)
    basis_ref[...] = dot_nt(residual, inverse)


def on_device(basis_now, basis_prev, coupling, tiles, tile_rows, tile_cols, tile_counts):
    rows_dev, width = basis_now.shape
    n_row, n_col = lax.axis_size("row"), lax.axis_size("col")
    tile_block = tiles[0, 0]
    total_rows = float(rows_dev * n_row * n_col)
    smem = pl.BlockSpec(memory_space=pltpu.SMEM)
    vmem = pl.BlockSpec(memory_space=pltpu.VMEM)
    params = pltpu.CompilerParams(vmem_limit_bytes=48 * 1024 * 1024)

    gathered = lax.all_gather(basis_now.astype(BF16), "col", axis=0, tiled=True)
    partial = pl.pallas_call(
        tiles_kernel,
        out_shape=jax.ShapeDtypeStruct((n_row * rows_dev, width), BF16),
        in_specs=[smem, smem, smem, vmem, vmem],
        out_specs=vmem,
        scratch_shapes=[pltpu.VMEM((n_row * rows_dev, width), F32)],
        compiler_params=params,
        name="tile_products",
    )(tile_rows.reshape(-1), tile_cols.reshape(-1), tile_counts.reshape(-1), tile_block, gathered)
    parts = lax.all_to_all(partial.reshape(n_row, rows_dev, width), "row", split_axis=0, concat_axis=0, tiled=True)

    shifted, grams = pl.pallas_call(
        grams_kernel,
        out_shape=(
            jax.ShapeDtypeStruct((rows_dev, width), F32),
            jax.ShapeDtypeStruct((4 * width, width), F32),
        ),
        in_specs=[vmem] * 4,
        out_specs=(vmem, vmem),
        compiler_params=params,
        name="local_grams",
    )(parts, basis_now, basis_prev, coupling)
    everyone = ("row", "col")
    pieces = lax.all_to_all(grams.reshape(n_row * n_col, -1, width), everyone, split_axis=0, concat_axis=0, tiled=True)
    piece = pl.pallas_call(
        sum_kernel,
        out_shape=jax.ShapeDtypeStruct(pieces.shape[1:], F32),
        in_specs=[vmem],
        out_specs=vmem,
        compiler_params=params,
        name="sum_of_pieces",
    )(pieces)
    grams = lax.all_gather(piece, everyone, axis=0, tiled=True)
    return pl.pallas_call(
        functools.partial(final_kernel, total_rows),
        out_shape=(
            jax.ShapeDtypeStruct((rows_dev, width), F32),
            jax.ShapeDtypeStruct((width, width), F32),
            jax.ShapeDtypeStruct((width, width), F32),
        ),
        in_specs=[vmem] * 4,
        out_specs=(vmem, vmem, vmem),
        compiler_params=params,
        name="factor_and_basis",
    )(grams, coupling, basis_now, shifted)


def solution(mesh):
    placed = (
        P(("row", "col"), None),
        P(("row", "col"), None),
        P(),
        P("row", "col", None, None, None),
        P("row", "col", None),
        P("row", "col", None),
        P("row", "col"),
    )
    return jax.shard_map(
        on_device,
        mesh=mesh,
        in_specs=placed,
        out_specs=(P(("row", "col"), None), P(), P()),
        check_vma=False,
    )
```

```python
import functools

import jax
import jax.numpy as jnp
from jax import lax
from jax.experimental import pallas as pl
from jax.experimental.pallas import tpu as pltpu
from jax.sharding import PartitionSpec as P

HIGHEST = lax.Precision.HIGHEST
F32 = jnp.float32
BF16 = jnp.bfloat16


def dot(a, b):
    return jnp.dot(a, b, precision=HIGHEST, preferred_element_type=F32)


def dot_tn(a, b, precision=HIGHEST):
    return lax.dot_general(a, b, (((0,), (0,)), ((), ())), precision=precision, preferred_element_type=F32)


def dot_nt(a, b):
    return lax.dot_general(a, b, (((1,), (1,)), ((), ())), precision=HIGHEST, preferred_element_type=F32)


def upper_of(x):
    rows = lax.broadcasted_iota(jnp.int32, x.shape, 0)
    cols = lax.broadcasted_iota(jnp.int32, x.shape, 1)
    return jnp.where(rows <= cols, x, 0.0)


def tiles_kernel(n_col, rows_ref, cols_ref, count_ref, me_ref, tiles_ref, basis_ref, out_ref, total_ref, early_ref):
    slots, size, _ = tiles_ref.shape
    n_row, depth, width = out_ref.shape
    rows_dev = total_ref.shape[0] // n_row
    piece = early_ref.shape[0] // (n_row * n_col)
    total_ref[...] = jnp.zeros_like(total_ref)
    used = count_ref[0]
    for slot in range(slots):
        col = cols_ref[slot]
        per_slab = rows_dev // size
        start = pl.multiple_of((2 * per_slab * (col // per_slab) + lax.rem(col, per_slab)) * size, size)
        value = jnp.dot(tiles_ref[slot], basis_ref[pl.ds(start, size), :], preferred_element_type=F32)
        value = jnp.where(slot < used, value, 0.0)
        place = pl.ds(pl.multiple_of(rows_ref[slot] * size, size), size)
        total_ref[place, :] += value
    square = jnp.zeros((width, width), F32)
    cross = jnp.zeros((width, width), F32)
    for slab in range(n_col):
        now = basis_ref[2 * slab * rows_dev : (2 * slab + 1) * rows_dev, :]
        prev = basis_ref[(2 * slab + 1) * rows_dev : (2 * slab + 2) * rows_dev, :]
        square += dot_tn(now, now, None)
        cross += dot_tn(now, prev, None)
    if early_ref.shape[0] > 2 * width:
        early_ref[...] = jnp.zeros_like(early_ref)
    early_ref[:width, :] = square
    early_ref[width : 2 * width, :] = cross
    me = me_ref[0]
    for row in range(n_row):
        out_ref[row, :rows_dev, :] = total_ref[row * rows_dev : (row + 1) * rows_dev, :].astype(BF16)
        value = early_ref[pl.ds(pl.multiple_of((row * n_col + me) * piece, piece), piece), :]
        high = value.astype(BF16)
        low = (value - high.astype(F32)).astype(BF16)
        out_ref[row, rows_dev:, :] = jnp.concatenate([high, low], axis=0)


def grams_kernel(parts_ref, now_ref, prev_ref, coupling_ref, shifted_ref, grams_ref, early_ref):
    rows_dev, width = now_ref.shape
    piece = early_ref.shape[0]
    product = jnp.zeros((rows_dev, width), F32)
    early = jnp.zeros((piece, width), F32)
    for part in range(parts_ref.shape[0]):
        product = product + parts_ref[part, :rows_dev, :].astype(F32)
        both = parts_ref[part, rows_dev:, :].astype(F32)
        early = early + (both[:piece] + both[piece:])
    early_ref[...] = early
    shifted = product - dot_nt(prev_ref[...], upper_of(coupling_ref[...]))
    shifted_ref[...] = shifted
    if grams_ref.shape[0] > 2 * width:
        grams_ref[...] = jnp.zeros_like(grams_ref)
    grams_ref[:width, :] = dot_tn(now_ref[...], product)
    grams_ref[width : 2 * width, :] = dot_tn(shifted, shifted)


def spread_kernel(parts_ref, early_ref, out_ref):
    piece = early_ref.shape[0]
    total = parts_ref[0]
    for part in range(1, parts_ref.shape[0]):
        total = total + parts_ref[part]
    early = early_ref[...]
    for part in range(out_ref.shape[0]):
        out_ref[part, :piece, :] = total
        out_ref[part, piece:, :] = early


def eliminate(gram):
    width = gram.shape[0]
    lanes = lax.broadcasted_iota(jnp.int32, (1, width), 1)
    block = 8
    strips = [gram[r : r + block, :] for r in range(0, width, block)]
    subs = lax.broadcasted_iota(jnp.int32, (block, 1), 0)
    for k in range(width):
        at, inside = divmod(k, block)
        row = strips[at][inside : inside + 1, :]
        pivot = row[:, k : k + 1]
        scaled = jnp.where(lanes == k, 1.0, row) * (1.0 / pivot)
        for s in range(at, len(strips)):
            factor = strips[s][:, k : k + 1]
            if s == at:
                factor = jnp.where(subs > inside, factor, 0.0)
                kept = jnp.where((lanes == k) & (subs > inside), 0.0, strips[s])
            else:
                kept = jnp.where(lanes == k, 0.0, strips[s])
            strips[s] = kept - factor * scaled
    return jnp.concatenate(strips, axis=0)


def final_kernel(total_rows, pieces_ref, coupling_ref, now_ref, shifted_ref, basis_ref, projection_ref, rfactor_ref):
    width = now_ref.shape[1]
    piece = pieces_ref.shape[1] // 2
    late = pieces_ref[:, :piece, :].reshape(-1, width)
    early = pieces_ref[:, piece:, :].reshape(-1, width)
    now_product, square = late[:width], late[width : 2 * width]
    now_square, now_prev = early[:width], early[width : 2 * width]
    norm_scale = total_rows**-0.5
    projection = now_product * norm_scale
    projection_ref[...] = projection
    scaled = projection * norm_scale
    cross = now_product - dot_nt(now_prev, upper_of(coupling_ref[...]))
    mixed = dot_tn(scaled, cross - 0.5 * dot(now_square, scaled))
    gram = square - mixed - mixed.T
    reduced = eliminate(gram * (1.0 / total_rows))
    rows = lax.broadcasted_iota(jnp.int32, reduced.shape, 0)
    cols = lax.broadcasted_iota(jnp.int32, reduced.shape, 1)
    diagonal = jnp.sum(jnp.where(rows == cols, reduced, 0.0), axis=1, keepdims=True)
    root = lax.rsqrt(diagonal)
    rfactor_ref[...] = jnp.where(rows <= cols, reduced, 0.0) * root
    inverse = jnp.where(rows > cols, reduced, jnp.where(rows == cols, 1.0, 0.0)) * root
    residual = shifted_ref[...] - dot(now_ref[...], scaled)
    basis_ref[...] = dot_nt(residual, inverse)


def on_device(basis_now, basis_prev, coupling, tiles, tile_rows, tile_cols, tile_counts):
    rows_dev, width = basis_now.shape
    n_row, n_col = lax.axis_size("row"), lax.axis_size("col")
    devices = n_row * n_col
    tile_block = tiles[0, 0]
    total_rows = float(rows_dev * devices)
    piece = -(-2 * width // (8 * devices)) * 8
    smem = pl.BlockSpec(memory_space=pltpu.SMEM)
    vmem = pl.BlockSpec(memory_space=pltpu.VMEM)
    params = pltpu.CompilerParams(vmem_limit_bytes=48 * 1024 * 1024)

    both = jnp.concatenate([basis_now, basis_prev], axis=0).astype(BF16)
    gathered = lax.all_gather(both, "col", axis=0, tiled=True)
    partial = pl.pallas_call(
        functools.partial(tiles_kernel, n_col),
        out_shape=jax.ShapeDtypeStruct((n_row, rows_dev + 2 * piece, width), BF16),
        in_specs=[smem, smem, smem, smem, vmem, vmem],
        out_specs=vmem,
        scratch_shapes=[
            pltpu.VMEM((n_row * rows_dev, width), F32),
            pltpu.VMEM((devices * piece, width), F32),
        ],
        compiler_params=params,
        name="tile_products",
    )(
        tile_rows.reshape(-1),
        tile_cols.reshape(-1),
        tile_counts.reshape(-1),
        lax.axis_index("col").reshape(1),
        tile_block,
        gathered,
    )
    parts = lax.all_to_all(partial, "row", split_axis=0, concat_axis=0, tiled=True)

    shifted, grams, early = pl.pallas_call(
        grams_kernel,
        out_shape=(
            jax.ShapeDtypeStruct((rows_dev, width), F32),
            jax.ShapeDtypeStruct((devices * piece, width), F32),
            jax.ShapeDtypeStruct((piece, width), F32),
        ),
        in_specs=[vmem] * 4,
        out_specs=(vmem, vmem, vmem),
        compiler_params=params,
        name="local_grams",
    )(parts, basis_now, basis_prev, coupling)
    everyone = ("row", "col")
    pieces = lax.all_to_all(grams.reshape(devices, piece, width), everyone, split_axis=0, concat_axis=0, tiled=True)
    copies = pl.pallas_call(
        spread_kernel,
        out_shape=jax.ShapeDtypeStruct((devices, 2 * piece, width), F32),
        in_specs=[vmem, vmem],
        out_specs=vmem,
        compiler_params=params,
        name="sum_and_spread",
    )(pieces, early)
    sums = lax.all_to_all(copies, everyone, split_axis=0, concat_axis=0, tiled=True)
    return pl.pallas_call(
        functools.partial(final_kernel, total_rows),
        out_shape=(
            jax.ShapeDtypeStruct((rows_dev, width), F32),
            jax.ShapeDtypeStruct((width, width), F32),
            jax.ShapeDtypeStruct((width, width), F32),
        ),
        in_specs=[vmem] * 4,
        out_specs=(vmem, vmem, vmem),
        compiler_params=params,
        name="factor_and_basis",
    )(sums, coupling, basis_now, shifted)


def solution(mesh):
    placed = (
        P(("row", "col"), None),
        P(("row", "col"), None),
        P(),
        P("row", "col", None, None, None),
        P("row", "col", None),
        P("row", "col", None),
        P("row", "col"),
    )
    return jax.shard_map(
        on_device,
        mesh=mesh,
        in_specs=placed,
        out_specs=(P(("row", "col"), None), P(), P()),
        check_vma=False,
    )
```

```python
import functools

import jax
import jax.numpy as jnp
from jax import lax
from jax.experimental import pallas as pl
from jax.experimental.pallas import tpu as pltpu
from jax.sharding import PartitionSpec as P

HIGHEST = lax.Precision.HIGHEST
F32 = jnp.float32
BF16 = jnp.bfloat16


def dot(a, b):
    return jnp.dot(a, b, precision=HIGHEST, preferred_element_type=F32)


def dot_tn(a, b, precision=HIGHEST):
    return lax.dot_general(a, b, (((0,), (0,)), ((), ())), precision=precision, preferred_element_type=F32)


def dot_nt(a, b):
    return lax.dot_general(a, b, (((1,), (1,)), ((), ())), precision=HIGHEST, preferred_element_type=F32)


def upper_of(x):
    rows = lax.broadcasted_iota(jnp.int32, x.shape, 0)
    cols = lax.broadcasted_iota(jnp.int32, x.shape, 1)
    return jnp.where(rows <= cols, x, 0.0)


def tiles_kernel(n_row, n_col, rows_ref, cols_ref, count_ref, me_ref, tiles_ref, *refs):
    basis_refs, out_refs = refs[:n_col], refs[n_col : n_col + n_row]
    total_ref, early_ref, basis_ref = refs[n_col + n_row :]
    slots, size, _ = tiles_ref.shape
    depth, width = out_refs[0].shape
    rows_dev = total_ref.shape[0] // n_row
    piece = early_ref.shape[0] // (n_row * n_col)
    my_row, my_col = me_ref[0], me_ref[1]
    square = jnp.zeros((width, width), F32)
    cross = jnp.zeros((width, width), F32)
    for step in range(n_col):
        now, prev = basis_refs[step][:rows_dev, :], basis_refs[step][rows_dev:, :]
        owner = lax.rem(my_col + n_col - step, n_col)
        basis_ref[pl.ds(pl.multiple_of(owner * rows_dev, rows_dev), rows_dev), :] = now
        square += dot_tn(now, now, None)
        cross += dot_tn(now, prev, None)
    total_ref[...] = jnp.zeros_like(total_ref)
    used = count_ref[0]
    for slot in range(slots):
        start = pl.multiple_of(cols_ref[slot] * size, size)
        value = jnp.dot(tiles_ref[slot], basis_ref[pl.ds(start, size), :], preferred_element_type=F32)
        value = jnp.where(slot < used, value, 0.0)
        place = pl.ds(pl.multiple_of(rows_ref[slot] * size, size), size)
        total_ref[place, :] += value
    if early_ref.shape[0] > 2 * width:
        early_ref[...] = jnp.zeros_like(early_ref)
    early_ref[:width, :] = square
    early_ref[width : 2 * width, :] = cross
    for step in range(n_row):
        row = lax.rem(my_row + step, n_row)
        out_ref = out_refs[step]
        out_ref[:rows_dev, :] = total_ref[pl.ds(pl.multiple_of(row * rows_dev, rows_dev), rows_dev), :].astype(BF16)
        value = early_ref[pl.ds(pl.multiple_of((row * n_col + my_col) * piece, piece), piece), :]
        high = value.astype(BF16)
        low = (value - high.astype(F32)).astype(BF16)
        out_ref[rows_dev:, :] = jnp.concatenate([high, low], axis=0)


def grams_kernel(now_ref, prev_ref, coupling_ref, *refs):
    part_refs, (shifted_ref, grams_ref, early_ref) = refs[:-3], refs[-3:]
    rows_dev, width = now_ref.shape
    piece = early_ref.shape[0]
    product = jnp.zeros((rows_dev, width), F32)
    early = jnp.zeros((piece, width), F32)
    for part_ref in part_refs:
        product = product + part_ref[:rows_dev, :].astype(F32)
        both = part_ref[rows_dev:, :].astype(F32)
        early = early + (both[:piece] + both[piece:])
    early_ref[...] = early
    shifted = product - dot_nt(prev_ref[...], upper_of(coupling_ref[...]))
    shifted_ref[...] = shifted
    if grams_ref.shape[0] > 2 * width:
        grams_ref[...] = jnp.zeros_like(grams_ref)
    grams_ref[:width, :] = dot_tn(now_ref[...], product)
    grams_ref[width : 2 * width, :] = dot_tn(shifted, shifted)


def spread_kernel(parts_ref, early_ref, out_ref):
    piece = early_ref.shape[0]
    total = parts_ref[0]
    for part in range(1, parts_ref.shape[0]):
        total = total + parts_ref[part]
    early = early_ref[...]
    for part in range(out_ref.shape[0]):
        out_ref[part, :piece, :] = total
        out_ref[part, piece:, :] = early


def eliminate(gram):
    width = gram.shape[0]
    lanes = lax.broadcasted_iota(jnp.int32, (1, width), 1)
    block = 8
    strips = [gram[r : r + block, :] for r in range(0, width, block)]
    subs = lax.broadcasted_iota(jnp.int32, (block, 1), 0)
    for k in range(width):
        at, inside = divmod(k, block)
        row = strips[at][inside : inside + 1, :]
        pivot = row[:, k : k + 1]
        scaled = jnp.where(lanes == k, 1.0, row) * (1.0 / pivot)
        for s in range(at, len(strips)):
            factor = strips[s][:, k : k + 1]
            if s == at:
                factor = jnp.where(subs > inside, factor, 0.0)
                kept = jnp.where((lanes == k) & (subs > inside), 0.0, strips[s])
            else:
                kept = jnp.where(lanes == k, 0.0, strips[s])
            strips[s] = kept - factor * scaled
    return jnp.concatenate(strips, axis=0)


def final_kernel(total_rows, pieces_ref, coupling_ref, now_ref, shifted_ref, basis_ref, projection_ref, rfactor_ref):
    width = now_ref.shape[1]
    piece = pieces_ref.shape[1] // 2
    late = pieces_ref[:, :piece, :].reshape(-1, width)
    early = pieces_ref[:, piece:, :].reshape(-1, width)
    now_product, square = late[:width], late[width : 2 * width]
    now_square, now_prev = early[:width], early[width : 2 * width]
    norm_scale = total_rows**-0.5
    projection = now_product * norm_scale
    projection_ref[...] = projection
    scaled = projection * norm_scale
    cross = now_product - dot_nt(now_prev, upper_of(coupling_ref[...]))
    mixed = dot_tn(scaled, cross - 0.5 * dot(now_square, scaled))
    gram = square - mixed - mixed.T
    reduced = eliminate(gram * (1.0 / total_rows))
    rows = lax.broadcasted_iota(jnp.int32, reduced.shape, 0)
    cols = lax.broadcasted_iota(jnp.int32, reduced.shape, 1)
    diagonal = jnp.sum(jnp.where(rows == cols, reduced, 0.0), axis=1, keepdims=True)
    root = lax.rsqrt(diagonal)
    rfactor_ref[...] = jnp.where(rows <= cols, reduced, 0.0) * root
    inverse = jnp.where(rows > cols, reduced, jnp.where(rows == cols, 1.0, 0.0)) * root
    residual = shifted_ref[...] - dot(now_ref[...], scaled)
    basis_ref[...] = dot_nt(residual, inverse)


def shifted_copies(blocks, axis):
    n = lax.axis_size(axis)
    return [blocks[0]] + [
        lax.ppermute(blocks[step], axis, [(source, (source + step) % n) for source in range(n)]) for step in range(1, n)
    ]


def on_device(basis_now, basis_prev, coupling, tiles, tile_rows, tile_cols, tile_counts):
    rows_dev, width = basis_now.shape
    n_row, n_col = lax.axis_size("row"), lax.axis_size("col")
    devices = n_row * n_col
    tile_block = tiles[0, 0]
    total_rows = float(rows_dev * devices)
    piece = -(-2 * width // (8 * devices)) * 8
    smem = pl.BlockSpec(memory_space=pltpu.SMEM)
    vmem = pl.BlockSpec(memory_space=pltpu.VMEM)
    params = pltpu.CompilerParams(vmem_limit_bytes=48 * 1024 * 1024)

    both = jnp.concatenate([basis_now, basis_prev], axis=0).astype(BF16)
    slabs = shifted_copies([both] * n_col, "col")
    blocks = pl.pallas_call(
        functools.partial(tiles_kernel, n_row, n_col),
        out_shape=[jax.ShapeDtypeStruct((rows_dev + 2 * piece, width), BF16)] * n_row,
        in_specs=[smem] * 4 + [vmem] * (1 + n_col),
        out_specs=[vmem] * n_row,
        scratch_shapes=[
            pltpu.VMEM((n_row * rows_dev, width), F32),
            pltpu.VMEM((devices * piece, width), F32),
            pltpu.VMEM((n_col * rows_dev, width), BF16),
        ],
        compiler_params=params,
        name="tile_products",
    )(
        tile_rows.reshape(-1),
        tile_cols.reshape(-1),
        tile_counts.reshape(-1),
        jnp.stack([lax.axis_index("row"), lax.axis_index("col")]),
        tile_block,
        *slabs,
    )
    parts = shifted_copies(blocks, "row")

    shifted, grams, early = pl.pallas_call(
        grams_kernel,
        out_shape=(
            jax.ShapeDtypeStruct((rows_dev, width), F32),
            jax.ShapeDtypeStruct((devices * piece, width), F32),
            jax.ShapeDtypeStruct((piece, width), F32),
        ),
        in_specs=[vmem] * (3 + n_row),
        out_specs=(vmem, vmem, vmem),
        compiler_params=params,
        name="local_grams",
    )(basis_now, basis_prev, coupling, *parts)
    everyone = ("row", "col")
    pieces = lax.all_to_all(grams.reshape(devices, piece, width), everyone, split_axis=0, concat_axis=0, tiled=True)
    copies = pl.pallas_call(
        spread_kernel,
        out_shape=jax.ShapeDtypeStruct((devices, 2 * piece, width), F32),
        in_specs=[vmem, vmem],
        out_specs=vmem,
        compiler_params=params,
        name="sum_and_spread",
    )(pieces, early)
    sums = lax.all_to_all(copies, everyone, split_axis=0, concat_axis=0, tiled=True)
    return pl.pallas_call(
        functools.partial(final_kernel, total_rows),
        out_shape=(
            jax.ShapeDtypeStruct((rows_dev, width), F32),
            jax.ShapeDtypeStruct((width, width), F32),
            jax.ShapeDtypeStruct((width, width), F32),
        ),
        in_specs=[vmem] * 4,
        out_specs=(vmem, vmem, vmem),
        compiler_params=params,
        name="factor_and_basis",
    )(sums, coupling, basis_now, shifted)


def solution(mesh):
    placed = (
        P(("row", "col"), None),
        P(("row", "col"), None),
        P(),
        P("row", "col", None, None, None),
        P("row", "col", None),
        P("row", "col", None),
        P("row", "col"),
    )
    return jax.shard_map(
        on_device,
        mesh=mesh,
        in_specs=placed,
        out_specs=(P(("row", "col"), None), P(), P()),
        check_vma=False,
    )
```

```python
import functools

import jax
import jax.numpy as jnp
from jax import lax
from jax.experimental import pallas as pl
from jax.experimental.pallas import tpu as pltpu
from jax.sharding import PartitionSpec as P

HIGHEST = lax.Precision.HIGHEST
F32 = jnp.float32
BF16 = jnp.bfloat16


def dot(a, b):
    return jnp.dot(a, b, precision=HIGHEST, preferred_element_type=F32)


def dot_tn(a, b, precision=HIGHEST):
    return lax.dot_general(a, b, (((0,), (0,)), ((), ())), precision=precision, preferred_element_type=F32)


def dot_nt(a, b):
    return lax.dot_general(a, b, (((1,), (1,)), ((), ())), precision=HIGHEST, preferred_element_type=F32)


def upper_of(x):
    rows = lax.broadcasted_iota(jnp.int32, x.shape, 0)
    cols = lax.broadcasted_iota(jnp.int32, x.shape, 1)
    return jnp.where(rows <= cols, x, 0.0)


def tiles_kernel(n_row, n_col, rows_ref, cols_ref, count_ref, me_ref, tiles_ref, *refs):
    basis_refs, out_refs = refs[:n_col], refs[n_col : n_col + n_row]
    total_ref, early_ref, basis_ref = refs[n_col + n_row :]
    slots, size, _ = tiles_ref.shape
    depth, width = out_refs[0].shape
    rows_dev = total_ref.shape[0] // n_row
    piece = early_ref.shape[0] // (n_row * n_col)
    my_row, my_col = me_ref[0], me_ref[1]
    square = jnp.zeros((width, width), F32)
    cross = jnp.zeros((width, width), F32)
    for step in range(n_col):
        now, prev = basis_refs[step][:rows_dev, :], basis_refs[step][rows_dev:, :]
        owner = lax.rem(my_col + n_col - step, n_col)
        basis_ref[pl.ds(pl.multiple_of(owner * rows_dev, rows_dev), rows_dev), :] = now
        square += dot_tn(now, now, None)
        cross += dot_tn(now, prev, None)
    total_ref[...] = jnp.zeros_like(total_ref)
    used = count_ref[0]
    for slot in range(slots):
        start = pl.multiple_of(cols_ref[slot] * size, size)
        value = jnp.dot(tiles_ref[slot], basis_ref[pl.ds(start, size), :], preferred_element_type=F32)
        value = jnp.where(slot < used, value, 0.0)
        place = pl.ds(pl.multiple_of(rows_ref[slot] * size, size), size)
        total_ref[place, :] += value
    if early_ref.shape[0] > 2 * width:
        early_ref[...] = jnp.zeros_like(early_ref)
    early_ref[:width, :] = square
    early_ref[width : 2 * width, :] = cross
    for step in range(n_row):
        row = lax.rem(my_row + step, n_row)
        out_ref = out_refs[step]
        out_ref[:rows_dev, :] = total_ref[pl.ds(pl.multiple_of(row * rows_dev, rows_dev), rows_dev), :].astype(BF16)
        value = early_ref[pl.ds(pl.multiple_of((row * n_col + my_col) * piece, piece), piece), :]
        high = value.astype(BF16)
        low = (value - high.astype(F32)).astype(BF16)
        out_ref[rows_dev:, :] = jnp.concatenate([high, low], axis=0)


def grams_kernel(now_ref, prev_ref, coupling_ref, *refs):
    part_refs, (shifted_ref, grams_ref, early_ref) = refs[:-3], refs[-3:]
    rows_dev, width = now_ref.shape
    piece = early_ref.shape[0]
    product = jnp.zeros((rows_dev, width), F32)
    early = jnp.zeros((piece, width), F32)
    for part_ref in part_refs:
        product = product + part_ref[:rows_dev, :].astype(F32)
        both = part_ref[rows_dev:, :].astype(F32)
        early = early + (both[:piece] + both[piece:])
    early_ref[...] = early
    shifted = product - dot_nt(prev_ref[...], upper_of(coupling_ref[...]))
    shifted_ref[...] = shifted
    if grams_ref.shape[0] > 2 * width:
        grams_ref[...] = jnp.zeros_like(grams_ref)
    grams_ref[:width, :] = dot_tn(now_ref[...], product)
    grams_ref[width : 2 * width, :] = dot_tn(shifted, shifted)


def spread_kernel(parts_ref, early_ref, out_ref):
    piece = early_ref.shape[0]
    total = parts_ref[0]
    for part in range(1, parts_ref.shape[0]):
        total = total + parts_ref[part]
    early = early_ref[...]
    for part in range(out_ref.shape[0]):
        out_ref[part, :piece, :] = total
        out_ref[part, piece:, :] = early


def eliminate(gram):
    width = gram.shape[0]
    block = 8
    lanes = lax.broadcasted_iota(jnp.int32, (block, width), 1)
    subs = lax.broadcasted_iota(jnp.int32, (block, width), 0)

    def column(strip, k):
        return jnp.broadcast_to(strip[:, k : k + 1], (block, width))

    def row(strip, k):
        return jnp.broadcast_to(strip[k : k + 1, :], (block, width))

    strips = [gram[r : r + block, :] for r in range(0, width, block)]
    finished = []
    for at in range(len(strips)):
        first = at * block
        panel = strips[at]
        columns = [column(panel, first + j) for j in range(block)]
        kept = panel
        for j in range(block):
            here, pivot_lane = subs == j, lanes == first + j
            inverse = 1.0 / row(columns[j], j)
            pivot_row = row(panel, j)
            kept = jnp.where(here, pivot_row, kept)
            unit = jnp.where(pivot_lane, 1.0, pivot_row) * inverse
            factor = columns[j]
            panel = jnp.where(here, unit, jnp.where(pivot_lane, 0.0, panel) - factor * unit)
            for m in range(j + 1, block):
                scaled = row(columns[m], j) * inverse
                columns[m] = jnp.where(here, scaled, columns[m] - factor * scaled)
        finished.append(kept)
        rows = [row(panel, m) for m in range(block)]
        inside = (lanes >= first) & (lanes < first + block)
        for s in range(at + 1, len(strips)):
            terms = [column(strips[s], first + m) * rows[m] for m in range(block)]
            while len(terms) > 1:
                terms = [x + y for x, y in zip(terms[::2], terms[1::2])]
            strips[s] = jnp.where(inside, 0.0, strips[s]) - terms[0]
    return jnp.concatenate(finished, axis=0)


def final_kernel(total_rows, pieces_ref, coupling_ref, now_ref, shifted_ref, basis_ref, projection_ref, rfactor_ref):
    width = now_ref.shape[1]
    piece = pieces_ref.shape[1] // 2
    late = pieces_ref[:, :piece, :].reshape(-1, width)
    early = pieces_ref[:, piece:, :].reshape(-1, width)
    now_product, square = late[:width], late[width : 2 * width]
    now_square, now_prev = early[:width], early[width : 2 * width]
    norm_scale = total_rows**-0.5
    projection = now_product * norm_scale
    projection_ref[...] = projection
    scaled = projection * norm_scale
    cross = now_product - dot_nt(now_prev, upper_of(coupling_ref[...]))
    mixed = dot_tn(scaled, cross - 0.5 * dot(now_square, scaled))
    gram = square - mixed - mixed.T
    reduced = eliminate(gram * (1.0 / total_rows))
    rows = lax.broadcasted_iota(jnp.int32, reduced.shape, 0)
    cols = lax.broadcasted_iota(jnp.int32, reduced.shape, 1)
    diagonal = jnp.sum(jnp.where(rows == cols, reduced, 0.0), axis=1, keepdims=True)
    root = lax.rsqrt(diagonal)
    rfactor_ref[...] = jnp.where(rows <= cols, reduced, 0.0) * root
    inverse = jnp.where(rows > cols, reduced, jnp.where(rows == cols, 1.0, 0.0)) * root
    residual = shifted_ref[...] - dot(now_ref[...], scaled)
    basis_ref[...] = dot_nt(residual, inverse)


def shifted_copies(blocks, axis):
    n = lax.axis_size(axis)
    return [blocks[0]] + [
        lax.ppermute(blocks[step], axis, [(source, (source + step) % n) for source in range(n)]) for step in range(1, n)
    ]


def on_device(basis_now, basis_prev, coupling, tiles, tile_rows, tile_cols, tile_counts):
    rows_dev, width = basis_now.shape
    n_row, n_col = lax.axis_size("row"), lax.axis_size("col")
    devices = n_row * n_col
    tile_block = tiles[0, 0]
    total_rows = float(rows_dev * devices)
    piece = -(-2 * width // (8 * devices)) * 8
    smem = pl.BlockSpec(memory_space=pltpu.SMEM)
    vmem = pl.BlockSpec(memory_space=pltpu.VMEM)
    params = pltpu.CompilerParams(vmem_limit_bytes=48 * 1024 * 1024)

    both = jnp.concatenate([basis_now, basis_prev], axis=0).astype(BF16)
    slabs = shifted_copies([both] * n_col, "col")
    blocks = pl.pallas_call(
        functools.partial(tiles_kernel, n_row, n_col),
        out_shape=[jax.ShapeDtypeStruct((rows_dev + 2 * piece, width), BF16)] * n_row,
        in_specs=[smem] * 4 + [vmem] * (1 + n_col),
        out_specs=[vmem] * n_row,
        scratch_shapes=[
            pltpu.VMEM((n_row * rows_dev, width), F32),
            pltpu.VMEM((devices * piece, width), F32),
            pltpu.VMEM((n_col * rows_dev, width), BF16),
        ],
        compiler_params=params,
        name="tile_products",
    )(
        tile_rows.reshape(-1),
        tile_cols.reshape(-1),
        tile_counts.reshape(-1),
        jnp.stack([lax.axis_index("row"), lax.axis_index("col")]),
        tile_block,
        *slabs,
    )
    parts = shifted_copies(blocks, "row")

    shifted, grams, early = pl.pallas_call(
        grams_kernel,
        out_shape=(
            jax.ShapeDtypeStruct((rows_dev, width), F32),
            jax.ShapeDtypeStruct((devices * piece, width), F32),
            jax.ShapeDtypeStruct((piece, width), F32),
        ),
        in_specs=[vmem] * (3 + n_row),
        out_specs=(vmem, vmem, vmem),
        compiler_params=params,
        name="local_grams",
    )(basis_now, basis_prev, coupling, *parts)
    everyone = ("row", "col")
    pieces = lax.all_to_all(grams.reshape(devices, piece, width), everyone, split_axis=0, concat_axis=0, tiled=True)
    copies = pl.pallas_call(
        spread_kernel,
        out_shape=jax.ShapeDtypeStruct((devices, 2 * piece, width), F32),
        in_specs=[vmem, vmem],
        out_specs=vmem,
        compiler_params=params,
        name="sum_and_spread",
    )(pieces, early)
    sums = lax.all_to_all(copies, everyone, split_axis=0, concat_axis=0, tiled=True)
    return pl.pallas_call(
        functools.partial(final_kernel, total_rows),
        out_shape=(
            jax.ShapeDtypeStruct((rows_dev, width), F32),
            jax.ShapeDtypeStruct((width, width), F32),
            jax.ShapeDtypeStruct((width, width), F32),
        ),
        in_specs=[vmem] * 4,
        out_specs=(vmem, vmem, vmem),
        compiler_params=params,
        name="factor_and_basis",
    )(sums, coupling, basis_now, shifted)


def solution(mesh):
    placed = (
        P(("row", "col"), None),
        P(("row", "col"), None),
        P(),
        P("row", "col", None, None, None),
        P("row", "col", None),
        P("row", "col", None),
        P("row", "col"),
    )
    return jax.shard_map(
        on_device,
        mesh=mesh,
        in_specs=placed,
        out_specs=(P(("row", "col"), None), P(), P()),
        check_vma=False,
    )
```

```python
import functools

import jax
import jax.numpy as jnp
from jax import lax
from jax.experimental import pallas as pl
from jax.experimental.pallas import tpu as pltpu
from jax.sharding import PartitionSpec as P

HIGHEST = lax.Precision.HIGHEST
F32 = jnp.float32
BF16 = jnp.bfloat16


def dot(a, b):
    return jnp.dot(a, b, precision=HIGHEST, preferred_element_type=F32)


def dot_tn(a, b, precision=HIGHEST):
    return lax.dot_general(a, b, (((0,), (0,)), ((), ())), precision=precision, preferred_element_type=F32)


def dot_nt(a, b):
    return lax.dot_general(a, b, (((1,), (1,)), ((), ())), precision=HIGHEST, preferred_element_type=F32)


def upper_of(x):
    rows = lax.broadcasted_iota(jnp.int32, x.shape, 0)
    cols = lax.broadcasted_iota(jnp.int32, x.shape, 1)
    return jnp.where(rows <= cols, x, 0.0)


def distances(n):
    return range(n - 1, -1, -1)


def high_and_low(value):
    high = value.astype(BF16)
    low = (value - high.astype(F32)).astype(BF16)
    return jnp.concatenate([high, low], axis=0)


def sum_high_and_low(value):
    half = value.shape[0] // 2
    value = value.astype(F32)
    return value[:half] + value[half:]


def start_kernel(n_row, n_col, me_ref, rows_ref, cols_ref, count_ref, now_ref, prev_ref, *refs):
    slab_refs, (rows_out_ref, cols_out_ref, count_out_ref, early_ref) = refs[:n_col], refs[n_col:]
    rows_out_ref[...] = rows_ref[...]
    cols_out_ref[...] = cols_ref[...]
    count_out_ref[...] = count_ref[...]
    rows_dev, width = now_ref.shape
    piece = early_ref.shape[0] // (n_row * n_col)
    now, prev = now_ref[...], prev_ref[...]
    if early_ref.shape[0] > 2 * width:
        early_ref[...] = jnp.zeros_like(early_ref)
    early_ref[:width, :] = dot_tn(now, now)
    early_ref[width : 2 * width, :] = dot_tn(now, prev)
    half = now.astype(BF16)
    for step, slab_ref in zip(distances(n_col), slab_refs):
        col = me_ref[1] ^ step
        places = [pl.multiple_of((row * n_col + col) * piece, piece) for row in range(n_row)]
        early = jnp.concatenate([early_ref[pl.ds(place, piece), :] for place in places], axis=0)
        slab_ref[:rows_dev, :] = half
        slab_ref[rows_dev:, :] = high_and_low(early)


def tiles_kernel(n_row, n_col, me_ref, rows_ref, cols_ref, count_ref, tiles_ref, *refs):
    slab_refs, out_refs = refs[:n_col], refs[n_col : n_col + n_row]
    total_ref, early_ref, basis_ref = refs[n_col + n_row :]
    slots, size, _ = tiles_ref.shape
    width = total_ref.shape[1]
    rows_dev = total_ref.shape[0] // n_row
    piece = early_ref.shape[0] // n_row
    early = jnp.zeros(early_ref.shape, F32)
    for step, slab_ref in zip(distances(n_col), slab_refs):
        place = pl.multiple_of((me_ref[1] ^ step) * rows_dev, rows_dev)
        basis_ref[pl.ds(place, rows_dev), :] = slab_ref[:rows_dev, :]
        early += sum_high_and_low(slab_ref[rows_dev:, :])
    early_ref[...] = early
    total_ref[...] = jnp.zeros_like(total_ref)
    used = count_ref[0]
    for slot in range(slots):
        start = pl.multiple_of(cols_ref[slot] * size, size)
        value = jnp.dot(tiles_ref[slot], basis_ref[pl.ds(start, size), :], preferred_element_type=F32)
        value = jnp.where(slot < used, value, 0.0)
        place = pl.ds(pl.multiple_of(rows_ref[slot] * size, size), size)
        total_ref[place, :] += value
    for step, out_ref in zip(distances(n_row), out_refs):
        row = me_ref[0] ^ step
        out_ref[:rows_dev, :] = total_ref[pl.ds(pl.multiple_of(row * rows_dev, rows_dev), rows_dev), :].astype(BF16)
        out_ref[rows_dev:, :] = high_and_low(early_ref[pl.ds(pl.multiple_of(row * piece, piece), piece), :])


def grams_kernel(now_ref, prev_ref, coupling_ref, *refs):
    part_refs, (shifted_ref, grams_ref, early_ref) = refs[:-3], refs[-3:]
    rows_dev, width = now_ref.shape
    piece = early_ref.shape[0]
    product = jnp.zeros((rows_dev, width), F32)
    early = jnp.zeros((piece, width), F32)
    for part_ref in part_refs:
        product = product + part_ref[:rows_dev, :].astype(F32)
        early = early + sum_high_and_low(part_ref[rows_dev:, :])
    early_ref[...] = early
    shifted = product - dot_nt(prev_ref[...], upper_of(coupling_ref[...]))
    shifted_ref[...] = shifted
    if grams_ref.shape[0] > 2 * width:
        grams_ref[...] = jnp.zeros_like(grams_ref)
    grams_ref[:width, :] = dot_tn(now_ref[...], product)
    grams_ref[width : 2 * width, :] = dot_tn(shifted, shifted)


def spread_kernel(parts_ref, early_ref, out_ref):
    piece = early_ref.shape[0]
    total = parts_ref[0]
    for part in range(1, parts_ref.shape[0]):
        total = total + parts_ref[part]
    early = early_ref[...]
    for part in range(out_ref.shape[0]):
        out_ref[part, :piece, :] = total
        out_ref[part, piece:, :] = early


def eliminate(gram):
    width = gram.shape[0]
    block = 8
    lanes = lax.broadcasted_iota(jnp.int32, (block, width), 1)
    subs = lax.broadcasted_iota(jnp.int32, (block, width), 0)

    def column(strip, k):
        return jnp.broadcast_to(strip[:, k : k + 1], (block, width))

    def row(strip, k):
        return jnp.broadcast_to(strip[k : k + 1, :], (block, width))

    strips = [gram[r : r + block, :] for r in range(0, width, block)]
    finished = []
    for at in range(len(strips)):
        first = at * block
        panel = strips[at]
        columns = [column(panel, first + j) for j in range(block)]
        kept = panel
        for j in range(block):
            here, pivot_lane = subs == j, lanes == first + j
            inverse = 1.0 / row(columns[j], j)
            pivot_row = row(panel, j)
            kept = jnp.where(here, pivot_row, kept)
            unit = jnp.where(pivot_lane, 1.0, pivot_row) * inverse
            factor = columns[j]
            panel = jnp.where(here, unit, jnp.where(pivot_lane, 0.0, panel) - factor * unit)
            for m in range(j + 1, block):
                scaled = row(columns[m], j) * inverse
                columns[m] = jnp.where(here, scaled, columns[m] - factor * scaled)
        finished.append(kept)
        rows = [row(panel, m) for m in range(block)]
        inside = (lanes >= first) & (lanes < first + block)
        for s in range(at + 1, len(strips)):
            terms = [column(strips[s], first + m) * rows[m] for m in range(block)]
            while len(terms) > 1:
                terms = [x + y for x, y in zip(terms[::2], terms[1::2])]
            strips[s] = jnp.where(inside, 0.0, strips[s]) - terms[0]
    return jnp.concatenate(finished, axis=0)


def final_kernel(total_rows, pieces_ref, coupling_ref, now_ref, shifted_ref, basis_ref, projection_ref, rfactor_ref):
    width = now_ref.shape[1]
    piece = pieces_ref.shape[1] // 2
    late = pieces_ref[:, :piece, :].reshape(-1, width)
    early = pieces_ref[:, piece:, :].reshape(-1, width)
    now_product, square = late[:width], late[width : 2 * width]
    now_square, now_prev = early[:width], early[width : 2 * width]
    norm_scale = total_rows**-0.5
    projection = now_product * norm_scale
    projection_ref[...] = projection
    scaled = projection * norm_scale
    cross = now_product - dot_nt(now_prev, upper_of(coupling_ref[...]))
    mixed = dot_tn(scaled, cross - 0.5 * dot(now_square, scaled))
    gram = square - mixed - mixed.T
    reduced = eliminate(gram * (1.0 / total_rows))
    rows = lax.broadcasted_iota(jnp.int32, reduced.shape, 0)
    cols = lax.broadcasted_iota(jnp.int32, reduced.shape, 1)
    diagonal = jnp.sum(jnp.where(rows == cols, reduced, 0.0), axis=1, keepdims=True)
    root = lax.rsqrt(diagonal)
    rfactor_ref[...] = jnp.where(rows <= cols, reduced, 0.0) * root
    inverse = jnp.where(rows > cols, reduced, jnp.where(rows == cols, 1.0, 0.0)) * root
    residual = shifted_ref[...] - dot(now_ref[...], scaled)
    basis_ref[...] = dot_nt(residual, inverse)


def exchange(blocks, axis):
    n = lax.axis_size(axis)
    assert n & (n - 1) == 0
    steps = distances(n)[:-1]
    return [lax.ppermute(block, axis, [(i, i ^ step) for i in range(n)]) for step, block in zip(steps, blocks)] + [blocks[-1]]


def on_device(basis_now, basis_prev, coupling, tiles, tile_rows, tile_cols, tile_counts):
    rows_dev, width = basis_now.shape
    n_row, n_col = lax.axis_size("row"), lax.axis_size("col")
    devices = n_row * n_col
    tile_block = tiles[0, 0]
    total_rows = float(rows_dev * devices)
    piece = -(-2 * width // (8 * devices)) * 8
    smem = pl.BlockSpec(memory_space=pltpu.SMEM)
    vmem = pl.BlockSpec(memory_space=pltpu.VMEM)
    params = pltpu.CompilerParams(vmem_limit_bytes=48 * 1024 * 1024)

    me = jnp.stack([lax.axis_index("row"), lax.axis_index("col")])
    index_arrays = (tile_rows.reshape(-1), tile_cols.reshape(-1), tile_counts.reshape(-1))
    *slabs, rows, cols, count = pl.pallas_call(
        functools.partial(start_kernel, n_row, n_col),
        out_shape=[jax.ShapeDtypeStruct((rows_dev + 2 * n_row * piece, width), BF16)] * n_col
        + [jax.ShapeDtypeStruct(array.shape, array.dtype) for array in index_arrays],
        in_specs=[smem] + [vmem] * 5,
        out_specs=[vmem] * (n_col + 3),
        scratch_shapes=[pltpu.VMEM((devices * piece, width), F32)],
        compiler_params=params,
        name="slab_and_early_grams",
    )(me, *index_arrays, basis_now, basis_prev)
    slabs = exchange(slabs, "col")
    blocks = pl.pallas_call(
        functools.partial(tiles_kernel, n_row, n_col),
        out_shape=[jax.ShapeDtypeStruct((rows_dev + 2 * piece, width), BF16)] * n_row,
        in_specs=[smem] * 4 + [vmem] * (1 + n_col),
        out_specs=[vmem] * n_row,
        scratch_shapes=[
            pltpu.VMEM((n_row * rows_dev, width), F32),
            pltpu.VMEM((n_row * piece, width), F32),
            pltpu.VMEM((n_col * rows_dev, width), BF16),
        ],
        compiler_params=params,
        name="tile_products",
    )(me, rows, cols, count, tile_block, *slabs)
    parts = exchange(blocks, "row")

    shifted, grams, early = pl.pallas_call(
        grams_kernel,
        out_shape=(
            jax.ShapeDtypeStruct((rows_dev, width), F32),
            jax.ShapeDtypeStruct((devices * piece, width), F32),
            jax.ShapeDtypeStruct((piece, width), F32),
        ),
        in_specs=[vmem] * (3 + n_row),
        out_specs=(vmem, vmem, vmem),
        compiler_params=params,
        name="local_grams",
    )(basis_now, basis_prev, coupling, *parts)
    everyone = ("row", "col")
    pieces = lax.all_to_all(grams.reshape(devices, piece, width), everyone, split_axis=0, concat_axis=0, tiled=True)
    copies = pl.pallas_call(
        spread_kernel,
        out_shape=jax.ShapeDtypeStruct((devices, 2 * piece, width), F32),
        in_specs=[vmem, vmem],
        out_specs=vmem,
        compiler_params=params,
        name="sum_and_spread",
    )(pieces, early)
    sums = lax.all_to_all(copies, everyone, split_axis=0, concat_axis=0, tiled=True)
    return pl.pallas_call(
        functools.partial(final_kernel, total_rows),
        out_shape=(
            jax.ShapeDtypeStruct((rows_dev, width), F32),
            jax.ShapeDtypeStruct((width, width), F32),
            jax.ShapeDtypeStruct((width, width), F32),
        ),
        in_specs=[vmem] * 4,
        out_specs=(vmem, vmem, vmem),
        compiler_params=params,
        name="factor_and_basis",
    )(sums, coupling, basis_now, shifted)


def solution(mesh):
    placed = (
        P(("row", "col"), None),
        P(("row", "col"), None),
        P(),
        P("row", "col", None, None, None),
        P("row", "col", None),
        P("row", "col", None),
        P("row", "col"),
    )
    return jax.shard_map(
        on_device,
        mesh=mesh,
        in_specs=placed,
        out_specs=(P(("row", "col"), None), P(), P()),
        check_vma=False,
    )
```

```python
import functools

import jax
import jax.numpy as jnp
from jax import lax
from jax.experimental import pallas as pl
from jax.experimental.pallas import tpu as pltpu
from jax.sharding import PartitionSpec as P

HIGHEST = lax.Precision.HIGHEST
F32 = jnp.float32
BF16 = jnp.bfloat16


def dot(a, b):
    return jnp.dot(a, b, precision=HIGHEST, preferred_element_type=F32)


def dot_tn(a, b, precision=HIGHEST):
    return lax.dot_general(a, b, (((0,), (0,)), ((), ())), precision=precision, preferred_element_type=F32)


def dot_nt(a, b):
    return lax.dot_general(a, b, (((1,), (1,)), ((), ())), precision=HIGHEST, preferred_element_type=F32)


def upper_of(x):
    rows = lax.broadcasted_iota(jnp.int32, x.shape, 0)
    cols = lax.broadcasted_iota(jnp.int32, x.shape, 1)
    return jnp.where(rows <= cols, x, 0.0)


def distances(n):
    return range(n - 1, -1, -1)


def high_and_low(value):
    high = value.astype(BF16)
    low = (value - high.astype(F32)).astype(BF16)
    return jnp.concatenate([high, low], axis=0)


def sum_high_and_low(value):
    half = value.shape[-2] // 2
    value = value.astype(F32)
    return value[..., :half, :] + value[..., half:, :]


def tiles_kernel(n_row, n_col, index_ref, tiles_ref, *refs):
    slab_refs, out_refs = refs[:n_col], refs[n_col : n_col + n_row]
    total_ref, early_ref, basis_ref = refs[n_col + n_row :]
    slots, size, _ = tiles_ref.shape
    width = total_ref.shape[1]
    rows_dev = total_ref.shape[0] // n_row
    piece = early_ref.shape[0] // (n_row * n_col)
    used, my_row, my_col = [index_ref[2 * slots + k] for k in range(3)]
    square = jnp.zeros((width, width), F32)
    cross = jnp.zeros((width, width), F32)
    for step in range(n_col):
        now, prev = slab_refs[step][:rows_dev, :], slab_refs[step][rows_dev:, :]
        owner = lax.rem(my_col + n_col - step, n_col)
        basis_ref[pl.ds(pl.multiple_of(owner * rows_dev, rows_dev), rows_dev), :] = now
        square += dot_tn(now, now, None)
        cross += dot_tn(now, prev, None)
    total_ref[...] = jnp.zeros_like(total_ref)
    for slot in range(slots):
        start = pl.multiple_of(index_ref[slots + slot] * size, size)
        value = jnp.dot(tiles_ref[slot], basis_ref[pl.ds(start, size), :], preferred_element_type=F32)
        value = jnp.where(slot < used, value, 0.0)
        place = pl.ds(pl.multiple_of(index_ref[slot] * size, size), size)
        total_ref[place, :] += value
    if early_ref.shape[0] > 2 * width:
        early_ref[...] = jnp.zeros_like(early_ref)
    early_ref[:width, :] = square
    early_ref[width : 2 * width, :] = cross
    for step, out_ref in zip(distances(n_row), out_refs):
        row = my_row ^ step
        out_ref[:rows_dev, :] = total_ref[pl.ds(pl.multiple_of(row * rows_dev, rows_dev), rows_dev), :].astype(BF16)
        value = early_ref[pl.ds(pl.multiple_of((row * n_col + my_col) * piece, piece), piece), :]
        out_ref[rows_dev:, :] = high_and_low(value)


def grams_kernel(total_rows, n_col, index_ref, now_ref, prev_ref, coupling_ref, *refs):
    part_refs, (shifted_ref, grams_ref, early_ref) = refs[:-3], refs[-3:]
    rows_dev, width = now_ref.shape
    piece = early_ref.shape[0]
    product = jnp.zeros((rows_dev, width), F32)
    early = jnp.zeros((piece, width), F32)
    for part_ref in part_refs:
        product = product + part_ref[:rows_dev, :].astype(F32)
        early = early + sum_high_and_low(part_ref[rows_dev:, :])
    upper = upper_of(coupling_ref[...])
    shifted = product - dot_nt(prev_ref[...], upper)
    shifted_ref[...] = shifted
    if grams_ref.shape[0] > 2 * width:
        grams_ref[...] = jnp.zeros_like(grams_ref)
    grams_ref[:width, :] = dot_tn(now_ref[...], product)
    grams_ref[width : 2 * width, :] = dot_tn(shifted, shifted)
    last = index_ref.shape[0] - 1
    first = (index_ref[last - 1] * n_col + index_ref[last]) * piece
    places = first + lax.broadcasted_iota(jnp.int32, early.shape, 0)
    lanes = lax.broadcasted_iota(jnp.int32, early.shape, 1)
    square = early - jnp.where(places == lanes, total_rows, 0.0)
    early_ref[...] = jnp.where(places < width, square, dot_nt(early, upper))


def spread_kernel(parts_ref, early_ref, out_ref):
    total = parts_ref[0]
    for part in range(1, parts_ref.shape[0]):
        total = total + parts_ref[part]
    value = jnp.concatenate([high_and_low(total), early_ref[...].astype(BF16)], axis=0)
    for part in range(out_ref.shape[0]):
        out_ref[part] = value


def reciprocal(x):
    estimate = pl.reciprocal(x, approx=True)
    estimate = estimate * (2.0 - x * estimate)
    return estimate * (2.0 - x * estimate)


def eliminate(gram):
    width = gram.shape[0]
    block = 8
    lanes = lax.broadcasted_iota(jnp.int32, (block, width), 1)
    subs = lax.broadcasted_iota(jnp.int32, (block, width), 0)

    def column(strip, k):
        return jnp.broadcast_to(strip[:, k : k + 1], (block, width))

    def row(strip, k):
        return jnp.broadcast_to(strip[k : k + 1, :], (block, width))

    strips = [gram[r : r + block, :] for r in range(0, width, block)]
    finished = []
    for at in range(len(strips)):
        first = at * block
        panel = strips[at]
        columns = [column(panel, first + j) for j in range(block)]
        kept = panel
        for j in range(0, block, 2):
            here, there = subs == j, subs == j + 1
            lane, next_lane = lanes == first + j, lanes == first + j + 1
            left, right = columns[j], columns[j + 1]
            a, b, c = row(left, j), row(right, j), row(right, j + 1)
            scale = reciprocal(a * c - b * b)
            top, bottom = row(panel, j), row(panel, j + 1)
            ratio = b * reciprocal(a)
            kept = jnp.where(here, top, jnp.where(there, bottom - ratio * jnp.where(lane, 1.0, top), kept))
            kept = jnp.where(there & lane, -ratio, kept)
            top = jnp.where(lane, 1.0, jnp.where(next_lane, 0.0, top))
            bottom = jnp.where(lane, 0.0, jnp.where(next_lane, 1.0, bottom))
            unit_top = (c * top - b * bottom) * scale
            unit_bottom = (a * bottom - b * top) * scale
            others = jnp.where(lane | next_lane, 0.0, panel) - (left * unit_top + right * unit_bottom)
            panel = jnp.where(here, unit_top, jnp.where(there, unit_bottom, others))
            for m in range(j + 2, block):
                up, down = row(columns[m], j), row(columns[m], j + 1)
                up, down = (c * up - b * down) * scale, (a * down - b * up) * scale
                others = columns[m] - (left * up + right * down)
                columns[m] = jnp.where(here, up, jnp.where(there, down, others))
        finished.append(kept)
        rows = [row(panel, m) for m in range(block)]
        inside = (lanes >= first) & (lanes < first + block)
        for s in range(at + 1, len(strips)):
            terms = [column(strips[s], first + m) * rows[m] for m in range(block)]
            while len(terms) > 1:
                terms = [x + y for x, y in zip(terms[::2], terms[1::2])]
            strips[s] = jnp.where(inside, 0.0, strips[s]) - terms[0]
    return jnp.concatenate(finished, axis=0)


def final_kernel(total_rows, pieces_ref, now_ref, shifted_ref, basis_ref, projection_ref, rfactor_ref):
    width = now_ref.shape[1]
    piece = pieces_ref.shape[1] // 3
    pieces = pieces_ref[...]
    late = sum_high_and_low(pieces[:, : 2 * piece, :]).reshape(-1, width)
    early = pieces[:, 2 * piece :, :].astype(F32).reshape(-1, width)
    now_product, square = late[:width], late[width : 2 * width]
    now_square, shift = early[:width], early[width : 2 * width]
    projection = now_product * total_rows**-0.5
    projection_ref[...] = projection
    scaled = now_product * (1.0 / total_rows)
    half = shift - 0.5 * now_product + 0.5 * dot(now_square, scaled)
    mixed = dot_tn(scaled, half)
    gram = square + mixed + mixed.T
    reduced = eliminate(gram * (1.0 / total_rows))
    rows = lax.broadcasted_iota(jnp.int32, reduced.shape, 0)
    cols = lax.broadcasted_iota(jnp.int32, reduced.shape, 1)
    diagonal = jnp.sum(jnp.where(rows == cols, reduced, 0.0), axis=1, keepdims=True)
    root = lax.rsqrt(diagonal)
    rfactor_ref[...] = jnp.where(rows <= cols, reduced, 0.0) * root
    inverse = jnp.where(rows > cols, reduced, jnp.where(rows == cols, 1.0, 0.0)) * root
    residual = shifted_ref[...] - dot(now_ref[...], scaled)
    basis_ref[...] = dot_nt(residual, inverse)


def gather(block, axis):
    n = lax.axis_size(axis)
    return [block] + [lax.ppermute(block, axis, [(i, (i + step) % n) for i in range(n)]) for step in range(1, n)]


def exchange(blocks, axis):
    n = lax.axis_size(axis)
    assert n & (n - 1) == 0
    steps = distances(n)[:-1]
    return [lax.ppermute(block, axis, [(i, i ^ step) for i in range(n)]) for step, block in zip(steps, blocks)] + [blocks[-1]]


def on_device(basis_now, basis_prev, coupling, tiles, tile_rows, tile_cols, tile_counts):
    rows_dev, width = basis_now.shape
    n_row, n_col = lax.axis_size("row"), lax.axis_size("col")
    devices = n_row * n_col
    tile_block = tiles[0, 0]
    total_rows = float(rows_dev * devices)
    piece = -(-2 * width // (8 * devices)) * 8
    smem = pl.BlockSpec(memory_space=pltpu.SMEM)
    vmem = pl.BlockSpec(memory_space=pltpu.VMEM)
    params = pltpu.CompilerParams(vmem_limit_bytes=48 * 1024 * 1024)

    both = jnp.concatenate([basis_now, basis_prev], axis=0).astype(BF16)
    slabs = gather(both, "col")
    index = jnp.concatenate(
        [tile_rows.reshape(-1), tile_cols.reshape(-1), tile_counts.reshape(-1)]
        + [lax.axis_index(axis).reshape(1) for axis in ("row", "col")]
    )
    blocks = pl.pallas_call(
        functools.partial(tiles_kernel, n_row, n_col),
        out_shape=[jax.ShapeDtypeStruct((rows_dev + 2 * piece, width), BF16)] * n_row,
        in_specs=[smem] + [vmem] * (1 + n_col),
        out_specs=[vmem] * n_row,
        scratch_shapes=[
            pltpu.VMEM((n_row * rows_dev, width), F32),
            pltpu.VMEM((devices * piece, width), F32),
            pltpu.VMEM((n_col * rows_dev, width), BF16),
        ],
        compiler_params=params,
        name="tile_products",
    )(index, tile_block, *slabs)
    parts = exchange(blocks, "row")

    shifted, grams, early = pl.pallas_call(
        functools.partial(grams_kernel, total_rows, n_col),
        out_shape=(
            jax.ShapeDtypeStruct((rows_dev, width), F32),
            jax.ShapeDtypeStruct((devices * piece, width), F32),
            jax.ShapeDtypeStruct((piece, width), F32),
        ),
        in_specs=[smem] + [vmem] * (3 + n_row),
        out_specs=(vmem, vmem, vmem),
        compiler_params=params,
        name="local_grams",
    )(index, basis_now, basis_prev, coupling, *parts)
    everyone = ("row", "col")
    pieces = lax.all_to_all(grams.reshape(devices, piece, width), everyone, split_axis=0, concat_axis=0, tiled=True)
    copies = pl.pallas_call(
        spread_kernel,
        out_shape=jax.ShapeDtypeStruct((devices, 3 * piece, width), BF16),
        in_specs=[vmem, vmem],
        out_specs=vmem,
        compiler_params=params,
        name="sum_and_spread",
    )(pieces, early)
    sums = lax.all_to_all(copies, everyone, split_axis=0, concat_axis=0, tiled=True)
    return pl.pallas_call(
        functools.partial(final_kernel, total_rows),
        out_shape=(
            jax.ShapeDtypeStruct((rows_dev, width), F32),
            jax.ShapeDtypeStruct((width, width), F32),
            jax.ShapeDtypeStruct((width, width), F32),
        ),
        in_specs=[vmem] * 3,
        out_specs=(vmem, vmem, vmem),
        compiler_params=params,
        name="factor_and_basis",
    )(sums, basis_now, shifted)


def solution(mesh):
    placed = (
        P(("row", "col"), None),
        P(("row", "col"), None),
        P(),
        P("row", "col", None, None, None),
        P("row", "col", None),
        P("row", "col", None),
        P("row", "col"),
    )
    return jax.shard_map(
        on_device,
        mesh=mesh,
        in_specs=placed,
        out_specs=(P(("row", "col"), None), P(), P()),
        check_vma=False,
    )
```

```python
import functools

import jax
import jax.numpy as jnp
from jax import lax
from jax.experimental import pallas as pl
from jax.experimental.pallas import tpu as pltpu
from jax.sharding import PartitionSpec as P

HIGHEST = lax.Precision.HIGHEST
F32 = jnp.float32
BF16 = jnp.bfloat16


def dot(a, b):
    return jnp.dot(a, b, precision=HIGHEST, preferred_element_type=F32)


def dot_tn(a, b, precision=HIGHEST):
    return lax.dot_general(a, b, (((0,), (0,)), ((), ())), precision=precision, preferred_element_type=F32)


def dot_nt(a, b):
    return lax.dot_general(a, b, (((1,), (1,)), ((), ())), precision=HIGHEST, preferred_element_type=F32)


def upper_of(x):
    rows = lax.broadcasted_iota(jnp.int32, x.shape, 0)
    cols = lax.broadcasted_iota(jnp.int32, x.shape, 1)
    return jnp.where(rows <= cols, x, 0.0)


def distances(n):
    return range(n - 1, -1, -1)


def high_and_low(value):
    high = value.astype(BF16)
    low = (value - high.astype(F32)).astype(BF16)
    return jnp.concatenate([high, low], axis=0)


def sum_high_and_low(value):
    half = value.shape[-2] // 2
    value = value.astype(F32)
    return value[..., :half, :] + value[..., half:, :]


def tiles_kernel(n_row, n_col, total_rows, index_ref, tiles_ref, basis_ref, coupling_ref, *refs):
    half = n_row // 2
    mirror_refs, near_refs, (far_ref, own_ref, total_ref, early_ref) = refs[: half - 1], refs[half - 1 : -4], refs[-4:]
    slots, size, _ = tiles_ref.shape
    width = total_ref.shape[1]
    rows_dev = total_ref.shape[0] // n_row
    piece = early_ref.shape[0] // (n_row * n_col)
    used, my_row, my_col = [index_ref[2 * slots + k] for k in range(3)]
    total_ref[...] = jnp.zeros_like(total_ref)
    per_slab = rows_dev // size
    for slot in range(slots):
        col = index_ref[slots + slot]
        start = pl.multiple_of((2 * per_slab * (col // per_slab) + lax.rem(col, per_slab)) * size, size)
        value = jnp.dot(tiles_ref[slot], basis_ref[pl.ds(start, size), :], preferred_element_type=F32)
        value = jnp.where(slot < used, value, 0.0)
        place = pl.ds(pl.multiple_of(index_ref[slot] * size, size), size)
        total_ref[place, :] += value
    square = jnp.zeros((width, width), F32)
    cross = jnp.zeros((width, width), F32)
    for slab in range(n_col):
        now = basis_ref[2 * slab * rows_dev : (2 * slab + 1) * rows_dev, :]
        prev = basis_ref[(2 * slab + 1) * rows_dev : (2 * slab + 2) * rows_dev, :]
        square += dot_tn(now, now, None)
        cross += dot_tn(now, prev, None)
    rows = lax.broadcasted_iota(jnp.int32, square.shape, 0)
    cols = lax.broadcasted_iota(jnp.int32, square.shape, 1)
    if early_ref.shape[0] > 2 * width:
        early_ref[...] = jnp.zeros_like(early_ref)
    early_ref[:width, :] = square - jnp.where(rows == cols, total_rows / n_row, 0.0)
    early_ref[width : 2 * width, :] = dot_nt(cross, upper_of(coupling_ref[...]))

    def parts_of(row):
        slab = total_ref[pl.ds(pl.multiple_of(row * rows_dev, rows_dev), rows_dev), :]
        return slab, early_ref[pl.ds(pl.multiple_of((row * n_col + my_col) * piece, piece), piece), :]

    for step, mirror_ref, near_ref in zip(distances(half), mirror_refs, near_refs):
        write_block(mirror_ref, *parts_of(my_row ^ (step + half)))
        write_block(near_ref, *parts_of(my_row ^ step))
    for row, ref in ((my_row ^ half, far_ref), (my_row, own_ref)):
        ref[:rows_dev, :], ref[rows_dev:, :] = parts_of(row)


def write_block(ref, slab, early):
    rows_dev = slab.shape[0]
    ref[:rows_dev, :] = slab.astype(BF16)
    ref[rows_dev:, :] = high_and_low(early)


def add_blocks(own_ref, block_refs, rows_dev):
    slab, early = own_ref[:rows_dev, :], own_ref[rows_dev:, :]
    for ref in block_refs:
        slab = slab + ref[:rows_dev, :].astype(F32)
        early = early + sum_high_and_low(ref[rows_dev:, :])
    return slab, early


def mirror_kernel(rows_dev, own_ref, *refs):
    block_refs, out_ref = refs[:-1], refs[-1]
    write_block(out_ref, *add_blocks(own_ref, block_refs, rows_dev))


def grams_kernel(now_ref, prev_ref, coupling_ref, own_ref, *refs):
    block_refs, (shifted_ref, grams_ref, early_ref) = refs[:-3], refs[-3:]
    rows_dev, width = now_ref.shape
    product, early_ref[...] = add_blocks(own_ref, block_refs, rows_dev)
    shifted = product - dot_nt(prev_ref[...], upper_of(coupling_ref[...]))
    shifted_ref[...] = shifted
    if grams_ref.shape[0] > 2 * width:
        grams_ref[...] = jnp.zeros_like(grams_ref)
    grams_ref[:width, :] = dot_tn(now_ref[...], product)
    grams_ref[width : 2 * width, :] = dot_tn(shifted, shifted)


def spread_kernel(parts_ref, early_ref, out_ref):
    total = parts_ref[0]
    for part in range(1, parts_ref.shape[0]):
        total = total + parts_ref[part]
    value = jnp.concatenate([high_and_low(total), early_ref[...].astype(BF16)], axis=0)
    for part in range(out_ref.shape[0]):
        out_ref[part] = value


def reciprocal(x):
    estimate = pl.reciprocal(x, approx=True)
    estimate = estimate * (2.0 - x * estimate)
    return estimate * (2.0 - x * estimate)


def eliminate(gram):
    width = gram.shape[0]
    block = 8
    lanes = lax.broadcasted_iota(jnp.int32, (block, width), 1)
    subs = lax.broadcasted_iota(jnp.int32, (block, width), 0)

    def column(strip, k):
        return jnp.broadcast_to(strip[:, k : k + 1], (block, width))

    def row(strip, k):
        return jnp.broadcast_to(strip[k : k + 1, :], (block, width))

    strips = [gram[r : r + block, :] for r in range(0, width, block)]
    finished = []
    per_group = 4
    for begin in range(0, len(strips), per_group):
        group = strips[:per_group]
        for at in range(per_group):
            first = (begin + at) * block
            panel = group[at]
            columns = [column(panel, first + j) for j in range(block)]
            kept = panel
            for j in range(0, block, 2):
                here, there = subs == j, subs == j + 1
                lane, next_lane = lanes == first + j, lanes == first + j + 1
                left, right = columns[j], columns[j + 1]
                a, b, c = row(left, j), row(right, j), row(right, j + 1)
                scale = reciprocal(a * c - b * b)
                top, bottom = row(panel, j), row(panel, j + 1)
                ratio = b * reciprocal(a)
                kept = jnp.where(here, top, jnp.where(there, bottom - ratio * jnp.where(lane, 1.0, top), kept))
                kept = jnp.where(there & lane, -ratio, kept)
                top = jnp.where(lane, 1.0, jnp.where(next_lane, 0.0, top))
                bottom = jnp.where(lane, 0.0, jnp.where(next_lane, 1.0, bottom))
                unit_top = (c * top - b * bottom) * scale
                unit_bottom = (a * bottom - b * top) * scale
                others = jnp.where(lane | next_lane, 0.0, panel) - (left * unit_top + right * unit_bottom)
                panel = jnp.where(here, unit_top, jnp.where(there, unit_bottom, others))
                for m in range(j + 2, block):
                    up, down = row(columns[m], j), row(columns[m], j + 1)
                    up, down = (c * up - b * down) * scale, (a * down - b * up) * scale
                    others = columns[m] - (left * up + right * down)
                    columns[m] = jnp.where(here, up, jnp.where(there, down, others))
            finished.append(kept)
            group[at] = panel
            rows = [row(panel, m) for m in range(block)]
            inside = (lanes >= first) & (lanes < first + block)
            for s in range(per_group):
                if s != at:
                    terms = [column(group[s], first + m) * rows[m] for m in range(block)]
                    while len(terms) > 1:
                        terms = [x + y for x, y in zip(terms[::2], terms[1::2])]
                    group[s] = jnp.where(inside, 0.0, group[s]) - terms[0]
        strips = strips[per_group:]
        if strips:
            first, last = begin * block, (begin + per_group) * block
            below = jnp.concatenate(strips, axis=0)
            solved = [jnp.zeros((first, width), F32)] if first else []
            solved = jnp.concatenate(solved + group + [jnp.zeros((width - last, width), F32)], axis=0)
            cols = lax.broadcasted_iota(jnp.int32, below.shape, 1)
            below = jnp.where((cols >= first) & (cols < last), 0.0, below) - dot(below, solved)
            strips = [below[r : r + block, :] for r in range(0, below.shape[0], block)]
    return jnp.concatenate(finished, axis=0)


def final_kernel(total_rows, pieces_ref, now_ref, shifted_ref, basis_ref, projection_ref, rfactor_ref):
    width = now_ref.shape[1]
    piece = pieces_ref.shape[1] // 3
    pieces = pieces_ref[...]
    late = sum_high_and_low(pieces[:, : 2 * piece, :]).reshape(-1, width)
    early = pieces[:, 2 * piece :, :].astype(F32).reshape(-1, width)
    now_product, square = late[:width], late[width : 2 * width]
    now_square, shift = early[:width], early[width : 2 * width]
    projection = now_product * total_rows**-0.5
    projection_ref[...] = projection
    scaled = now_product * (1.0 / total_rows)
    half = shift - 0.5 * now_product + 0.5 * dot(now_square, scaled)
    mixed = dot_tn(scaled, half)
    gram = square + mixed + mixed.T
    reduced = eliminate(gram * (1.0 / total_rows))
    rows = lax.broadcasted_iota(jnp.int32, reduced.shape, 0)
    cols = lax.broadcasted_iota(jnp.int32, reduced.shape, 1)
    diagonal = jnp.sum(jnp.where(rows == cols, reduced, 0.0), axis=1, keepdims=True)
    root = lax.rsqrt(diagonal)
    rfactor_ref[...] = jnp.where(rows <= cols, reduced, 0.0) * root
    inverse = jnp.where(rows > cols, reduced, jnp.where(rows == cols, 1.0, 0.0)) * root
    residual = shifted_ref[...] - dot(now_ref[...], scaled)
    basis_ref[...] = dot_nt(residual, inverse)


def exchange(blocks, axis, steps):
    n = lax.axis_size(axis)
    assert n & (n - 1) == 0
    return [lax.ppermute(block, axis, [(i, i ^ step) for i in range(n)]) for step, block in zip(steps, blocks)]


def on_device(basis_now, basis_prev, coupling, tiles, tile_rows, tile_cols, tile_counts):
    rows_dev, width = basis_now.shape
    n_row, n_col = lax.axis_size("row"), lax.axis_size("col")
    devices = n_row * n_col
    tile_block = tiles[0, 0]
    total_rows = float(rows_dev * devices)
    piece = -(-2 * width // (8 * devices)) * 8
    smem = pl.BlockSpec(memory_space=pltpu.SMEM)
    vmem = pl.BlockSpec(memory_space=pltpu.VMEM)
    params = pltpu.CompilerParams(vmem_limit_bytes=48 * 1024 * 1024)

    both = jnp.concatenate([basis_now, basis_prev], axis=0).astype(BF16)
    gathered = lax.all_gather(both, "col", axis=0, tiled=True)
    index = jnp.concatenate(
        [tile_rows.reshape(-1), tile_cols.reshape(-1), tile_counts.reshape(-1)]
        + [lax.axis_index(axis).reshape(1) for axis in ("row", "col")]
    )
    half = n_row // 2
    block = jax.ShapeDtypeStruct((rows_dev + 2 * piece, width), BF16)
    sums = jax.ShapeDtypeStruct((rows_dev + piece, width), F32)
    *blocks, far, own = pl.pallas_call(
        functools.partial(tiles_kernel, n_row, n_col, total_rows),
        out_shape=[block] * (2 * half - 2) + [sums] * 2,
        in_specs=[smem] + [vmem] * 3,
        out_specs=[vmem] * (2 * half),
        scratch_shapes=[
            pltpu.VMEM((n_row * rows_dev, width), F32),
            pltpu.VMEM((devices * piece, width), F32),
        ],
        compiler_params=params,
        name="tile_products",
    )(index, tile_block, gathered, coupling)
    steps = distances(half)[:-1]
    mirrors = exchange(blocks[: half - 1], "row", steps)
    near = exchange(blocks[half - 1 :], "row", steps)
    mirror = pl.pallas_call(
        functools.partial(mirror_kernel, rows_dev),
        out_shape=block,
        in_specs=[vmem] * half,
        out_specs=vmem,
        compiler_params=params,
        name="mirror_sum",
    )(far, *mirrors)
    across = exchange([mirror], "row", [half])

    shifted, grams, early = pl.pallas_call(
        grams_kernel,
        out_shape=(
            jax.ShapeDtypeStruct((rows_dev, width), F32),
            jax.ShapeDtypeStruct((devices * piece, width), F32),
            jax.ShapeDtypeStruct((piece, width), F32),
        ),
        in_specs=[vmem] * (4 + half),
        out_specs=(vmem, vmem, vmem),
        compiler_params=params,
        name="local_grams",
    )(basis_now, basis_prev, coupling, own, *near, *across)
    everyone = ("row", "col")
    pieces = lax.all_to_all(grams.reshape(devices, piece, width), everyone, split_axis=0, concat_axis=0, tiled=True)
    copies = pl.pallas_call(
        spread_kernel,
        out_shape=jax.ShapeDtypeStruct((devices, 3 * piece, width), BF16),
        in_specs=[vmem, vmem],
        out_specs=vmem,
        compiler_params=params,
        name="sum_and_spread",
    )(pieces, early)
    gathered_sums = lax.all_to_all(copies, everyone, split_axis=0, concat_axis=0, tiled=True)
    return pl.pallas_call(
        functools.partial(final_kernel, total_rows),
        out_shape=(
            jax.ShapeDtypeStruct((rows_dev, width), F32),
            jax.ShapeDtypeStruct((width, width), F32),
            jax.ShapeDtypeStruct((width, width), F32),
        ),
        in_specs=[vmem] * 3,
        out_specs=(vmem, vmem, vmem),
        compiler_params=params,
        name="factor_and_basis",
    )(gathered_sums, basis_now, shifted)


def solution(mesh):
    placed = (
        P(("row", "col"), None),
        P(("row", "col"), None),
        P(),
        P("row", "col", None, None, None),
        P("row", "col", None),
        P("row", "col", None),
        P("row", "col"),
    )
    return jax.shard_map(
        on_device,
        mesh=mesh,
        in_specs=placed,
        out_specs=(P(("row", "col"), None), P(), P()),
        check_vma=False,
    )
```

```python
import functools

import jax
import jax.numpy as jnp
from jax import lax
from jax.experimental import pallas as pl
from jax.experimental.pallas import tpu as pltpu
from jax.sharding import PartitionSpec as P

HIGHEST = lax.Precision.HIGHEST
F32 = jnp.float32
BF16 = jnp.bfloat16


def dot(a, b):
    return jnp.dot(a, b, precision=HIGHEST, preferred_element_type=F32)


def dot_tn(a, b, precision=HIGHEST):
    return lax.dot_general(a, b, (((0,), (0,)), ((), ())), precision=precision, preferred_element_type=F32)


def dot_nt(a, b):
    return lax.dot_general(a, b, (((1,), (1,)), ((), ())), precision=HIGHEST, preferred_element_type=F32)


def upper_of(x):
    rows = lax.broadcasted_iota(jnp.int32, x.shape, 0)
    cols = lax.broadcasted_iota(jnp.int32, x.shape, 1)
    return jnp.where(rows <= cols, x, 0.0)


def distances(n):
    return range(n - 1, -1, -1)


def high_and_low(value):
    high = value.astype(BF16)
    low = (value - high.astype(F32)).astype(BF16)
    return jnp.concatenate([high, low], axis=0)


def sum_high_and_low(value):
    half = value.shape[-2] // 2
    value = value.astype(F32)
    return value[..., :half, :] + value[..., half:, :]


def tiles_kernel(n_row, n_col, total_rows, me_ref, rows_ref, cols_ref, count_ref, tiles_ref, basis_ref, coupling_ref, *refs):
    half = n_row // 2
    mirror_refs, near_refs, (far_ref, own_ref, total_ref, early_ref) = refs[: half - 1], refs[half - 1 : -4], refs[-4:]
    slots, size, _ = tiles_ref.shape
    width = total_ref.shape[1]
    rows_dev = total_ref.shape[0] // n_row
    piece = early_ref.shape[0] // (n_row * n_col)
    my_row, my_col = me_ref[0], me_ref[1]
    total_ref[...] = jnp.zeros_like(total_ref)
    grams = jnp.zeros((width, 2 * width), F32)
    for slab in range(n_col):
        now = basis_ref[2 * slab * rows_dev : (2 * slab + 1) * rows_dev, :]
        prev = basis_ref[(2 * slab + 1) * rows_dev : (2 * slab + 2) * rows_dev, :]
        grams += dot_tn(now, jnp.concatenate([now, prev], axis=1), None)
    square, cross = grams[:, :width], grams[:, width:]
    rows = lax.broadcasted_iota(jnp.int32, square.shape, 0)
    cols = lax.broadcasted_iota(jnp.int32, square.shape, 1)
    if early_ref.shape[0] > 2 * width:
        early_ref[...] = jnp.zeros_like(early_ref)
    early_ref[:width, :] = square - jnp.where(rows == cols, total_rows / n_row, 0.0)
    early_ref[width : 2 * width, :] = dot_nt(cross, upper_of(coupling_ref[...]))
    used = count_ref[...]
    per_slab = rows_dev // size
    for slot in range(slots):
        col = cols_ref[0, 0, slot]
        start = pl.multiple_of((2 * per_slab * (col // per_slab) + lax.rem(col, per_slab)) * size, size)
        value = jnp.dot(tiles_ref[slot], basis_ref[pl.ds(start, size), :], preferred_element_type=F32)
        value = value * (slot < used).astype(F32)
        place = pl.ds(pl.multiple_of(rows_ref[0, 0, slot] * size, size), size)
        total_ref[place, :] += value

    def parts_of(row):
        slab = total_ref[pl.ds(pl.multiple_of(row * rows_dev, rows_dev), rows_dev), :]
        return slab, early_ref[pl.ds(pl.multiple_of((row * n_col + my_col) * piece, piece), piece), :]

    for step, mirror_ref, near_ref in zip(distances(half), mirror_refs, near_refs):
        write_block(mirror_ref, *parts_of(my_row ^ (step + half)))
        write_block(near_ref, *parts_of(my_row ^ step))
    for row, ref in ((my_row ^ half, far_ref), (my_row, own_ref)):
        ref[:rows_dev, :], ref[rows_dev:, :] = parts_of(row)


def write_block(ref, slab, early):
    rows_dev = slab.shape[0]
    ref[:rows_dev, :] = slab.astype(BF16)
    ref[rows_dev:, :] = high_and_low(early)


def add_blocks(own_ref, block_refs, rows_dev):
    slab, early = own_ref[:rows_dev, :], own_ref[rows_dev:, :]
    for ref in block_refs:
        slab = slab + ref[:rows_dev, :].astype(F32)
        early = early + sum_high_and_low(ref[rows_dev:, :])
    return slab, early


def mirror_kernel(rows_dev, own_ref, *refs):
    block_refs, out_ref = refs[:-1], refs[-1]
    write_block(out_ref, *add_blocks(own_ref, block_refs, rows_dev))


def shift_kernel(prev_ref, coupling_ref, shift_ref):
    shift_ref[...] = dot_nt(prev_ref[...], upper_of(coupling_ref[...]))


def grams_kernel(now_ref, shift_ref, own_ref, *refs):
    block_refs, (shifted_ref, grams_ref, early_ref) = refs[:-3], refs[-3:]
    rows_dev, width = now_ref.shape
    product, early_ref[...] = add_blocks(own_ref, block_refs, rows_dev)
    shifted = product - shift_ref[...]
    shifted_ref[...] = shifted
    if grams_ref.shape[0] > 2 * width:
        grams_ref[...] = jnp.zeros_like(grams_ref)
    grams_ref[:width, :] = dot_tn(now_ref[...], product)
    grams_ref[width : 2 * width, :] = dot_tn(shifted, shifted)


def spread_kernel(parts_ref, early_ref, out_ref):
    total = parts_ref[0]
    for part in range(1, parts_ref.shape[0]):
        total = total + parts_ref[part]
    value = jnp.concatenate([high_and_low(total), early_ref[...].astype(BF16)], axis=0)
    for part in range(out_ref.shape[0]):
        out_ref[part] = value


def split(x):
    high = x.astype(BF16)
    return high, (x - high.astype(F32)).astype(BF16)


def dot3(a, b, dims=((1,), (0,))):
    (a_high, a_low), (b_high, b_low) = split(a), split(b)

    def one(x, y):
        return lax.dot_general(x, y, (dims, ((), ())), preferred_element_type=F32)

    return one(a_high, b_low) + one(a_low, b_high) + one(a_high, b_high)


def eliminate(gram):
    width = gram.shape[0]
    block, per_group = 16, 2
    lanes = lax.broadcasted_iota(jnp.int32, (block, width), 1)
    subs = lax.broadcasted_iota(jnp.int32, (block, width), 0)

    def column(strip, k):
        return jnp.broadcast_to(strip[:, k : k + 1], (block, width))

    def row(strip, k):
        return jnp.broadcast_to(strip[k : k + 1, :], (block, width))

    strips = [gram[r : r + block, :] for r in range(0, width, block)]
    finished = []
    for begin in range(0, len(strips), per_group):
        group = strips[:per_group]
        for at in range(per_group):
            first = (begin + at) * block
            panel = group[at]
            columns = [column(panel, first + j) for j in range(block)]
            kept = panel
            for j in range(0, block, 2):
                here, there = subs == j, subs == j + 1
                lane, next_lane = lanes == first + j, lanes == first + j + 1
                left, right = columns[j], columns[j + 1]
                a, b, c = row(left, j), row(right, j), row(right, j + 1)
                scale = 1.0 / (a * c - b * b)
                top, bottom = row(panel, j), row(panel, j + 1)
                ratio = b / a
                kept = jnp.where(here, top, jnp.where(there, bottom - ratio * jnp.where(lane, 1.0, top), kept))
                kept = jnp.where(there & lane, -ratio, kept)
                top = jnp.where(lane, 1.0, jnp.where(next_lane, 0.0, top))
                bottom = jnp.where(lane, 0.0, jnp.where(next_lane, 1.0, bottom))
                unit_top = (c * top - b * bottom) * scale
                unit_bottom = (a * bottom - b * top) * scale
                others = jnp.where(lane | next_lane, 0.0, panel) - (left * unit_top + right * unit_bottom)
                panel = jnp.where(here, unit_top, jnp.where(there, unit_bottom, others))
                for m in range(j + 2, block):
                    up, down = row(columns[m], j), row(columns[m], j + 1)
                    up, down = (c * up - b * down) * scale, (a * down - b * up) * scale
                    others = columns[m] - (left * up + right * down)
                    columns[m] = jnp.where(here, up, jnp.where(there, down, others))
            finished.append(kept)
            group[at] = panel
            rows = [row(panel, m) for m in range(block)]
            inside = (lanes >= first) & (lanes < first + block)
            for s in range(per_group):
                if s != at:
                    terms = [column(group[s], first + m) * rows[m] for m in range(block)]
                    while len(terms) > 1:
                        terms = [x + y for x, y in zip(terms[::2], terms[1::2])]
                    group[s] = jnp.where(inside, 0.0, group[s]) - terms[0]
        strips = strips[per_group:]
        if strips:
            first, last = begin * block, (begin + per_group) * block
            below = jnp.concatenate(strips, axis=0)
            solved = [jnp.zeros((first, width), F32)] if first else []
            solved = jnp.concatenate(solved + group + [jnp.zeros((width - last, width), F32)], axis=0)
            cols = lax.broadcasted_iota(jnp.int32, below.shape, 1)
            below = jnp.where((cols >= first) & (cols < last), 0.0, below) - dot3(below, solved)
            strips = [below[r : r + block, :] for r in range(0, below.shape[0], block)]
    return jnp.concatenate(finished, axis=0)


def final_kernel(total_rows, pieces_ref, now_ref, shifted_ref, basis_ref, projection_ref, rfactor_ref):
    width = now_ref.shape[1]
    piece = pieces_ref.shape[1] // 3
    pieces = pieces_ref[...]
    late = sum_high_and_low(pieces[:, : 2 * piece, :]).reshape(-1, width)
    early = pieces[:, 2 * piece :, :].astype(F32).reshape(-1, width)
    now_product, square = late[:width], late[width : 2 * width]
    now_square, shift = early[:width], early[width : 2 * width]
    projection = now_product * total_rows**-0.5
    projection_ref[...] = projection
    scaled = now_product * (1.0 / total_rows)
    half = shift - 0.5 * now_product + 0.5 * dot3(now_square, scaled)
    mixed = dot3(scaled, half, ((0,), (0,)))
    gram = square + mixed + mixed.T
    reduced = eliminate(gram * (1.0 / total_rows))
    rows = lax.broadcasted_iota(jnp.int32, reduced.shape, 0)
    cols = lax.broadcasted_iota(jnp.int32, reduced.shape, 1)
    diagonal = jnp.sum(jnp.where(rows == cols, reduced, 0.0), axis=1, keepdims=True)
    root = lax.rsqrt(diagonal)
    rfactor_ref[...] = jnp.where(rows <= cols, reduced, 0.0) * root
    inverse = jnp.where(rows > cols, reduced, jnp.where(rows == cols, 1.0, 0.0)) * root
    residual = shifted_ref[...] - dot3(now_ref[...], scaled)
    basis_ref[...] = dot3(residual, inverse, ((1,), (1,)))


def exchange(blocks, axis, steps):
    n = lax.axis_size(axis)
    assert n & (n - 1) == 0
    return [lax.ppermute(block, axis, [(i, i ^ step) for i in range(n)]) for step, block in zip(steps, blocks)]


def on_device(basis_now, basis_prev, coupling, tiles, tile_rows, tile_cols, tile_counts):
    rows_dev, width = basis_now.shape
    n_row, n_col = lax.axis_size("row"), lax.axis_size("col")
    devices = n_row * n_col
    tile_block = tiles[0, 0]
    total_rows = float(rows_dev * devices)
    piece = -(-2 * width // (8 * devices)) * 8
    smem = pl.BlockSpec(memory_space=pltpu.SMEM)
    vmem = pl.BlockSpec(memory_space=pltpu.VMEM)
    params = pltpu.CompilerParams(vmem_limit_bytes=48 * 1024 * 1024)

    both = jnp.concatenate([basis_now, basis_prev], axis=0).astype(BF16)
    gathered = lax.all_gather(both, "col", axis=0, tiled=True)
    me = jnp.stack([lax.axis_index("row"), lax.axis_index("col")])
    half = n_row // 2
    block = jax.ShapeDtypeStruct((rows_dev + 2 * piece, width), BF16)
    sums = jax.ShapeDtypeStruct((rows_dev + piece, width), F32)
    *blocks, far, own = pl.pallas_call(
        functools.partial(tiles_kernel, n_row, n_col, total_rows),
        out_shape=[block] * (2 * half - 2) + [sums] * 2,
        in_specs=[smem] * 3 + [vmem] * 4,
        out_specs=[vmem] * (2 * half),
        scratch_shapes=[
            pltpu.VMEM((n_row * rows_dev, width), F32),
            pltpu.VMEM((devices * piece, width), F32),
        ],
        compiler_params=params,
        name="tile_products",
    )(me, tile_rows, tile_cols, tile_counts, tile_block, gathered, coupling)
    steps = distances(half)[:-1]
    mirrors = exchange(blocks[: half - 1], "row", steps)
    near = exchange(blocks[half - 1 :], "row", steps)
    mirror = pl.pallas_call(
        functools.partial(mirror_kernel, rows_dev),
        out_shape=block,
        in_specs=[vmem] * half,
        out_specs=vmem,
        compiler_params=params,
        name="mirror_sum",
    )(far, *mirrors)
    across = exchange([mirror], "row", [half])

    shift = pl.pallas_call(
        shift_kernel,
        out_shape=jax.ShapeDtypeStruct((rows_dev, width), F32),
        in_specs=[vmem] * 2,
        out_specs=vmem,
        compiler_params=params,
        cost_estimate=pl.CostEstimate(flops=12 * rows_dev * width * width, bytes_accessed=12 * rows_dev * width, transcendentals=0),
        name="shift_by_previous",
    )(basis_prev, coupling)
    shifted, grams, early = pl.pallas_call(
        grams_kernel,
        out_shape=(
            jax.ShapeDtypeStruct((rows_dev, width), F32),
            jax.ShapeDtypeStruct((devices * piece, width), F32),
            jax.ShapeDtypeStruct((piece, width), F32),
        ),
        in_specs=[vmem] * (3 + half),
        out_specs=(vmem, vmem, vmem),
        compiler_params=params,
        name="local_grams",
    )(basis_now, shift, own, *near, *across)
    everyone = ("row", "col")
    pieces = lax.all_to_all(grams.reshape(devices, piece, width), everyone, split_axis=0, concat_axis=0, tiled=True)
    copies = pl.pallas_call(
        spread_kernel,
        out_shape=jax.ShapeDtypeStruct((devices, 3 * piece, width), BF16),
        in_specs=[vmem, vmem],
        out_specs=vmem,
        compiler_params=params,
        name="sum_and_spread",
    )(pieces, early)
    gathered_sums = lax.all_to_all(copies, everyone, split_axis=0, concat_axis=0, tiled=True)
    return pl.pallas_call(
        functools.partial(final_kernel, total_rows),
        out_shape=(
            jax.ShapeDtypeStruct((rows_dev, width), F32),
            jax.ShapeDtypeStruct((width, width), F32),
            jax.ShapeDtypeStruct((width, width), F32),
        ),
        in_specs=[vmem] * 3,
        out_specs=(vmem, vmem, vmem),
        compiler_params=params,
        name="factor_and_basis",
    )(gathered_sums, basis_now, shifted)


def solution(mesh):
    placed = (
        P(("row", "col"), None),
        P(("row", "col"), None),
        P(),
        P("row", "col", None, None, None),
        P("row", "col", None),
        P("row", "col", None),
        P("row", "col"),
    )
    return jax.shard_map(
        on_device,
        mesh=mesh,
        in_specs=placed,
        out_specs=(P(("row", "col"), None), P(), P()),
        check_vma=False,
    )
```

```python
import functools

import jax
import jax.numpy as jnp
from jax import lax
from jax.experimental import pallas as pl
from jax.experimental.pallas import tpu as pltpu
from jax.sharding import PartitionSpec as P

HIGHEST = lax.Precision.HIGHEST
F32 = jnp.float32
BF16 = jnp.bfloat16


def dot(a, b):
    return jnp.dot(a, b, precision=HIGHEST, preferred_element_type=F32)


def dot_tn(a, b, precision=HIGHEST):
    return lax.dot_general(a, b, (((0,), (0,)), ((), ())), precision=precision, preferred_element_type=F32)


def dot_nt(a, b):
    return lax.dot_general(a, b, (((1,), (1,)), ((), ())), precision=HIGHEST, preferred_element_type=F32)


def upper_of(x):
    rows = lax.broadcasted_iota(jnp.int32, x.shape, 0)
    cols = lax.broadcasted_iota(jnp.int32, x.shape, 1)
    return jnp.where(rows <= cols, x, 0.0)


def distances(n):
    return range(n - 1, -1, -1)


def high_and_low(value):
    high = value.astype(BF16)
    low = (value - high.astype(F32)).astype(BF16)
    return jnp.concatenate([high, low], axis=0)


def sum_high_and_low(value):
    half = value.shape[-2] // 2
    value = value.astype(F32)
    return value[..., :half, :] + value[..., half:, :]


def tiles_kernel(n_row, n_col, total_rows, me_ref, rows_hbm, cols_hbm, used_ref, tiles_ref, basis_ref, coupling_ref, *refs):
    half = n_row // 2
    refs, (far_ref, own_ref, total_ref, early_ref, rows_ref, cols_ref, sems) = refs[:-7], refs[-7:]
    mirror_refs, near_refs = refs[: half - 1], refs[half - 1 :]
    copies = [
        pltpu.make_async_copy(source, target, sems.at[k])
        for k, (source, target) in enumerate(((rows_hbm, rows_ref), (cols_hbm, cols_ref)))
    ]
    for copy in copies:
        copy.start()
    slots, size, _ = tiles_ref.shape
    width = total_ref.shape[1]
    rows_dev = total_ref.shape[0] // n_row
    piece = early_ref.shape[0] // (n_row * n_col)
    my_row, my_col = me_ref[0], me_ref[1]
    total_ref[...] = jnp.zeros_like(total_ref)
    grams = jnp.zeros((width, 2 * width), F32)
    for slab in range(n_col):
        now = basis_ref[2 * slab * rows_dev : (2 * slab + 1) * rows_dev, :]
        prev = basis_ref[(2 * slab + 1) * rows_dev : (2 * slab + 2) * rows_dev, :]
        grams += dot_tn(now, jnp.concatenate([now, prev], axis=1), None)
    square, cross = grams[:, :width], grams[:, width:]
    rows = lax.broadcasted_iota(jnp.int32, square.shape, 0)
    cols = lax.broadcasted_iota(jnp.int32, square.shape, 1)
    if early_ref.shape[0] > 2 * width:
        early_ref[...] = jnp.zeros_like(early_ref)
    early_ref[:width, :] = square - jnp.where(rows == cols, total_rows / n_row, 0.0)
    early_ref[width : 2 * width, :] = dot_nt(cross, upper_of(coupling_ref[...]))
    for copy in copies:
        copy.wait()
    per_slab = rows_dev // size
    for slot in range(slots):
        col = cols_ref[0, 0, slot]
        start = pl.multiple_of((2 * per_slab * (col // per_slab) + lax.rem(col, per_slab)) * size, size)
        value = jnp.dot(tiles_ref[slot], basis_ref[pl.ds(start, size), :], preferred_element_type=F32)
        value = value * used_ref[slot : slot + 1, :]
        place = pl.ds(pl.multiple_of(rows_ref[0, 0, slot] * size, size), size)
        total_ref[place, :] += value

    def parts_of(row):
        slab = total_ref[pl.ds(pl.multiple_of(row * rows_dev, rows_dev), rows_dev), :]
        return slab, early_ref[pl.ds(pl.multiple_of((row * n_col + my_col) * piece, piece), piece), :]

    for step, mirror_ref, near_ref in zip(distances(half), mirror_refs, near_refs):
        write_block(mirror_ref, *parts_of(my_row ^ (step + half)))
        write_block(near_ref, *parts_of(my_row ^ step))
    for row, ref in ((my_row ^ half, far_ref), (my_row, own_ref)):
        ref[:rows_dev, :], ref[rows_dev:, :] = parts_of(row)


def write_block(ref, slab, early):
    rows_dev = slab.shape[0]
    ref[:rows_dev, :] = slab.astype(BF16)
    ref[rows_dev:, :] = high_and_low(early)


def add_blocks(own_ref, block_refs, rows_dev):
    slab, early = own_ref[:rows_dev, :], own_ref[rows_dev:, :]
    for ref in block_refs:
        slab = slab + ref[:rows_dev, :].astype(F32)
        early = early + sum_high_and_low(ref[rows_dev:, :])
    return slab, early


def mirror_kernel(rows_dev, own_ref, *refs):
    block_refs, out_ref = refs[:-1], refs[-1]
    write_block(out_ref, *add_blocks(own_ref, block_refs, rows_dev))


def shift_kernel(prev_ref, coupling_ref, shift_ref):
    shift_ref[...] = dot_nt(prev_ref[...], upper_of(coupling_ref[...]))


def grams_kernel(now_ref, shift_ref, own_ref, *refs):
    block_refs, (shifted_ref, grams_ref, early_ref) = refs[:-3], refs[-3:]
    rows_dev, width = now_ref.shape
    product, early_ref[...] = add_blocks(own_ref, block_refs, rows_dev)
    shifted = product - shift_ref[...]
    shifted_ref[...] = shifted
    if grams_ref.shape[0] > 2 * width:
        grams_ref[...] = jnp.zeros_like(grams_ref)
    grams_ref[:width, :] = dot_tn(now_ref[...], product)
    grams_ref[width : 2 * width, :] = dot_tn(shifted, shifted)


def spread_kernel(parts_ref, early_ref, out_ref):
    total = parts_ref[0]
    for part in range(1, parts_ref.shape[0]):
        total = total + parts_ref[part]
    value = jnp.concatenate([high_and_low(total), early_ref[...].astype(BF16)], axis=0)
    for part in range(out_ref.shape[0]):
        out_ref[part] = value


def split(x):
    high = x.astype(BF16)
    return high, (x - high.astype(F32)).astype(BF16)


def dot3(a, b, dims=((1,), (0,))):
    (a_high, a_low), (b_high, b_low) = split(a), split(b)

    def one(x, y):
        return lax.dot_general(x, y, (dims, ((), ())), preferred_element_type=F32)

    return one(a_high, b_low) + one(a_low, b_high) + one(a_high, b_high)


def eliminate(gram):
    width = gram.shape[0]
    block, per_group = 16, 2
    lanes = lax.broadcasted_iota(jnp.int32, (block, width), 1)
    subs = lax.broadcasted_iota(jnp.int32, (block, width), 0)

    def column(strip, k):
        return jnp.broadcast_to(strip[:, k : k + 1], (block, width))

    def row(strip, k):
        return jnp.broadcast_to(strip[k : k + 1, :], (block, width))

    strips = [gram[r : r + block, :] for r in range(0, width, block)]
    finished = []
    for begin in range(0, len(strips), per_group):
        group = strips[:per_group]
        for at in range(per_group):
            first = (begin + at) * block
            panel = group[at]
            columns = [column(panel, first + j) for j in range(block)]
            kept = panel
            for j in range(0, block, 2):
                here, there = subs == j, subs == j + 1
                lane, next_lane = lanes == first + j, lanes == first + j + 1
                left, right = columns[j], columns[j + 1]
                a, b, c = row(left, j), row(right, j), row(right, j + 1)
                scale = 1.0 / (a * c - b * b)
                top, bottom = row(panel, j), row(panel, j + 1)
                ratio = b / a
                kept = jnp.where(here, top, jnp.where(there, bottom - ratio * jnp.where(lane, 1.0, top), kept))
                kept = jnp.where(there & lane, -ratio, kept)
                top = jnp.where(lane, 1.0, jnp.where(next_lane, 0.0, top))
                bottom = jnp.where(lane, 0.0, jnp.where(next_lane, 1.0, bottom))
                unit_top = (c * top - b * bottom) * scale
                unit_bottom = (a * bottom - b * top) * scale
                others = jnp.where(lane | next_lane, 0.0, panel) - (left * unit_top + right * unit_bottom)
                panel = jnp.where(here, unit_top, jnp.where(there, unit_bottom, others))
                for m in range(j + 2, block):
                    up, down = row(columns[m], j), row(columns[m], j + 1)
                    up, down = (c * up - b * down) * scale, (a * down - b * up) * scale
                    others = columns[m] - (left * up + right * down)
                    columns[m] = jnp.where(here, up, jnp.where(there, down, others))
            finished.append(kept)
            group[at] = panel
            rows = [row(panel, m) for m in range(block)]
            inside = (lanes >= first) & (lanes < first + block)
            for s in range(per_group):
                if s != at:
                    terms = [column(group[s], first + m) * rows[m] for m in range(block)]
                    while len(terms) > 1:
                        terms = [x + y for x, y in zip(terms[::2], terms[1::2])]
                    group[s] = jnp.where(inside, 0.0, group[s]) - terms[0]
        strips = strips[per_group:]
        if strips:
            first, last = begin * block, (begin + per_group) * block
            below = jnp.concatenate(strips, axis=0)
            solved = [jnp.zeros((first, width), F32)] if first else []
            solved = jnp.concatenate(solved + group + [jnp.zeros((width - last, width), F32)], axis=0)
            cols = lax.broadcasted_iota(jnp.int32, below.shape, 1)
            below = jnp.where((cols >= first) & (cols < last), 0.0, below) - dot3(below, solved)
            strips = [below[r : r + block, :] for r in range(0, below.shape[0], block)]
    return jnp.concatenate(finished, axis=0)


def final_kernel(total_rows, pieces_ref, now_ref, shifted_ref, basis_ref, projection_ref, rfactor_ref):
    width = now_ref.shape[1]
    piece = pieces_ref.shape[1] // 3
    pieces = pieces_ref[...]
    late = sum_high_and_low(pieces[:, : 2 * piece, :]).reshape(-1, width)
    early = pieces[:, 2 * piece :, :].astype(F32).reshape(-1, width)
    now_product, square = late[:width], late[width : 2 * width]
    now_square, shift = early[:width], early[width : 2 * width]
    projection = now_product * total_rows**-0.5
    projection_ref[...] = projection
    scaled = now_product * (1.0 / total_rows)
    half = shift - 0.5 * now_product + 0.5 * dot3(now_square, scaled)
    mixed = dot3(scaled, half, ((0,), (0,)))
    gram = square + mixed + mixed.T
    reduced = eliminate(gram * (1.0 / total_rows))
    rows = lax.broadcasted_iota(jnp.int32, reduced.shape, 0)
    cols = lax.broadcasted_iota(jnp.int32, reduced.shape, 1)
    diagonal = jnp.sum(jnp.where(rows == cols, reduced, 0.0), axis=1, keepdims=True)
    root = lax.rsqrt(diagonal)
    rfactor_ref[...] = jnp.where(rows <= cols, reduced, 0.0) * root
    inverse = jnp.where(rows > cols, reduced, jnp.where(rows == cols, 1.0, 0.0)) * root
    residual = shifted_ref[...] - dot3(now_ref[...], scaled)
    basis_ref[...] = dot3(residual, inverse, ((1,), (1,)))


def exchange(blocks, axis, steps):
    n = lax.axis_size(axis)
    assert n & (n - 1) == 0
    return [lax.ppermute(block, axis, [(i, i ^ step) for i in range(n)]) for step, block in zip(steps, blocks)]


def on_device(basis_now, basis_prev, coupling, tiles, tile_rows, tile_cols, tile_counts):
    rows_dev, width = basis_now.shape
    n_row, n_col = lax.axis_size("row"), lax.axis_size("col")
    devices = n_row * n_col
    tile_block = tiles[0, 0]
    total_rows = float(rows_dev * devices)
    piece = -(-2 * width // (8 * devices)) * 8
    smem = pl.BlockSpec(memory_space=pltpu.SMEM)
    vmem = pl.BlockSpec(memory_space=pltpu.VMEM)
    hbm = pl.BlockSpec(memory_space=pltpu.HBM)
    params = pltpu.CompilerParams(vmem_limit_bytes=48 * 1024 * 1024)

    both = jnp.concatenate([basis_now, basis_prev], axis=0).astype(BF16)
    gathered = lax.all_gather(both, "col", axis=0, tiled=True)
    index_arrays = [pltpu.with_memory_space_constraint(x, pltpu.HBM) for x in (tile_rows, tile_cols)]
    slots = lax.broadcasted_iota(jnp.int32, (tile_rows.shape[-1], width), 0)
    used = (slots < tile_counts).astype(F32)
    me = jnp.stack([lax.axis_index("row"), lax.axis_index("col")])
    half = n_row // 2
    block = jax.ShapeDtypeStruct((rows_dev + 2 * piece, width), BF16)
    sums = jax.ShapeDtypeStruct((rows_dev + piece, width), F32)
    *blocks, far, own = pl.pallas_call(
        functools.partial(tiles_kernel, n_row, n_col, total_rows),
        out_shape=[block] * (2 * half - 2) + [sums] * 2,
        in_specs=[smem] + [hbm] * 2 + [vmem] * 4,
        out_specs=[vmem] * (2 * half),
        scratch_shapes=[
            pltpu.VMEM((n_row * rows_dev, width), F32),
            pltpu.VMEM((devices * piece, width), F32),
            pltpu.SMEM(tile_rows.shape, tile_rows.dtype),
            pltpu.SMEM(tile_cols.shape, tile_cols.dtype),
            pltpu.SemaphoreType.DMA((2,)),
        ],
        compiler_params=params,
        name="tile_products",
    )(me, *index_arrays, used, tile_block, gathered, coupling)
    steps = distances(half)[:-1]
    mirrors = exchange(blocks[: half - 1], "row", steps)
    near = blocks[half - 1 :]
    nearest = exchange(near[-1:], "row", steps[-1:])
    mirror = pl.pallas_call(
        functools.partial(mirror_kernel, rows_dev),
        out_shape=block,
        in_specs=[vmem] * half,
        out_specs=vmem,
        compiler_params=params,
        name="mirror_sum",
    )(far, *mirrors)
    mirror, *near = lax.optimization_barrier((mirror, *near[:-1]))
    across = exchange([mirror], "row", [half])
    near = exchange(near, "row", steps[:-1])

    shift = pl.pallas_call(
        shift_kernel,
        out_shape=jax.ShapeDtypeStruct((rows_dev, width), F32),
        in_specs=[vmem] * 2,
        out_specs=vmem,
        compiler_params=params,
        cost_estimate=pl.CostEstimate(flops=12 * rows_dev * width * width, bytes_accessed=12 * rows_dev * width, transcendentals=0),
        name="shift_by_previous",
    )(basis_prev, coupling)
    shifted, grams, early = pl.pallas_call(
        grams_kernel,
        out_shape=(
            jax.ShapeDtypeStruct((rows_dev, width), F32),
            jax.ShapeDtypeStruct((devices * piece, width), F32),
            jax.ShapeDtypeStruct((piece, width), F32),
        ),
        in_specs=[vmem] * (3 + half),
        out_specs=(vmem, vmem, vmem),
        compiler_params=params,
        name="local_grams",
    )(basis_now, shift, own, *nearest, *across, *near)
    everyone = ("row", "col")
    pieces = lax.all_to_all(grams.reshape(devices, piece, width), everyone, split_axis=0, concat_axis=0, tiled=True)
    copies = pl.pallas_call(
        spread_kernel,
        out_shape=jax.ShapeDtypeStruct((devices, 3 * piece, width), BF16),
        in_specs=[vmem, vmem],
        out_specs=vmem,
        compiler_params=params,
        name="sum_and_spread",
    )(pieces, early)
    gathered_sums = lax.all_to_all(copies, everyone, split_axis=0, concat_axis=0, tiled=True)
    return pl.pallas_call(
        functools.partial(final_kernel, total_rows),
        out_shape=(
            jax.ShapeDtypeStruct((rows_dev, width), F32),
            jax.ShapeDtypeStruct((width, width), F32),
            jax.ShapeDtypeStruct((width, width), F32),
        ),
        in_specs=[vmem] * 3,
        out_specs=(vmem, vmem, vmem),
        compiler_params=params,
        name="factor_and_basis",
    )(gathered_sums, basis_now, shifted)


def solution(mesh):
    placed = (
        P(("row", "col"), None),
        P(("row", "col"), None),
        P(),
        P("row", "col", None, None, None),
        P("row", "col", None),
        P("row", "col", None),
        P("row", "col"),
    )
    return jax.shard_map(
        on_device,
        mesh=mesh,
        in_specs=placed,
        out_specs=(P(("row", "col"), None), P(), P()),
        check_vma=False,
    )
```

```python
import functools

import jax
import jax.numpy as jnp
from jax import lax
from jax.experimental import pallas as pl
from jax.experimental.pallas import tpu as pltpu
from jax.sharding import PartitionSpec as P

F32 = jnp.float32
BF16 = jnp.bfloat16
NN, TN, NT = [(((x,), (y,)), ((), ())) for x, y in ((1, 0), (0, 0), (1, 1))]


def split(x):
    high = x.astype(BF16)
    return high, (x - high.astype(F32)).astype(BF16)


def dot3(a, b, dims=NN):
    (a_high, a_low), (b_high, b_low) = split(a), split(b)

    def one(x, y):
        return lax.dot_general(x, y, dims, preferred_element_type=F32)

    return one(a_high, b_low) + one(a_low, b_high) + one(a_high, b_high)


def upper_of(x):
    rows = lax.broadcasted_iota(jnp.int32, x.shape, 0)
    cols = lax.broadcasted_iota(jnp.int32, x.shape, 1)
    return jnp.where(rows <= cols, x, 0.0)


def distances(n):
    return range(n - 1, -1, -1)


def high_and_low(value):
    high = value.astype(BF16)
    low = (value - high.astype(F32)).astype(BF16)
    return jnp.concatenate([high, low], axis=0)


def sum_high_and_low(value):
    half = value.shape[-2] // 2
    value = value.astype(F32)
    return value[..., :half, :] + value[..., half:, :]


def tiles_kernel(n_row, n_col, total_rows, me_ref, rows_ref, cols_ref, count_ref, tiles_ref, basis_ref, coupling_ref, *refs):
    half = n_row // 2
    mirror_refs, near_refs, (far_ref, own_ref, total_ref, early_ref) = refs[: half - 1], refs[half - 1 : -4], refs[-4:]
    slots, size, _ = tiles_ref.shape
    width = total_ref.shape[1]
    rows_dev = total_ref.shape[0] // n_row
    piece = early_ref.shape[0] // (n_row * n_col)
    my_row, my_col = me_ref[0], me_ref[1]
    total_ref[...] = jnp.zeros_like(total_ref)
    grams = jnp.zeros((width, 2 * width), F32)
    for slab in range(n_col):
        now = basis_ref[2 * slab * rows_dev : (2 * slab + 1) * rows_dev, :]
        prev = basis_ref[(2 * slab + 1) * rows_dev : (2 * slab + 2) * rows_dev, :]
        grams += lax.dot_general(now, jnp.concatenate([now, prev], axis=1), TN, preferred_element_type=F32)
    square, cross = grams[:, :width], grams[:, width:]
    rows = lax.broadcasted_iota(jnp.int32, square.shape, 0)
    cols = lax.broadcasted_iota(jnp.int32, square.shape, 1)
    if early_ref.shape[0] > 2 * width:
        early_ref[...] = jnp.zeros_like(early_ref)
    early_ref[:width, :] = square - jnp.where(rows == cols, total_rows / n_row, 0.0)
    early_ref[width : 2 * width, :] = dot3(cross, upper_of(coupling_ref[...]), NT)
    used = count_ref[...]
    per_slab = rows_dev // size
    for slot in range(slots):
        col = cols_ref[0, 0, slot]
        start = pl.multiple_of((2 * per_slab * (col // per_slab) + lax.rem(col, per_slab)) * size, size)
        value = jnp.dot(tiles_ref[slot], basis_ref[pl.ds(start, size), :], preferred_element_type=F32)
        value = value * (slot < used).astype(F32)
        place = pl.ds(pl.multiple_of(rows_ref[0, 0, slot] * size, size), size)
        total_ref[place, :] += value

    def parts_of(row):
        slab = total_ref[pl.ds(pl.multiple_of(row * rows_dev, rows_dev), rows_dev), :]
        return slab, early_ref[pl.ds(pl.multiple_of((row * n_col + my_col) * piece, piece), piece), :]

    for step, mirror_ref, near_ref in zip(distances(half), mirror_refs, near_refs):
        write_block(mirror_ref, *parts_of(my_row ^ (step + half)))
        write_block(near_ref, *parts_of(my_row ^ step))
    for row, ref in ((my_row ^ half, far_ref), (my_row, own_ref)):
        ref[:rows_dev, :], ref[rows_dev:, :] = parts_of(row)


def write_block(ref, slab, early):
    rows_dev = slab.shape[0]
    ref[:rows_dev, :] = slab.astype(BF16)
    ref[rows_dev:, :] = high_and_low(early)


def add_blocks(own_ref, block_refs, rows_dev):
    slab, early = own_ref[:rows_dev, :], own_ref[rows_dev:, :]
    for ref in block_refs:
        slab = slab + ref[:rows_dev, :].astype(F32)
        early = early + sum_high_and_low(ref[rows_dev:, :])
    return slab, early


def mirror_kernel(rows_dev, own_ref, *refs):
    block_refs, out_ref = refs[:-1], refs[-1]
    write_block(out_ref, *add_blocks(own_ref, block_refs, rows_dev))


def shift_kernel(prev_ref, coupling_ref, shift_ref):
    shift_ref[...] = dot3(prev_ref[...], upper_of(coupling_ref[...]), NT)


def grams_kernel(now_ref, shift_ref, own_ref, *refs):
    block_refs, (shifted_ref, grams_ref, early_ref) = refs[:-3], refs[-3:]
    rows_dev, width = now_ref.shape
    product, early_ref[...] = add_blocks(own_ref, block_refs, rows_dev)
    shifted = product - shift_ref[...]
    shifted_ref[...] = shifted
    if grams_ref.shape[0] > 2 * width:
        grams_ref[...] = jnp.zeros_like(grams_ref)
    grams_ref[:width, :] = dot3(now_ref[...], product, TN)
    grams_ref[width : 2 * width, :] = dot3(shifted, shifted, TN)


def spread_kernel(parts_ref, early_ref, out_ref):
    total = parts_ref[0]
    for part in range(1, parts_ref.shape[0]):
        total = total + parts_ref[part]
    value = jnp.concatenate([high_and_low(total), early_ref[...].astype(BF16)], axis=0)
    for part in range(out_ref.shape[0]):
        out_ref[part] = value


def eliminate(gram):
    width = gram.shape[0]
    block, per_group = 16, 2
    lanes = lax.broadcasted_iota(jnp.int32, (block, width), 1)
    subs = lax.broadcasted_iota(jnp.int32, (block, width), 0)

    def column(strip, k):
        return jnp.broadcast_to(strip[:, k : k + 1], (block, width))

    def row(strip, k):
        return jnp.broadcast_to(strip[k : k + 1, :], (block, width))

    strips = [gram[r : r + block, :] for r in range(0, width, block)]
    finished = []
    for begin in range(0, len(strips), per_group):
        group = strips[:per_group]
        for at in range(per_group):
            first = (begin + at) * block
            panel = group[at]
            columns = [column(panel, first + j) for j in range(block)]
            kept = panel
            for j in range(0, block, 2):
                here, there = subs == j, subs == j + 1
                both = here | there
                lane, next_lane = lanes == first + j, lanes == first + j + 1
                left, right = columns[j], columns[j + 1]
                a, b, c = row(left, j), row(right, j), row(right, j + 1)
                scale = 1.0 / (a * c - b * b)
                by_top = jnp.where(here, -c, jnp.where(there, b, left * c - right * b))
                by_bottom = jnp.where(here, b, jnp.where(there, -a, right * a - left * b))
                top, bottom = row(panel, j), row(panel, j + 1)
                ratio = b / a
                kept = jnp.where(here, top, jnp.where(there, bottom - ratio * jnp.where(lane, 1.0, top), kept))
                kept = jnp.where(there & lane, -ratio, kept)
                top = jnp.where(lane, 1.0, jnp.where(next_lane, 0.0, top))
                bottom = jnp.where(lane, 0.0, jnp.where(next_lane, 1.0, bottom))
                panel = jnp.where(both | lane | next_lane, 0.0, panel) - (by_top * top + by_bottom * bottom) * scale
                for m in range(j + 2, block):
                    up, down = row(columns[m], j), row(columns[m], j + 1)
                    columns[m] = jnp.where(both, 0.0, columns[m]) - (by_top * up + by_bottom * down) * scale
            finished.append(kept)
            group[at] = panel
            rows = [row(panel, m) for m in range(block)]
            inside = (lanes >= first) & (lanes < first + block)
            for s in range(per_group):
                if s != at:
                    terms = [column(group[s], first + m) * rows[m] for m in range(block)]
                    while len(terms) > 1:
                        terms = [x + y for x, y in zip(terms[::2], terms[1::2])]
                    group[s] = jnp.where(inside, 0.0, group[s]) - terms[0]
        strips = strips[per_group:]
        if strips:
            first, last = begin * block, (begin + per_group) * block
            below = jnp.concatenate(strips, axis=0)
            solved = [jnp.zeros((first, width), F32)] if first else []
            solved = jnp.concatenate(solved + group + [jnp.zeros((width - last, width), F32)], axis=0)
            cols = lax.broadcasted_iota(jnp.int32, below.shape, 1)
            below = jnp.where((cols >= first) & (cols < last), 0.0, below) - dot3(below, solved)
            strips = [below[r : r + block, :] for r in range(0, below.shape[0], block)]
    return jnp.concatenate(finished, axis=0)


def final_kernel(total_rows, pieces_ref, now_ref, shifted_ref, basis_ref, projection_ref, rfactor_ref):
    width = now_ref.shape[1]
    piece = pieces_ref.shape[1] // 3
    pieces = pieces_ref[...]
    late = sum_high_and_low(pieces[:, : 2 * piece, :]).reshape(-1, width)
    early = pieces[:, 2 * piece :, :].astype(F32).reshape(-1, width)
    now_product, square = late[:width], late[width : 2 * width]
    now_square, shift = early[:width], early[width : 2 * width]
    projection = now_product * total_rows**-0.5
    projection_ref[...] = projection
    scaled = now_product * (1.0 / total_rows)
    half = shift - 0.5 * now_product + 0.5 * dot3(now_square, scaled)
    mixed = dot3(scaled, half, TN)
    gram = square + mixed + mixed.T
    reduced = eliminate(gram * (1.0 / total_rows))
    rows = lax.broadcasted_iota(jnp.int32, reduced.shape, 0)
    cols = lax.broadcasted_iota(jnp.int32, reduced.shape, 1)
    diagonal = jnp.sum(jnp.where(rows == cols, reduced, 0.0), axis=1, keepdims=True)
    root = lax.rsqrt(diagonal)
    rfactor_ref[...] = jnp.where(rows <= cols, reduced, 0.0) * root
    inverse = jnp.where(rows > cols, reduced, jnp.where(rows == cols, 1.0, 0.0)) * root
    residual = shifted_ref[...] - dot3(now_ref[...], scaled)
    basis_ref[...] = dot3(residual, inverse, NT)


def exchange(blocks, axis, steps):
    n = lax.axis_size(axis)
    assert n & (n - 1) == 0
    return [lax.ppermute(block, axis, [(i, i ^ step) for i in range(n)]) for step, block in zip(steps, blocks)]


def on_device(basis_now, basis_prev, coupling, tiles, tile_rows, tile_cols, tile_counts):
    rows_dev, width = basis_now.shape
    n_row, n_col = lax.axis_size("row"), lax.axis_size("col")
    devices = n_row * n_col
    tile_block = tiles[0, 0]
    total_rows = float(rows_dev * devices)
    piece = -(-2 * width // (8 * devices)) * 8
    smem = pl.BlockSpec(memory_space=pltpu.SMEM)
    vmem = pl.BlockSpec(memory_space=pltpu.VMEM)
    params = pltpu.CompilerParams(vmem_limit_bytes=48 * 1024 * 1024)

    both = jnp.concatenate([basis_now, basis_prev], axis=0).astype(BF16)
    gathered = lax.all_gather(both, "col", axis=0, tiled=True)
    me = jnp.stack([lax.axis_index("row"), lax.axis_index("col")])
    half = n_row // 2
    block = jax.ShapeDtypeStruct((rows_dev + 2 * piece, width), BF16)
    sums = jax.ShapeDtypeStruct((rows_dev + piece, width), F32)
    *blocks, far, own = pl.pallas_call(
        functools.partial(tiles_kernel, n_row, n_col, total_rows),
        out_shape=[block] * (2 * half - 2) + [sums] * 2,
        in_specs=[smem] * 3 + [vmem] * 4,
        out_specs=[vmem] * (2 * half),
        scratch_shapes=[
            pltpu.VMEM((n_row * rows_dev, width), F32),
            pltpu.VMEM((devices * piece, width), F32),
        ],
        compiler_params=params,
        name="tile_products",
    )(me, tile_rows, tile_cols, tile_counts, tile_block, gathered, coupling)
    steps = distances(half)[:-1]
    mirrors = exchange(blocks[: half - 1], "row", steps)
    near = exchange(blocks[half - 1 :], "row", steps)
    mirror = pl.pallas_call(
        functools.partial(mirror_kernel, rows_dev),
        out_shape=block,
        in_specs=[vmem] * half,
        out_specs=vmem,
        compiler_params=params,
        name="mirror_sum",
    )(far, *mirrors)
    across = exchange([mirror], "row", [half])

    shift = pl.pallas_call(
        shift_kernel,
        out_shape=jax.ShapeDtypeStruct((rows_dev, width), F32),
        in_specs=[vmem] * 2,
        out_specs=vmem,
        compiler_params=params,
        cost_estimate=pl.CostEstimate(flops=12 * rows_dev * width * width, bytes_accessed=12 * rows_dev * width, transcendentals=0),
        name="shift_by_previous",
    )(basis_prev, coupling)
    shifted, grams, early = pl.pallas_call(
        grams_kernel,
        out_shape=(
            jax.ShapeDtypeStruct((rows_dev, width), F32),
            jax.ShapeDtypeStruct((devices * piece, width), F32),
            jax.ShapeDtypeStruct((piece, width), F32),
        ),
        in_specs=[vmem] * (3 + half),
        out_specs=(vmem, vmem, vmem),
        compiler_params=params,
        name="local_grams",
    )(basis_now, shift, own, *near, *across)
    everyone = ("row", "col")
    pieces = lax.all_to_all(grams.reshape(devices, piece, width), everyone, split_axis=0, concat_axis=0, tiled=True)
    copies = pl.pallas_call(
        spread_kernel,
        out_shape=jax.ShapeDtypeStruct((devices, 3 * piece, width), BF16),
        in_specs=[vmem, vmem],
        out_specs=vmem,
        compiler_params=params,
        name="sum_and_spread",
    )(pieces, early)
    gathered_sums = lax.all_to_all(copies, everyone, split_axis=0, concat_axis=0, tiled=True)
    return pl.pallas_call(
        functools.partial(final_kernel, total_rows),
        out_shape=(
            jax.ShapeDtypeStruct((rows_dev, width), F32),
            jax.ShapeDtypeStruct((width, width), F32),
            jax.ShapeDtypeStruct((width, width), F32),
        ),
        in_specs=[vmem] * 3,
        out_specs=(vmem, vmem, vmem),
        compiler_params=params,
        name="factor_and_basis",
    )(gathered_sums, basis_now, shifted)


def solution(mesh):
    placed = (
        P(("row", "col"), None),
        P(("row", "col"), None),
        P(),
        P("row", "col", None, None, None),
        P("row", "col", None),
        P("row", "col", None),
        P("row", "col"),
    )
    return jax.shard_map(
        on_device,
        mesh=mesh,
        in_specs=placed,
        out_specs=(P(("row", "col"), None), P(), P()),
        check_vma=False,
    )
```

```python
import functools

import jax
import jax.numpy as jnp
from jax import lax
from jax.experimental import pallas as pl
from jax.experimental.pallas import tpu as pltpu
from jax.sharding import PartitionSpec as P

F32 = jnp.float32
BF16 = jnp.bfloat16
NN, TN, NT = [(((x,), (y,)), ((), ())) for x, y in ((1, 0), (0, 0), (1, 1))]


def split(x):
    high = x.astype(BF16)
    return high, (x - high.astype(F32)).astype(BF16)


def dot3(a, b, dims=NN):
    (a_high, a_low), (b_high, b_low) = split(a), split(b)

    def one(x, y):
        return lax.dot_general(x, y, dims, preferred_element_type=F32)

    return one(a_high, b_low) + one(a_low, b_high) + one(a_high, b_high)


def upper_of(x):
    rows = lax.broadcasted_iota(jnp.int32, x.shape, 0)
    cols = lax.broadcasted_iota(jnp.int32, x.shape, 1)
    return jnp.where(rows <= cols, x, 0.0)


def distances(n):
    return range(n - 1, -1, -1)


def high_and_low(value):
    high = value.astype(BF16)
    low = (value - high.astype(F32)).astype(BF16)
    return jnp.concatenate([high, low], axis=0)


def sum_high_and_low(value):
    half = value.shape[-2] // 2
    value = value.astype(F32)
    return value[..., :half, :] + value[..., half:, :]


def tiles_kernel(n_row, n_col, total_rows, me_ref, rows_ref, cols_ref, count_ref, tiles_ref, basis_ref, coupling_ref, *refs):
    half = n_row // 2
    mirror_refs, near_refs, (far_ref, own_ref, total_ref, early_ref) = refs[: half - 1], refs[half - 1 : -4], refs[-4:]
    slots, size, _ = tiles_ref.shape
    width = total_ref.shape[1]
    rows_dev = total_ref.shape[0] // n_row
    piece = early_ref.shape[0] // (n_row * n_col)
    my_row, my_col = me_ref[0], me_ref[1]
    total_ref[...] = jnp.zeros_like(total_ref)
    grams = jnp.zeros((width, 2 * width), F32)
    for slab in range(n_col):
        now = basis_ref[2 * slab * rows_dev : (2 * slab + 1) * rows_dev, :]
        prev = basis_ref[(2 * slab + 1) * rows_dev : (2 * slab + 2) * rows_dev, :]
        grams += lax.dot_general(now, jnp.concatenate([now, prev], axis=1), TN, preferred_element_type=F32)
    square, cross = grams[:, :width], grams[:, width:]
    rows = lax.broadcasted_iota(jnp.int32, square.shape, 0)
    cols = lax.broadcasted_iota(jnp.int32, square.shape, 1)
    if early_ref.shape[0] > 2 * width:
        early_ref[...] = jnp.zeros_like(early_ref)
    early_ref[:width, :] = square - jnp.where(rows == cols, total_rows / n_row, 0.0)
    early_ref[width : 2 * width, :] = dot3(cross, upper_of(coupling_ref[...]), NT)
    used = count_ref[...]
    per_slab = rows_dev // size
    for slot in range(slots):
        col = cols_ref[0, 0, slot]
        start = pl.multiple_of((2 * per_slab * (col // per_slab) + lax.rem(col, per_slab)) * size, size)
        value = jnp.dot(tiles_ref[slot], basis_ref[pl.ds(start, size), :], preferred_element_type=F32)
        value = value * (slot < used).astype(F32)
        place = pl.ds(pl.multiple_of(rows_ref[0, 0, slot] * size, size), size)
        total_ref[place, :] += value

    def parts_of(row):
        slab = total_ref[pl.ds(pl.multiple_of(row * rows_dev, rows_dev), rows_dev), :]
        return slab, early_ref[pl.ds(pl.multiple_of((row * n_col + my_col) * piece, piece), piece), :]

    for step, mirror_ref, near_ref in zip(distances(half), mirror_refs, near_refs):
        write_block(mirror_ref, *parts_of(my_row ^ (step + half)))
        write_block(near_ref, *parts_of(my_row ^ step))
    for row, ref in ((my_row ^ half, far_ref), (my_row, own_ref)):
        ref[:rows_dev, :], ref[rows_dev:, :] = parts_of(row)


def write_block(ref, slab, early):
    rows_dev = slab.shape[0]
    ref[:rows_dev, :] = slab.astype(BF16)
    ref[rows_dev:, :] = early.astype(BF16)


def add_blocks(own_ref, block_refs, rows_dev):
    slab, early = own_ref[:rows_dev, :], own_ref[rows_dev:, :]
    for ref in block_refs:
        slab = slab + ref[:rows_dev, :].astype(F32)
        early = early + ref[rows_dev:, :].astype(F32)
    return slab, early


def mirror_kernel(rows_dev, own_ref, *refs):
    block_refs, out_ref = refs[:-1], refs[-1]
    write_block(out_ref, *add_blocks(own_ref, block_refs, rows_dev))


def shift_kernel(prev_ref, coupling_ref, shift_ref):
    shift_ref[...] = dot3(prev_ref[...], upper_of(coupling_ref[...]), NT)


def grams_kernel(now_ref, shift_ref, own_ref, *refs):
    block_refs, (shifted_ref, grams_ref, early_ref) = refs[:-3], refs[-3:]
    rows_dev, width = now_ref.shape
    product, early_ref[...] = add_blocks(own_ref, block_refs, rows_dev)
    shifted = product - shift_ref[...]
    shifted_ref[...] = shifted
    if grams_ref.shape[0] > 2 * width:
        grams_ref[...] = jnp.zeros_like(grams_ref)
    grams_ref[:width, :] = dot3(now_ref[...], product, TN)
    grams_ref[width : 2 * width, :] = dot3(shifted, shifted, TN)


def spread_kernel(parts_ref, early_ref, out_ref):
    total = parts_ref[0]
    for part in range(1, parts_ref.shape[0]):
        total = total + parts_ref[part]
    value = jnp.concatenate([high_and_low(total), early_ref[...].astype(BF16)], axis=0)
    for part in range(out_ref.shape[0]):
        out_ref[part] = value


def eliminate(gram):
    width = gram.shape[0]
    block, per_group = 16, 2
    lanes = lax.broadcasted_iota(jnp.int32, (block, width), 1)
    subs = lax.broadcasted_iota(jnp.int32, (block, width), 0)

    def column(strip, k):
        return jnp.broadcast_to(strip[:, k : k + 1], (block, width))

    def row(strip, k):
        return jnp.broadcast_to(strip[k : k + 1, :], (block, width))

    strips = [gram[r : r + block, :] for r in range(0, width, block)]
    finished = []
    for begin in range(0, len(strips), per_group):
        group = strips[:per_group]
        for at in range(per_group):
            first = (begin + at) * block
            panel = group[at]
            columns = [column(panel, first + j) for j in range(block)]
            kept = panel
            for j in range(0, block, 4):
                here = [subs == j + k for k in range(4)]
                lane = [lanes == first + j + k for k in range(4)]
                mine = (subs >= j) & (subs < j + 4)
                old = columns[j : j + 4]
                g = {(x, y): row(old[y], j + x) for x in range(4) for y in range(x, 4)}
                scale = 1.0 / (g[0, 0] * g[1, 1] - g[0, 1] * g[0, 1])
                a00, a01, a11 = g[1, 1] * scale, -g[0, 1] * scale, g[0, 0] * scale
                t = {(0, y): a00 * g[0, y] + a01 * g[1, y] for y in (2, 3)}
                t.update({(1, y): a01 * g[0, y] + a11 * g[1, y] for y in (2, 3)})
                s22, s23, s33 = [
                    g[x, y] - (g[0, x] * t[0, y] + g[1, x] * t[1, y]) for x, y in ((2, 2), (2, 3), (3, 3))
                ]
                scale = 1.0 / (s22 * s33 - s23 * s23)
                inverse = {(2, 2): s33 * scale, (2, 3): -s23 * scale, (3, 3): s22 * scale}
                for x in (0, 1):
                    inverse[x, 2] = -(t[x, 2] * inverse[2, 2] + t[x, 3] * inverse[2, 3])
                    inverse[x, 3] = -(t[x, 2] * inverse[2, 3] + t[x, 3] * inverse[3, 3])
                for x, y, start in ((0, 0, a00), (0, 1, a01), (1, 1, a11)):
                    inverse[x, y] = start - (t[x, 2] * inverse[y, 2] + t[x, 3] * inverse[y, 3])
                inverse.update({(y, x): value for (x, y), value in list(inverse.items())})
                by = []
                for y in range(4):
                    terms = [old[x] * inverse[x, y] for x in range(4)]
                    value = (terms[0] + terms[1]) + (terms[2] + terms[3])
                    for x in range(4):
                        value = jnp.where(here[x], -inverse[x, y], value)
                    by.append(value)

                def update(x, rows):
                    return jnp.where(mine, 0.0, x) - ((by[0] * rows[0] + by[1] * rows[1]) + (by[2] * rows[2] + by[3] * rows[3]))

                plain = [row(panel, j + k) for k in range(4)]
                in_pivots = (lanes >= first + j) & (lanes < first + j + 4)
                unit = [jnp.where(lane[k], 1.0, jnp.where(in_pivots, 0.0, plain[k])) for k in range(4)]
                done_0 = plain[0]
                done_1 = jnp.where(lane[0], 0.0, plain[1]) - (g[0, 1] / g[0, 0]) * jnp.where(lane[0], 1.0, plain[0])
                first_two = lane[0] | lane[1]
                top = jnp.where(lane[0], 1.0, jnp.where(lane[1], 0.0, plain[0]))
                bottom = jnp.where(lane[0], 0.0, jnp.where(lane[1], 1.0, plain[1]))
                done_2, done_3 = [
                    jnp.where(first_two, 0.0, plain[y]) - (t[0, y] * top + t[1, y] * bottom) for y in (2, 3)
                ]
                done_3 = jnp.where(lane[2], 0.0, done_3) - (s23 / s22) * jnp.where(lane[2], 1.0, done_2)
                for k, done in enumerate((done_0, done_1, done_2, done_3)):
                    kept = jnp.where(here[k], done, kept)
                panel = update(jnp.where(in_pivots, 0.0, panel), unit)
                for m in range(j + 4, block):
                    columns[m] = update(columns[m], [row(columns[m], j + k) for k in range(4)])
            finished.append(kept)
            group[at] = panel
            rows = [row(panel, m) for m in range(block)]
            inside = (lanes >= first) & (lanes < first + block)
            for s in range(per_group):
                if s != at:
                    terms = [column(group[s], first + m) * rows[m] for m in range(block)]
                    while len(terms) > 1:
                        terms = [x + y for x, y in zip(terms[::2], terms[1::2])]
                    group[s] = jnp.where(inside, 0.0, group[s]) - terms[0]
        strips = strips[per_group:]
        if strips:
            first, last = begin * block, (begin + per_group) * block
            below = jnp.concatenate(strips, axis=0)
            solved = [jnp.zeros((first, width), F32)] if first else []
            solved = jnp.concatenate(solved + group + [jnp.zeros((width - last, width), F32)], axis=0)
            cols = lax.broadcasted_iota(jnp.int32, below.shape, 1)
            below = jnp.where((cols >= first) & (cols < last), 0.0, below) - dot3(below, solved)
            strips = [below[r : r + block, :] for r in range(0, below.shape[0], block)]
    return jnp.concatenate(finished, axis=0)


def final_kernel(total_rows, pieces_ref, now_ref, shifted_ref, basis_ref, projection_ref, rfactor_ref):
    width = now_ref.shape[1]
    piece = pieces_ref.shape[1] // 3
    pieces = pieces_ref[...]
    late = sum_high_and_low(pieces[:, : 2 * piece, :]).reshape(-1, width)
    early = pieces[:, 2 * piece :, :].astype(F32).reshape(-1, width)
    now_product, square = late[:width], late[width : 2 * width]
    now_square, shift = early[:width], early[width : 2 * width]
    projection = now_product * total_rows**-0.5
    projection_ref[...] = projection
    scaled = now_product * (1.0 / total_rows)
    half = shift - 0.5 * now_product + 0.5 * dot3(now_square, scaled)
    mixed = dot3(scaled, half, TN)
    gram = square + mixed + mixed.T
    reduced = eliminate(gram * (1.0 / total_rows))
    rows = lax.broadcasted_iota(jnp.int32, reduced.shape, 0)
    cols = lax.broadcasted_iota(jnp.int32, reduced.shape, 1)
    diagonal = jnp.sum(jnp.where(rows == cols, reduced, 0.0), axis=1, keepdims=True)
    root = lax.rsqrt(diagonal)
    rfactor_ref[...] = jnp.where(rows <= cols, reduced, 0.0) * root
    inverse = jnp.where(rows > cols, reduced, jnp.where(rows == cols, 1.0, 0.0)) * root
    residual = shifted_ref[...] - dot3(now_ref[...], scaled)
    basis_ref[...] = dot3(residual, inverse, NT)


def exchange(blocks, axis, steps):
    n = lax.axis_size(axis)
    assert n & (n - 1) == 0
    return [lax.ppermute(block, axis, [(i, i ^ step) for i in range(n)]) for step, block in zip(steps, blocks)]


def on_device(basis_now, basis_prev, coupling, tiles, tile_rows, tile_cols, tile_counts):
    rows_dev, width = basis_now.shape
    n_row, n_col = lax.axis_size("row"), lax.axis_size("col")
    devices = n_row * n_col
    tile_block = tiles[0, 0]
    total_rows = float(rows_dev * devices)
    piece = -(-2 * width // (8 * devices)) * 8
    smem = pl.BlockSpec(memory_space=pltpu.SMEM)
    vmem = pl.BlockSpec(memory_space=pltpu.VMEM)
    params = pltpu.CompilerParams(vmem_limit_bytes=48 * 1024 * 1024)

    both = jnp.concatenate([basis_now, basis_prev], axis=0).astype(BF16)
    gathered = lax.all_gather(both, "col", axis=0, tiled=True)
    me = jnp.stack([lax.axis_index("row"), lax.axis_index("col")])
    half = n_row // 2
    block = jax.ShapeDtypeStruct((rows_dev + piece, width), BF16)
    sums = jax.ShapeDtypeStruct((rows_dev + piece, width), F32)
    *blocks, far, own = pl.pallas_call(
        functools.partial(tiles_kernel, n_row, n_col, total_rows),
        out_shape=[block] * (2 * half - 2) + [sums] * 2,
        in_specs=[smem] * 3 + [vmem] * 4,
        out_specs=[vmem] * (2 * half),
        scratch_shapes=[
            pltpu.VMEM((n_row * rows_dev, width), F32),
            pltpu.VMEM((devices * piece, width), F32),
        ],
        compiler_params=params,
        name="tile_products",
    )(me, tile_rows, tile_cols, tile_counts, tile_block, gathered, coupling)
    steps = distances(half)[:-1]
    mirrors = exchange(blocks[: half - 1], "row", steps)
    near = exchange(blocks[half - 1 :], "row", steps)
    mirror = pl.pallas_call(
        functools.partial(mirror_kernel, rows_dev),
        out_shape=block,
        in_specs=[vmem] * half,
        out_specs=vmem,
        compiler_params=params,
        name="mirror_sum",
    )(far, *mirrors)
    across = exchange([mirror], "row", [half])

    shift = pl.pallas_call(
        shift_kernel,
        out_shape=jax.ShapeDtypeStruct((rows_dev, width), F32),
        in_specs=[vmem] * 2,
        out_specs=vmem,
        compiler_params=params,
        cost_estimate=pl.CostEstimate(flops=12 * rows_dev * width * width, bytes_accessed=12 * rows_dev * width, transcendentals=0),
        name="shift_by_previous",
    )(basis_prev, coupling)
    shifted, grams, early = pl.pallas_call(
        grams_kernel,
        out_shape=(
            jax.ShapeDtypeStruct((rows_dev, width), F32),
            jax.ShapeDtypeStruct((devices * piece, width), F32),
            jax.ShapeDtypeStruct((piece, width), F32),
        ),
        in_specs=[vmem] * (3 + half),
        out_specs=(vmem, vmem, vmem),
        compiler_params=params,
        name="local_grams",
    )(basis_now, shift, own, *near, *across)
    everyone = ("row", "col")
    pieces = lax.all_to_all(grams.reshape(devices, piece, width), everyone, split_axis=0, concat_axis=0, tiled=True)
    copies = pl.pallas_call(
        spread_kernel,
        out_shape=jax.ShapeDtypeStruct((devices, 3 * piece, width), BF16),
        in_specs=[vmem, vmem],
        out_specs=vmem,
        compiler_params=params,
        name="sum_and_spread",
    )(pieces, early)
    gathered_sums = lax.all_to_all(copies, everyone, split_axis=0, concat_axis=0, tiled=True)
    return pl.pallas_call(
        functools.partial(final_kernel, total_rows),
        out_shape=(
            jax.ShapeDtypeStruct((rows_dev, width), F32),
            jax.ShapeDtypeStruct((width, width), F32),
            jax.ShapeDtypeStruct((width, width), F32),
        ),
        in_specs=[vmem] * 3,
        out_specs=(vmem, vmem, vmem),
        compiler_params=params,
        name="factor_and_basis",
    )(gathered_sums, basis_now, shifted)


def solution(mesh):
    placed = (
        P(("row", "col"), None),
        P(("row", "col"), None),
        P(),
        P("row", "col", None, None, None),
        P("row", "col", None),
        P("row", "col", None),
        P("row", "col"),
    )
    return jax.shard_map(
        on_device,
        mesh=mesh,
        in_specs=placed,
        out_specs=(P(("row", "col"), None), P(), P()),
        check_vma=False,
    )
```

```python
import functools

import jax
import jax.numpy as jnp
from jax import lax
from jax.experimental import pallas as pl
from jax.experimental.pallas import tpu as pltpu
from jax.sharding import PartitionSpec as P

F32 = jnp.float32
BF16 = jnp.bfloat16
NN, TN, NT = [(((x,), (y,)), ((), ())) for x, y in ((1, 0), (0, 0), (1, 1))]


def split(x):
    high = x.astype(BF16)
    return high, (x - high.astype(F32)).astype(BF16)


def dot3(a, b, dims=NN):
    (a_high, a_low), (b_high, b_low) = split(a), split(b)

    def one(x, y):
        return lax.dot_general(x, y, dims, preferred_element_type=F32)

    return one(a_high, b_low) + one(a_low, b_high) + one(a_high, b_high)


def upper_of(x):
    rows = lax.broadcasted_iota(jnp.int32, x.shape, 0)
    cols = lax.broadcasted_iota(jnp.int32, x.shape, 1)
    return jnp.where(rows <= cols, x, 0.0)


def distances(n):
    return range(n - 1, -1, -1)


def high_and_low(value):
    high = value.astype(BF16)
    low = (value - high.astype(F32)).astype(BF16)
    return jnp.concatenate([high, low], axis=0)


def sum_high_and_low(value):
    half = value.shape[-2] // 2
    value = value.astype(F32)
    return value[..., :half, :] + value[..., half:, :]


def tiles_kernel(n_row, n_col, total_rows, me_ref, rows_ref, cols_ref, count_ref, tiles_ref, basis_ref, coupling_ref, *refs):
    half = n_row // 2
    mirror_refs, near_refs, (far_ref, own_ref, total_ref, early_ref) = refs[: half - 1], refs[half - 1 : -4], refs[-4:]
    slots, size, _ = tiles_ref.shape
    width = total_ref.shape[1]
    rows_dev = total_ref.shape[0] // n_row
    piece = early_ref.shape[0] // (n_row * n_col)
    my_row, my_col = me_ref[0], me_ref[1]
    total_ref[...] = jnp.zeros_like(total_ref)
    grams = lax.dot_general(basis_ref[:, :width], basis_ref[...], TN, preferred_element_type=F32)
    square, cross = grams[:, :width], grams[:, width:]
    rows = lax.broadcasted_iota(jnp.int32, square.shape, 0)
    cols = lax.broadcasted_iota(jnp.int32, square.shape, 1)
    if early_ref.shape[0] > 2 * width:
        early_ref[...] = jnp.zeros_like(early_ref)
    early_ref[:width, :] = square - jnp.where(rows == cols, total_rows / n_row, 0.0)
    early_ref[width : 2 * width, :] = dot3(cross, upper_of(coupling_ref[...]), NT)
    used = count_ref[...]
    for slot in range(slots):
        start = pl.multiple_of(cols_ref[0, 0, slot] * size, size)
        value = jnp.dot(tiles_ref[slot], basis_ref[pl.ds(start, size), :width], preferred_element_type=F32)
        value = value * (slot < used).astype(F32)
        place = pl.ds(pl.multiple_of(rows_ref[0, 0, slot] * size, size), size)
        total_ref[place, :] += value

    def parts_of(row):
        slab = total_ref[pl.ds(pl.multiple_of(row * rows_dev, rows_dev), rows_dev), :]
        return slab, early_ref[pl.ds(pl.multiple_of((row * n_col + my_col) * piece, piece), piece), :]

    for step, mirror_ref, near_ref in zip(distances(half), mirror_refs, near_refs):
        write_block(mirror_ref, *parts_of(my_row ^ (step + half)))
        write_block(near_ref, *parts_of(my_row ^ step))
    for row, ref in ((my_row ^ half, far_ref), (my_row, own_ref)):
        ref[:rows_dev, :], ref[rows_dev:, :] = parts_of(row)


def write_block(ref, slab, early):
    rows_dev = slab.shape[0]
    ref[:rows_dev, :] = slab.astype(BF16)
    ref[rows_dev:, :] = high_and_low(early)


def add_blocks(own_ref, block_refs, rows_dev):
    slab, early = own_ref[:rows_dev, :], own_ref[rows_dev:, :]
    for ref in block_refs:
        slab = slab + ref[:rows_dev, :].astype(F32)
        early = early + sum_high_and_low(ref[rows_dev:, :])
    return slab, early


def mirror_kernel(rows_dev, own_ref, *refs):
    block_refs, out_ref = refs[:-1], refs[-1]
    write_block(out_ref, *add_blocks(own_ref, block_refs, rows_dev))


def shift_kernel(prev_ref, coupling_ref, shift_ref):
    shift_ref[...] = dot3(prev_ref[...], upper_of(coupling_ref[...]), NT)


def grams_kernel(now_ref, shift_ref, own_ref, *refs):
    block_refs, (shifted_ref, grams_ref, early_ref) = refs[:-3], refs[-3:]
    rows_dev, width = now_ref.shape
    product, early_ref[...] = add_blocks(own_ref, block_refs, rows_dev)
    shifted = product - shift_ref[...]
    shifted_ref[...] = shifted
    if grams_ref.shape[0] > 2 * width:
        grams_ref[...] = jnp.zeros_like(grams_ref)
    grams_ref[:width, :] = dot3(now_ref[...], product, TN)
    grams_ref[width : 2 * width, :] = dot3(shifted, shifted, TN)


def spread_kernel(parts_ref, early_ref, out_ref):
    total = parts_ref[0]
    for part in range(1, parts_ref.shape[0]):
        total = total + parts_ref[part]
    value = jnp.concatenate([high_and_low(total), early_ref[...].astype(BF16)], axis=0)
    for part in range(out_ref.shape[0]):
        out_ref[part] = value


def eliminate(gram):
    width = gram.shape[0]
    block, per_group = 8, 4
    lanes = lax.broadcasted_iota(jnp.int32, (block, width), 1)
    subs = lax.broadcasted_iota(jnp.int32, (block, width), 0)

    def column(strip, k):
        return jnp.broadcast_to(strip[:, k : k + 1], (block, width))

    def row(strip, k):
        return jnp.broadcast_to(strip[k : k + 1, :], (block, width))

    strips = [gram[r : r + block, :] for r in range(0, width, block)]
    finished = []
    for begin in range(0, len(strips), per_group):
        group = strips[:per_group]
        for at in range(per_group):
            first = (begin + at) * block
            panel = group[at]
            columns = [column(panel, first + j) for j in range(block)]
            kept = panel
            for j in range(0, block, 2):
                here, there = subs == j, subs == j + 1
                both = here | there
                lane, next_lane = lanes == first + j, lanes == first + j + 1
                left, right = columns[j], columns[j + 1]
                a, b, c = row(left, j), row(right, j), row(right, j + 1)
                scale = 1.0 / (a * c - b * b)
                by_top = jnp.where(here, -c, jnp.where(there, b, left * c - right * b))
                by_bottom = jnp.where(here, b, jnp.where(there, -a, right * a - left * b))
                top, bottom = row(panel, j), row(panel, j + 1)
                ratio = b / a
                kept = jnp.where(here, top, jnp.where(there, bottom - ratio * jnp.where(lane, 1.0, top), kept))
                kept = jnp.where(there & lane, -ratio, kept)
                top = jnp.where(lane, 1.0, jnp.where(next_lane, 0.0, top))
                bottom = jnp.where(lane, 0.0, jnp.where(next_lane, 1.0, bottom))
                panel = jnp.where(both | lane | next_lane, 0.0, panel) - (by_top * top + by_bottom * bottom) * scale
                for m in range(j + 2, block):
                    up, down = row(columns[m], j), row(columns[m], j + 1)
                    columns[m] = jnp.where(both, 0.0, columns[m]) - (by_top * up + by_bottom * down) * scale
            finished.append(kept)
            group[at] = panel
            rows = [row(panel, m) for m in range(block)]
            inside = (lanes >= first) & (lanes < first + block)
            for s in range(per_group):
                if s != at:
                    terms = [column(group[s], first + m) * rows[m] for m in range(block)]
                    while len(terms) > 1:
                        terms = [x + y for x, y in zip(terms[::2], terms[1::2])]
                    group[s] = jnp.where(inside, 0.0, group[s]) - terms[0]
        strips = strips[per_group:]
        if strips:
            first, last = begin * block, (begin + per_group) * block
            below = jnp.concatenate(strips, axis=0)
            solved = [jnp.zeros((first, width), F32)] if first else []
            solved = jnp.concatenate(solved + group + [jnp.zeros((width - last, width), F32)], axis=0)
            cols = lax.broadcasted_iota(jnp.int32, below.shape, 1)
            below = jnp.where((cols >= first) & (cols < last), 0.0, below) - dot3(below, solved)
            strips = [below[r : r + block, :] for r in range(0, below.shape[0], block)]
    return jnp.concatenate(finished, axis=0)


def final_kernel(total_rows, pieces_ref, now_ref, shifted_ref, basis_ref, projection_ref, rfactor_ref):
    width = now_ref.shape[1]
    piece = pieces_ref.shape[1] // 3
    pieces = pieces_ref[...]
    late = sum_high_and_low(pieces[:, : 2 * piece, :]).reshape(-1, width)
    early = pieces[:, 2 * piece :, :].astype(F32).reshape(-1, width)
    now_product, square = late[:width], late[width : 2 * width]
    now_square, shift = early[:width], early[width : 2 * width]
    projection = now_product * total_rows**-0.5
    projection_ref[...] = projection
    scaled = now_product * (1.0 / total_rows)
    half = shift - 0.5 * now_product + 0.5 * dot3(now_square, scaled)
    mixed = dot3(scaled, half, TN)
    gram = square + mixed + mixed.T
    reduced = eliminate(gram * (1.0 / total_rows))
    rows = lax.broadcasted_iota(jnp.int32, reduced.shape, 0)
    cols = lax.broadcasted_iota(jnp.int32, reduced.shape, 1)
    diagonal = jnp.sum(jnp.where(rows == cols, reduced, 0.0), axis=1, keepdims=True)
    root = lax.rsqrt(diagonal)
    rfactor_ref[...] = jnp.where(rows <= cols, reduced, 0.0) * root
    inverse = jnp.where(rows > cols, reduced, jnp.where(rows == cols, 1.0, 0.0)) * root
    residual = shifted_ref[...] - dot3(now_ref[...], scaled)
    basis_ref[...] = dot3(residual, inverse, NT)


def exchange(blocks, axis, steps):
    n = lax.axis_size(axis)
    assert n & (n - 1) == 0
    return [lax.ppermute(block, axis, [(i, i ^ step) for i in range(n)]) for step, block in zip(steps, blocks)]


def on_device(basis_now, basis_prev, coupling, tiles, tile_rows, tile_cols, tile_counts):
    rows_dev, width = basis_now.shape
    n_row, n_col = lax.axis_size("row"), lax.axis_size("col")
    devices = n_row * n_col
    tile_block = tiles[0, 0]
    total_rows = float(rows_dev * devices)
    piece = -(-2 * width // (8 * devices)) * 8
    smem = pl.BlockSpec(memory_space=pltpu.SMEM)
    vmem = pl.BlockSpec(memory_space=pltpu.VMEM)
    params = pltpu.CompilerParams(vmem_limit_bytes=48 * 1024 * 1024)

    both = jnp.concatenate([basis_now, basis_prev], axis=1).astype(BF16)
    gathered = lax.all_gather(both, "col", axis=0, tiled=True)
    me = jnp.stack([lax.axis_index("row"), lax.axis_index("col")])
    half = n_row // 2
    block = jax.ShapeDtypeStruct((rows_dev + 2 * piece, width), BF16)
    sums = jax.ShapeDtypeStruct((rows_dev + piece, width), F32)
    *blocks, far, own = pl.pallas_call(
        functools.partial(tiles_kernel, n_row, n_col, total_rows),
        out_shape=[block] * (2 * half - 2) + [sums] * 2,
        in_specs=[smem] * 3 + [vmem] * 4,
        out_specs=[vmem] * (2 * half),
        scratch_shapes=[
            pltpu.VMEM((n_row * rows_dev, width), F32),
            pltpu.VMEM((devices * piece, width), F32),
        ],
        compiler_params=params,
        name="tile_products",
    )(me, tile_rows, tile_cols, tile_counts, tile_block, gathered, coupling)
    steps = distances(half)[:-1]
    mirrors = exchange(blocks[: half - 1], "row", steps)
    near = exchange(blocks[half - 1 :], "row", steps)
    mirror = pl.pallas_call(
        functools.partial(mirror_kernel, rows_dev),
        out_shape=block,
        in_specs=[vmem] * half,
        out_specs=vmem,
        compiler_params=params,
        name="mirror_sum",
    )(far, *mirrors)
    across = exchange([mirror], "row", [half])

    shift = pl.pallas_call(
        shift_kernel,
        out_shape=jax.ShapeDtypeStruct((rows_dev, width), F32),
        in_specs=[vmem] * 2,
        out_specs=vmem,
        compiler_params=params,
        cost_estimate=pl.CostEstimate(flops=12 * rows_dev * width * width, bytes_accessed=12 * rows_dev * width, transcendentals=0),
        name="shift_by_previous",
    )(basis_prev, coupling)
    shifted, grams, early = pl.pallas_call(
        grams_kernel,
        out_shape=(
            jax.ShapeDtypeStruct((rows_dev, width), F32),
            jax.ShapeDtypeStruct((devices * piece, width), F32),
            jax.ShapeDtypeStruct((piece, width), F32),
        ),
        in_specs=[vmem] * (3 + half),
        out_specs=(vmem, vmem, vmem),
        compiler_params=params,
        name="local_grams",
    )(basis_now, shift, own, *near, *across)
    everyone = ("row", "col")
    pieces = lax.all_to_all(grams.reshape(devices, piece, width), everyone, split_axis=0, concat_axis=0, tiled=True)
    copies = pl.pallas_call(
        spread_kernel,
        out_shape=jax.ShapeDtypeStruct((devices, 3 * piece, width), BF16),
        in_specs=[vmem, vmem],
        out_specs=vmem,
        compiler_params=params,
        name="sum_and_spread",
    )(pieces, early)
    gathered_sums = lax.all_to_all(copies, everyone, split_axis=0, concat_axis=0, tiled=True)
    return pl.pallas_call(
        functools.partial(final_kernel, total_rows),
        out_shape=(
            jax.ShapeDtypeStruct((rows_dev, width), F32),
            jax.ShapeDtypeStruct((width, width), F32),
            jax.ShapeDtypeStruct((width, width), F32),
        ),
        in_specs=[vmem] * 3,
        out_specs=(vmem, vmem, vmem),
        compiler_params=params,
        name="factor_and_basis",
    )(gathered_sums, basis_now, shifted)


def solution(mesh):
    placed = (
        P(("row", "col"), None),
        P(("row", "col"), None),
        P(),
        P("row", "col", None, None, None),
        P("row", "col", None),
        P("row", "col", None),
        P("row", "col"),
    )
    return jax.shard_map(
        on_device,
        mesh=mesh,
        in_specs=placed,
        out_specs=(P(("row", "col"), None), P(), P()),
        check_vma=False,
    )
```

```python
import functools

import jax
import jax.numpy as jnp
from jax import lax
from jax.experimental import pallas as pl
from jax.experimental.pallas import tpu as pltpu
from jax.sharding import PartitionSpec as P

F32 = jnp.float32
BF16 = jnp.bfloat16
NN, TN, NT = [(((x,), (y,)), ((), ())) for x, y in ((1, 0), (0, 0), (1, 1))]


def split(x):
    high = x.astype(BF16)
    return high, (x - high.astype(F32)).astype(BF16)


def dot3(a, b, dims=NN):
    (a_high, a_low), (b_high, b_low) = split(a), split(b)

    def one(x, y):
        return lax.dot_general(x, y, dims, preferred_element_type=F32)

    return one(a_high, b_low) + one(a_low, b_high) + one(a_high, b_high)


def upper_of(x):
    rows = lax.broadcasted_iota(jnp.int32, x.shape, 0)
    cols = lax.broadcasted_iota(jnp.int32, x.shape, 1)
    return jnp.where(rows <= cols, x, 0.0)


def distances(n):
    return range(n - 1, -1, -1)


def high_and_low(value):
    high = value.astype(BF16)
    low = (value - high.astype(F32)).astype(BF16)
    return jnp.concatenate([high, low], axis=0)


def sum_high_and_low(value):
    half = value.shape[-2] // 2
    value = value.astype(F32)
    return value[..., :half, :] + value[..., half:, :]


def prepare_kernel(now_hbm, prev_hbm, rows_hbm, cols_hbm, tiles_hbm, both_ref, rows_ref, cols_ref, tiles_ref, now_ref, prev_ref, sems):
    pairs = (
        (now_hbm, now_ref),
        (prev_hbm, prev_ref),
        (rows_hbm, rows_ref),
        (cols_hbm, cols_ref),
        (tiles_hbm, tiles_ref),
    )
    copies = [pltpu.make_async_copy(source, target, sems.at[k]) for k, (source, target) in enumerate(pairs)]
    for copy in copies:
        copy.start()
    rows_dev = now_ref.shape[0]
    copies[0].wait()
    both_ref[:rows_dev, :] = now_ref[...].astype(BF16)
    copies[1].wait()
    both_ref[rows_dev:, :] = prev_ref[...].astype(BF16)
    for copy in copies[2:]:
        copy.wait()


def tiles_kernel(n_row, n_col, total_rows, me_ref, rows_ref, cols_ref, count_ref, tiles_ref, basis_ref, coupling_ref, *refs):
    half = n_row // 2
    mirror_refs, near_refs, (far_ref, own_ref, total_ref, early_ref) = refs[: half - 1], refs[half - 1 : -4], refs[-4:]
    slots, size, _ = tiles_ref.shape
    width = total_ref.shape[1]
    rows_dev = total_ref.shape[0] // n_row
    piece = early_ref.shape[0] // (n_row * n_col)
    my_row, my_col = me_ref[0], me_ref[1]
    total_ref[...] = jnp.zeros_like(total_ref)
    grams = jnp.zeros((width, 2 * width), F32)
    for slab in range(n_col):
        now = basis_ref[2 * slab * rows_dev : (2 * slab + 1) * rows_dev, :]
        prev = basis_ref[(2 * slab + 1) * rows_dev : (2 * slab + 2) * rows_dev, :]
        grams += lax.dot_general(now, jnp.concatenate([now, prev], axis=1), TN, preferred_element_type=F32)
    square, cross = grams[:, :width], grams[:, width:]
    rows = lax.broadcasted_iota(jnp.int32, square.shape, 0)
    cols = lax.broadcasted_iota(jnp.int32, square.shape, 1)
    if early_ref.shape[0] > 2 * width:
        early_ref[...] = jnp.zeros_like(early_ref)
    early_ref[:width, :] = square - jnp.where(rows == cols, total_rows / n_row, 0.0)
    early_ref[width : 2 * width, :] = dot3(cross, upper_of(coupling_ref[...]), NT)
    used = count_ref[...]
    per_slab = rows_dev // size
    for slot in range(slots):
        col = cols_ref[0, 0, slot]
        start = pl.multiple_of((2 * per_slab * (col // per_slab) + lax.rem(col, per_slab)) * size, size)
        value = jnp.dot(tiles_ref[slot], basis_ref[pl.ds(start, size), :], preferred_element_type=F32)
        value = value * (slot < used).astype(F32)
        place = pl.ds(pl.multiple_of(rows_ref[0, 0, slot] * size, size), size)
        total_ref[place, :] += value

    def parts_of(row):
        slab = total_ref[pl.ds(pl.multiple_of(row * rows_dev, rows_dev), rows_dev), :]
        return slab, early_ref[pl.ds(pl.multiple_of((row * n_col + my_col) * piece, piece), piece), :]

    for step, mirror_ref, near_ref in zip(distances(half), mirror_refs, near_refs):
        write_block(mirror_ref, *parts_of(my_row ^ (step + half)))
        write_block(near_ref, *parts_of(my_row ^ step))
    for row, ref in ((my_row ^ half, far_ref), (my_row, own_ref)):
        ref[:rows_dev, :], ref[rows_dev:, :] = parts_of(row)


def write_block(ref, slab, early):
    rows_dev = slab.shape[0]
    ref[:rows_dev, :] = slab.astype(BF16)
    ref[rows_dev:, :] = high_and_low(early)


def add_blocks(own_ref, block_refs, rows_dev):
    slab, early = own_ref[:rows_dev, :], own_ref[rows_dev:, :]
    for ref in block_refs:
        slab = slab + ref[:rows_dev, :].astype(F32)
        early = early + sum_high_and_low(ref[rows_dev:, :])
    return slab, early


def mirror_kernel(rows_dev, own_ref, *refs):
    block_refs, out_ref = refs[:-1], refs[-1]
    write_block(out_ref, *add_blocks(own_ref, block_refs, rows_dev))


def shift_kernel(prev_ref, coupling_ref, shift_ref):
    shift_ref[...] = dot3(prev_ref[...], upper_of(coupling_ref[...]), NT)


def grams_kernel(now_ref, shift_ref, own_ref, *refs):
    block_refs, (shifted_ref, grams_ref, early_ref) = refs[:-3], refs[-3:]
    rows_dev, width = now_ref.shape
    product, early_ref[...] = add_blocks(own_ref, block_refs, rows_dev)
    shifted = product - shift_ref[...]
    shifted_ref[...] = shifted
    if grams_ref.shape[0] > 2 * width:
        grams_ref[...] = jnp.zeros_like(grams_ref)
    grams_ref[:width, :] = dot3(now_ref[...], product, TN)
    grams_ref[width : 2 * width, :] = dot3(shifted, shifted, TN)


def spread_kernel(parts_ref, early_ref, out_ref):
    total = parts_ref[0]
    for part in range(1, parts_ref.shape[0]):
        total = total + parts_ref[part]
    value = jnp.concatenate([high_and_low(total), early_ref[...].astype(BF16)], axis=0)
    for part in range(out_ref.shape[0]):
        out_ref[part] = value


def eliminate(gram):
    width = gram.shape[0]
    block, per_group = 16, 2
    lanes = lax.broadcasted_iota(jnp.int32, (block, width), 1)
    subs = lax.broadcasted_iota(jnp.int32, (block, width), 0)

    def column(strip, k):
        return jnp.broadcast_to(strip[:, k : k + 1], (block, width))

    def row(strip, k):
        return jnp.broadcast_to(strip[k : k + 1, :], (block, width))

    strips = [gram[r : r + block, :] for r in range(0, width, block)]
    finished = []
    for begin in range(0, len(strips), per_group):
        group = strips[:per_group]
        for at in range(per_group):
            first = (begin + at) * block
            panel = group[at]
            columns = [column(panel, first + j) for j in range(block)]
            kept = panel
            for j in range(0, block, 2):
                here, there = subs == j, subs == j + 1
                both = here | there
                lane, next_lane = lanes == first + j, lanes == first + j + 1
                left, right = columns[j], columns[j + 1]
                a, b, c = row(left, j), row(right, j), row(right, j + 1)
                scale = 1.0 / (a * c - b * b)
                by_top = jnp.where(here, -c, jnp.where(there, b, left * c - right * b))
                by_bottom = jnp.where(here, b, jnp.where(there, -a, right * a - left * b))
                top, bottom = row(panel, j), row(panel, j + 1)
                ratio = b / a
                kept = jnp.where(here, top, jnp.where(there, bottom - ratio * jnp.where(lane, 1.0, top), kept))
                kept = jnp.where(there & lane, -ratio, kept)
                top = jnp.where(lane, 1.0, jnp.where(next_lane, 0.0, top))
                bottom = jnp.where(lane, 0.0, jnp.where(next_lane, 1.0, bottom))
                panel = jnp.where(both | lane | next_lane, 0.0, panel) - (by_top * top + by_bottom * bottom) * scale
                for m in range(j + 2, block):
                    up, down = row(columns[m], j), row(columns[m], j + 1)
                    columns[m] = jnp.where(both, 0.0, columns[m]) - (by_top * up + by_bottom * down) * scale
            finished.append(kept)
            group[at] = panel
            rows = [row(panel, m) for m in range(block)]
            inside = (lanes >= first) & (lanes < first + block)
            for s in range(per_group):
                if s != at:
                    terms = [column(group[s], first + m) * rows[m] for m in range(block)]
                    while len(terms) > 1:
                        terms = [x + y for x, y in zip(terms[::2], terms[1::2])]
                    group[s] = jnp.where(inside, 0.0, group[s]) - terms[0]
        strips = strips[per_group:]
        if strips:
            first, last = begin * block, (begin + per_group) * block
            below = jnp.concatenate(strips, axis=0)
            solved = [jnp.zeros((first, width), F32)] if first else []
            solved = jnp.concatenate(solved + group + [jnp.zeros((width - last, width), F32)], axis=0)
            cols = lax.broadcasted_iota(jnp.int32, below.shape, 1)
            below = jnp.where((cols >= first) & (cols < last), 0.0, below) - dot3(below, solved)
            strips = [below[r : r + block, :] for r in range(0, below.shape[0], block)]
    return jnp.concatenate(finished, axis=0)


def final_kernel(total_rows, pieces_ref, now_ref, shifted_ref, basis_ref, projection_ref, rfactor_ref):
    width = now_ref.shape[1]
    piece = pieces_ref.shape[1] // 3
    pieces = pieces_ref[...]
    late = sum_high_and_low(pieces[:, : 2 * piece, :]).reshape(-1, width)
    early = pieces[:, 2 * piece :, :].astype(F32).reshape(-1, width)
    now_product, square = late[:width], late[width : 2 * width]
    now_square, shift = early[:width], early[width : 2 * width]
    projection = now_product * total_rows**-0.5
    projection_ref[...] = projection
    scaled = now_product * (1.0 / total_rows)
    half = shift - 0.5 * now_product + 0.5 * dot3(now_square, scaled)
    mixed = dot3(scaled, half, TN)
    gram = square + mixed + mixed.T
    reduced = eliminate(gram * (1.0 / total_rows))
    rows = lax.broadcasted_iota(jnp.int32, reduced.shape, 0)
    cols = lax.broadcasted_iota(jnp.int32, reduced.shape, 1)
    diagonal = jnp.sum(jnp.where(rows == cols, reduced, 0.0), axis=1, keepdims=True)
    root = lax.rsqrt(diagonal)
    rfactor_ref[...] = jnp.where(rows <= cols, reduced, 0.0) * root
    inverse = jnp.where(rows > cols, reduced, jnp.where(rows == cols, 1.0, 0.0)) * root
    residual = shifted_ref[...] - dot3(now_ref[...], scaled)
    basis_ref[...] = dot3(residual, inverse, NT)


def exchange(blocks, axis, steps):
    n = lax.axis_size(axis)
    assert n & (n - 1) == 0
    return [lax.ppermute(block, axis, [(i, i ^ step) for i in range(n)]) for step, block in zip(steps, blocks)]


def on_device(basis_now, basis_prev, coupling, tiles, tile_rows, tile_cols, tile_counts):
    rows_dev, width = basis_now.shape
    n_row, n_col = lax.axis_size("row"), lax.axis_size("col")
    devices = n_row * n_col
    tile_block = tiles[0, 0]
    total_rows = float(rows_dev * devices)
    piece = -(-2 * width // (8 * devices)) * 8
    smem = pl.BlockSpec(memory_space=pltpu.SMEM)
    vmem = pl.BlockSpec(memory_space=pltpu.VMEM)
    params = pltpu.CompilerParams(vmem_limit_bytes=48 * 1024 * 1024)

    in_hbm = [pltpu.with_memory_space_constraint(x, pltpu.HBM) for x in (basis_now, basis_prev, tile_rows, tile_cols, tile_block)]
    both, rows, cols, tile_block = pl.pallas_call(
        prepare_kernel,
        out_shape=(
            jax.ShapeDtypeStruct((2 * rows_dev, width), BF16),
            jax.ShapeDtypeStruct(tile_rows.shape, tile_rows.dtype),
            jax.ShapeDtypeStruct(tile_cols.shape, tile_cols.dtype),
            jax.ShapeDtypeStruct(tile_block.shape, tile_block.dtype),
        ),
        in_specs=[pl.BlockSpec(memory_space=pltpu.HBM)] * 5,
        out_specs=(vmem, vmem, vmem, vmem),
        scratch_shapes=[
            pltpu.VMEM(basis_now.shape, F32),
            pltpu.VMEM(basis_prev.shape, F32),
            pltpu.SemaphoreType.DMA((5,)),
        ],
        compiler_params=params,
        name="prepare",
    )(*in_hbm)
    gathered = lax.all_gather(both, "col", axis=0, tiled=True)
    me = jnp.stack([lax.axis_index("row"), lax.axis_index("col")])
    half = n_row // 2
    block = jax.ShapeDtypeStruct((rows_dev + 2 * piece, width), BF16)
    sums = jax.ShapeDtypeStruct((rows_dev + piece, width), F32)
    *blocks, far, own = pl.pallas_call(
        functools.partial(tiles_kernel, n_row, n_col, total_rows),
        out_shape=[block] * (2 * half - 2) + [sums] * 2,
        in_specs=[smem] * 3 + [vmem] * 4,
        out_specs=[vmem] * (2 * half),
        scratch_shapes=[
            pltpu.VMEM((n_row * rows_dev, width), F32),
            pltpu.VMEM((devices * piece, width), F32),
        ],
        compiler_params=params,
        name="tile_products",
    )(me, rows, cols, tile_counts, tile_block, gathered, coupling)
    steps = distances(half)[:-1]
    mirrors = exchange(blocks[: half - 1], "row", steps)
    near = exchange(blocks[half - 1 :], "row", steps)
    mirror = pl.pallas_call(
        functools.partial(mirror_kernel, rows_dev),
        out_shape=block,
        in_specs=[vmem] * half,
        out_specs=vmem,
        compiler_params=params,
        name="mirror_sum",
    )(far, *mirrors)
    across = exchange([mirror], "row", [half])

    shift = pl.pallas_call(
        shift_kernel,
        out_shape=jax.ShapeDtypeStruct((rows_dev, width), F32),
        in_specs=[vmem] * 2,
        out_specs=vmem,
        compiler_params=params,
        cost_estimate=pl.CostEstimate(flops=12 * rows_dev * width * width, bytes_accessed=12 * rows_dev * width, transcendentals=0),
        name="shift_by_previous",
    )(basis_prev, coupling)
    shifted, grams, early = pl.pallas_call(
        grams_kernel,
        out_shape=(
            jax.ShapeDtypeStruct((rows_dev, width), F32),
            jax.ShapeDtypeStruct((devices * piece, width), F32),
            jax.ShapeDtypeStruct((piece, width), F32),
        ),
        in_specs=[vmem] * (3 + half),
        out_specs=(vmem, vmem, vmem),
        compiler_params=params,
        name="local_grams",
    )(basis_now, shift, own, *near, *across)
    everyone = ("row", "col")
    pieces = lax.all_to_all(grams.reshape(devices, piece, width), everyone, split_axis=0, concat_axis=0, tiled=True)
    copies = pl.pallas_call(
        spread_kernel,
        out_shape=jax.ShapeDtypeStruct((devices, 3 * piece, width), BF16),
        in_specs=[vmem, vmem],
        out_specs=vmem,
        compiler_params=params,
        name="sum_and_spread",
    )(pieces, early)
    gathered_sums = lax.all_to_all(copies, everyone, split_axis=0, concat_axis=0, tiled=True)
    return pl.pallas_call(
        functools.partial(final_kernel, total_rows),
        out_shape=(
            jax.ShapeDtypeStruct((rows_dev, width), F32),
            jax.ShapeDtypeStruct((width, width), F32),
            jax.ShapeDtypeStruct((width, width), F32),
        ),
        in_specs=[vmem] * 3,
        out_specs=(vmem, vmem, vmem),
        compiler_params=params,
        name="factor_and_basis",
    )(gathered_sums, basis_now, shifted)


def solution(mesh):
    placed = (
        P(("row", "col"), None),
        P(("row", "col"), None),
        P(),
        P("row", "col", None, None, None),
        P("row", "col", None),
        P("row", "col", None),
        P("row", "col"),
    )
    return jax.shard_map(
        on_device,
        mesh=mesh,
        in_specs=placed,
        out_specs=(P(("row", "col"), None), P(), P()),
        check_vma=False,
    )
```

```python
import functools

import jax
import jax.numpy as jnp
from jax import lax
from jax.experimental import pallas as pl
from jax.experimental.pallas import tpu as pltpu
from jax.sharding import PartitionSpec as P

F32 = jnp.float32
BF16 = jnp.bfloat16
NN, TN, NT = [(((x,), (y,)), ((), ())) for x, y in ((1, 0), (0, 0), (1, 1))]


def split(x):
    high = x.astype(BF16)
    return high, (x - high.astype(F32)).astype(BF16)


def dot3(a, b, dims=NN):
    (a_high, a_low), (b_high, b_low) = split(a), split(b)

    def one(x, y):
        return lax.dot_general(x, y, dims, preferred_element_type=F32)

    return one(a_high, b_low) + one(a_low, b_high) + one(a_high, b_high)


def upper_of(x):
    rows = lax.broadcasted_iota(jnp.int32, x.shape, 0)
    cols = lax.broadcasted_iota(jnp.int32, x.shape, 1)
    return jnp.where(rows <= cols, x, 0.0)


def distances(n):
    even = list(range(n - 1, 0, -1))
    odd = list(even)
    for k in range(1, len(odd) - 1, 2):
        odd[k], odd[k + 1] = odd[k + 1], odd[k]
    return list(zip(even, odd))


def high_and_low(value):
    high = value.astype(BF16)
    low = (value - high.astype(F32)).astype(BF16)
    return jnp.concatenate([high, low], axis=0)


def sum_high_and_low(value):
    half = value.shape[-2] // 2
    value = value.astype(F32)
    return value[..., :half, :] + value[..., half:, :]


def prepare_kernel(now_hbm, prev_hbm, rows_hbm, cols_hbm, tiles_hbm, both_ref, rows_ref, cols_ref, tiles_ref, now_ref, prev_ref, sems):
    pairs = (
        (now_hbm, now_ref),
        (prev_hbm, prev_ref),
        (rows_hbm, rows_ref),
        (cols_hbm, cols_ref),
        (tiles_hbm, tiles_ref),
    )
    copies = [pltpu.make_async_copy(source, target, sems.at[k]) for k, (source, target) in enumerate(pairs)]
    for copy in copies:
        copy.start()
    rows_dev = now_ref.shape[0]
    copies[0].wait()
    both_ref[:rows_dev, :] = now_ref[...].astype(BF16)
    copies[1].wait()
    both_ref[rows_dev:, :] = prev_ref[...].astype(BF16)
    for copy in copies[2:]:
        copy.wait()


def tiles_kernel(n_row, n_col, total_rows, me_ref, rows_ref, cols_ref, count_ref, tiles_ref, basis_ref, coupling_ref, *refs):
    half = n_row // 2
    mirror_refs, near_refs, (far_ref, own_ref, total_ref, early_ref) = refs[: half - 1], refs[half - 1 : -4], refs[-4:]
    slots, size, _ = tiles_ref.shape
    width = total_ref.shape[1]
    rows_dev = total_ref.shape[0] // n_row
    piece = early_ref.shape[0] // (n_row * n_col)
    my_row, my_col = me_ref[0], me_ref[1]
    total_ref[...] = jnp.zeros_like(total_ref)
    grams = jnp.zeros((width, 2 * width), F32)
    for slab in range(n_col):
        now = basis_ref[2 * slab * rows_dev : (2 * slab + 1) * rows_dev, :]
        prev = basis_ref[(2 * slab + 1) * rows_dev : (2 * slab + 2) * rows_dev, :]
        grams += lax.dot_general(now, jnp.concatenate([now, prev], axis=1), TN, preferred_element_type=F32)
    square, cross = grams[:, :width], grams[:, width:]
    rows = lax.broadcasted_iota(jnp.int32, square.shape, 0)
    cols = lax.broadcasted_iota(jnp.int32, square.shape, 1)
    if early_ref.shape[0] > 2 * width:
        early_ref[...] = jnp.zeros_like(early_ref)
    early_ref[:width, :] = square - jnp.where(rows == cols, total_rows / n_row, 0.0)
    early_ref[width : 2 * width, :] = dot3(cross, upper_of(coupling_ref[...]), NT)
    used = count_ref[...]
    per_slab = rows_dev // size
    for slot in range(slots):
        col = cols_ref[0, 0, slot]
        start = pl.multiple_of((2 * per_slab * (col // per_slab) + lax.rem(col, per_slab)) * size, size)
        value = jnp.dot(tiles_ref[slot], basis_ref[pl.ds(start, size), :], preferred_element_type=F32)
        value = value * (slot < used).astype(F32)
        place = pl.ds(pl.multiple_of(rows_ref[0, 0, slot] * size, size), size)
        total_ref[place, :] += value

    def parts_of(row):
        slab = total_ref[pl.ds(pl.multiple_of(row * rows_dev, rows_dev), rows_dev), :]
        return slab, early_ref[pl.ds(pl.multiple_of((row * n_col + my_col) * piece, piece), piece), :]

    odd_col = lax.rem(my_col, 2) == 1
    for (even, odd), mirror_ref, near_ref in zip(distances(half), mirror_refs, near_refs):
        step = jnp.where(odd_col, odd, even)
        write_block(mirror_ref, *parts_of(my_row ^ (step + half)))
        write_block(near_ref, *parts_of(my_row ^ step))
    for row, ref in ((my_row ^ half, far_ref), (my_row, own_ref)):
        ref[:rows_dev, :], ref[rows_dev:, :] = parts_of(row)


def write_block(ref, slab, early):
    rows_dev = slab.shape[0]
    ref[:rows_dev, :] = slab.astype(BF16)
    ref[rows_dev:, :] = high_and_low(early)


def add_blocks(own_ref, block_refs, rows_dev):
    slab, early = own_ref[:rows_dev, :], own_ref[rows_dev:, :]
    for ref in block_refs:
        slab = slab + ref[:rows_dev, :].astype(F32)
        early = early + sum_high_and_low(ref[rows_dev:, :])
    return slab, early


def mirror_kernel(rows_dev, own_ref, *refs):
    block_refs, out_ref = refs[:-1], refs[-1]
    write_block(out_ref, *add_blocks(own_ref, block_refs, rows_dev))


def shift_kernel(prev_ref, coupling_ref, shift_ref):
    shift_ref[...] = dot3(prev_ref[...], upper_of(coupling_ref[...]), NT)


def grams_kernel(now_ref, shift_ref, own_ref, *refs):
    block_refs, (shifted_ref, grams_ref, early_ref) = refs[:-3], refs[-3:]
    rows_dev, width = now_ref.shape
    product, early_ref[...] = add_blocks(own_ref, block_refs, rows_dev)
    shifted = product - shift_ref[...]
    shifted_ref[...] = shifted
    if grams_ref.shape[0] > 2 * width:
        grams_ref[...] = jnp.zeros_like(grams_ref)
    grams_ref[:width, :] = dot3(now_ref[...], product, TN)
    grams_ref[width : 2 * width, :] = dot3(shifted, shifted, TN)


def spread_kernel(parts_ref, early_ref, out_ref):
    total = parts_ref[0]
    for part in range(1, parts_ref.shape[0]):
        total = total + parts_ref[part]
    value = jnp.concatenate([high_and_low(total), early_ref[...].astype(BF16)], axis=0)
    for part in range(out_ref.shape[0]):
        out_ref[part] = value


def eliminate(gram):
    width = gram.shape[0]
    block, per_group = 16, 4
    lanes = lax.broadcasted_iota(jnp.int32, (block, width), 1)
    subs = lax.broadcasted_iota(jnp.int32, (block, width), 0)

    def column(strip, k):
        return jnp.broadcast_to(strip[:, k : k + 1], (block, width))

    def row(strip, k):
        return jnp.broadcast_to(strip[k : k + 1, :], (block, width))

    strips = [gram[r : r + block, :] for r in range(0, width, block)]
    finished = []
    for begin in range(0, len(strips), per_group):
        group = strips[:per_group]
        for at in range(per_group):
            first = (begin + at) * block
            panel = group[at]
            columns = [column(panel, first + j) for j in range(block)]
            kept = panel
            for j in range(0, block, 2):
                here, there = subs == j, subs == j + 1
                both = here | there
                lane, next_lane = lanes == first + j, lanes == first + j + 1
                left, right = columns[j], columns[j + 1]
                a, b, c = row(left, j), row(right, j), row(right, j + 1)
                scale = 1.0 / (a * c - b * b)
                by_top = jnp.where(here, -c, jnp.where(there, b, left * c - right * b))
                by_bottom = jnp.where(here, b, jnp.where(there, -a, right * a - left * b))
                top, bottom = row(panel, j), row(panel, j + 1)
                ratio = b / a
                kept = jnp.where(here, top, jnp.where(there, bottom - ratio * jnp.where(lane, 1.0, top), kept))
                kept = jnp.where(there & lane, -ratio, kept)
                top = jnp.where(lane, 1.0, jnp.where(next_lane, 0.0, top))
                bottom = jnp.where(lane, 0.0, jnp.where(next_lane, 1.0, bottom))
                panel = jnp.where(both | lane | next_lane, 0.0, panel) - (by_top * top + by_bottom * bottom) * scale
                for m in range(j + 2, block):
                    up, down = row(columns[m], j), row(columns[m], j + 1)
                    columns[m] = jnp.where(both, 0.0, columns[m]) - (by_top * up + by_bottom * down) * scale
            finished.append(kept)
            group[at] = panel
            rows = [row(panel, m) for m in range(block)]
            inside = (lanes >= first) & (lanes < first + block)
            for s in range(per_group):
                if s != at:
                    terms = [column(group[s], first + m) * rows[m] for m in range(block)]
                    while len(terms) > 1:
                        terms = [x + y for x, y in zip(terms[::2], terms[1::2])]
                    group[s] = jnp.where(inside, 0.0, group[s]) - terms[0]
        strips = strips[per_group:]
        if strips:
            first, last = begin * block, (begin + per_group) * block
            below = jnp.concatenate(strips, axis=0)
            solved = [jnp.zeros((first, width), F32)] if first else []
            solved = jnp.concatenate(solved + group + [jnp.zeros((width - last, width), F32)], axis=0)
            cols = lax.broadcasted_iota(jnp.int32, below.shape, 1)
            below = jnp.where((cols >= first) & (cols < last), 0.0, below) - dot3(below, solved)
            strips = [below[r : r + block, :] for r in range(0, below.shape[0], block)]
    return jnp.concatenate(finished, axis=0)


def final_kernel(total_rows, pieces_ref, now_ref, shifted_ref, basis_ref, projection_ref, rfactor_ref):
    width = now_ref.shape[1]
    piece = pieces_ref.shape[1] // 3
    pieces = pieces_ref[...]
    late = sum_high_and_low(pieces[:, : 2 * piece, :]).reshape(-1, width)
    early = pieces[:, 2 * piece :, :].astype(F32).reshape(-1, width)
    now_product, square = late[:width], late[width : 2 * width]
    now_square, shift = early[:width], early[width : 2 * width]
    projection = now_product * total_rows**-0.5
    projection_ref[...] = projection
    scaled = now_product * (1.0 / total_rows)
    half = shift - 0.5 * now_product + 0.5 * dot3(now_square, scaled)
    mixed = dot3(scaled, half, TN)
    gram = square + mixed + mixed.T
    reduced = eliminate(gram * (1.0 / total_rows))
    rows = lax.broadcasted_iota(jnp.int32, reduced.shape, 0)
    cols = lax.broadcasted_iota(jnp.int32, reduced.shape, 1)
    diagonal = jnp.sum(jnp.where(rows == cols, reduced, 0.0), axis=1, keepdims=True)
    root = lax.rsqrt(diagonal)
    rfactor_ref[...] = jnp.where(rows <= cols, reduced, 0.0) * root
    inverse = jnp.where(rows > cols, reduced, jnp.where(rows == cols, 1.0, 0.0)) * root
    residual = shifted_ref[...] - dot3(now_ref[...], scaled)
    basis_ref[...] = dot3(residual, inverse, NT)


def exchange(blocks, steps):
    n_row, n_col = lax.axis_size("row"), lax.axis_size("col")
    assert n_row & (n_row - 1) == 0
    received = []
    for step, block in zip(steps, blocks):
        pairs = [(i * n_col + j, (i ^ step[j % 2]) * n_col + j) for i in range(n_row) for j in range(n_col)]
        received.append(lax.ppermute(block, ("row", "col"), pairs))
    return received


def on_device(basis_now, basis_prev, coupling, tiles, tile_rows, tile_cols, tile_counts):
    rows_dev, width = basis_now.shape
    n_row, n_col = lax.axis_size("row"), lax.axis_size("col")
    devices = n_row * n_col
    tile_block = tiles[0, 0]
    total_rows = float(rows_dev * devices)
    piece = -(-2 * width // (8 * devices)) * 8
    smem = pl.BlockSpec(memory_space=pltpu.SMEM)
    vmem = pl.BlockSpec(memory_space=pltpu.VMEM)
    params = pltpu.CompilerParams(vmem_limit_bytes=48 * 1024 * 1024)

    in_hbm = [pltpu.with_memory_space_constraint(x, pltpu.HBM) for x in (basis_now, basis_prev, tile_rows, tile_cols, tile_block)]
    both, rows, cols, tile_block = pl.pallas_call(
        prepare_kernel,
        out_shape=(
            jax.ShapeDtypeStruct((2 * rows_dev, width), BF16),
            jax.ShapeDtypeStruct(tile_rows.shape, tile_rows.dtype),
            jax.ShapeDtypeStruct(tile_cols.shape, tile_cols.dtype),
            jax.ShapeDtypeStruct(tile_block.shape, tile_block.dtype),
        ),
        in_specs=[pl.BlockSpec(memory_space=pltpu.HBM)] * 5,
        out_specs=(vmem, vmem, vmem, vmem),
        scratch_shapes=[
            pltpu.VMEM(basis_now.shape, F32),
            pltpu.VMEM(basis_prev.shape, F32),
            pltpu.SemaphoreType.DMA((5,)),
        ],
        compiler_params=params,
        name="prepare",
    )(*in_hbm)
    gathered = lax.all_gather(both, "col", axis=0, tiled=True)
    me = jnp.stack([lax.axis_index("row"), lax.axis_index("col")])
    half = n_row // 2
    block = jax.ShapeDtypeStruct((rows_dev + 2 * piece, width), BF16)
    sums = jax.ShapeDtypeStruct((rows_dev + piece, width), F32)
    *blocks, far, own = pl.pallas_call(
        functools.partial(tiles_kernel, n_row, n_col, total_rows),
        out_shape=[block] * (2 * half - 2) + [sums] * 2,
        in_specs=[smem] * 3 + [vmem] * 4,
        out_specs=[vmem] * (2 * half),
        scratch_shapes=[
            pltpu.VMEM((n_row * rows_dev, width), F32),
            pltpu.VMEM((devices * piece, width), F32),
        ],
        compiler_params=params,
        name="tile_products",
    )(me, rows, cols, tile_counts, tile_block, gathered, coupling)
    steps = distances(half)
    mirrors = exchange(blocks[: half - 1], steps)
    near = exchange(blocks[half - 1 :], steps)
    mirror = pl.pallas_call(
        functools.partial(mirror_kernel, rows_dev),
        out_shape=block,
        in_specs=[vmem] * half,
        out_specs=vmem,
        compiler_params=params,
        name="mirror_sum",
    )(far, *mirrors)
    across = exchange([mirror], [(half, half)])

    shift = pl.pallas_call(
        shift_kernel,
        out_shape=jax.ShapeDtypeStruct((rows_dev, width), F32),
        in_specs=[vmem] * 2,
        out_specs=vmem,
        compiler_params=params,
        cost_estimate=pl.CostEstimate(flops=12 * rows_dev * width * width, bytes_accessed=12 * rows_dev * width, transcendentals=0),
        name="shift_by_previous",
    )(basis_prev, coupling)
    shifted, grams, early = pl.pallas_call(
        grams_kernel,
        out_shape=(
            jax.ShapeDtypeStruct((rows_dev, width), F32),
            jax.ShapeDtypeStruct((devices * piece, width), F32),
            jax.ShapeDtypeStruct((piece, width), F32),
        ),
        in_specs=[vmem] * (3 + half),
        out_specs=(vmem, vmem, vmem),
        compiler_params=params,
        name="local_grams",
    )(basis_now, shift, own, *near, *across)
    everyone = ("row", "col")
    pieces = lax.all_to_all(grams.reshape(devices, piece, width), everyone, split_axis=0, concat_axis=0, tiled=True)
    copies = pl.pallas_call(
        spread_kernel,
        out_shape=jax.ShapeDtypeStruct((devices, 3 * piece, width), BF16),
        in_specs=[vmem, vmem],
        out_specs=vmem,
        compiler_params=params,
        name="sum_and_spread",
    )(pieces, early)
    gathered_sums = lax.all_to_all(copies, everyone, split_axis=0, concat_axis=0, tiled=True)
    return pl.pallas_call(
        functools.partial(final_kernel, total_rows),
        out_shape=(
            jax.ShapeDtypeStruct((rows_dev, width), F32),
            jax.ShapeDtypeStruct((width, width), F32),
            jax.ShapeDtypeStruct((width, width), F32),
        ),
        in_specs=[vmem] * 3,
        out_specs=(vmem, vmem, vmem),
        compiler_params=params,
        name="factor_and_basis",
    )(gathered_sums, basis_now, shifted)


def solution(mesh):
    placed = (
        P(("row", "col"), None),
        P(("row", "col"), None),
        P(),
        P("row", "col", None, None, None),
        P("row", "col", None),
        P("row", "col", None),
        P("row", "col"),
    )
    return jax.shard_map(
        on_device,
        mesh=mesh,
        in_specs=placed,
        out_specs=(P(("row", "col"), None), P(), P()),
        check_vma=False,
    )
```

```python
import functools

import jax
import jax.numpy as jnp
from jax import lax
from jax.experimental import pallas as pl
from jax.experimental.pallas import tpu as pltpu
from jax.sharding import PartitionSpec as P

F32 = jnp.float32
BF16 = jnp.bfloat16
NN, TN, NT = [(((x,), (y,)), ((), ())) for x, y in ((1, 0), (0, 0), (1, 1))]


def split(x):
    high = x.astype(BF16)
    return high, (x - high.astype(F32)).astype(BF16)


def dot3(a, b, dims=NN):
    (a_high, a_low), (b_high, b_low) = split(a), split(b)

    def one(x, y):
        return lax.dot_general(x, y, dims, preferred_element_type=F32)

    return one(a_high, b_low) + one(a_low, b_high) + one(a_high, b_high)


def upper_of(x):
    rows = lax.broadcasted_iota(jnp.int32, x.shape, 0)
    cols = lax.broadcasted_iota(jnp.int32, x.shape, 1)
    return jnp.where(rows <= cols, x, 0.0)


def distances(n):
    return [1, *range(n - 1, 1, -1)]


def high_and_low(value):
    high = value.astype(BF16)
    low = (value - high.astype(F32)).astype(BF16)
    return jnp.concatenate([high, low], axis=0)


def sum_high_and_low(value):
    half = value.shape[-2] // 2
    value = value.astype(F32)
    return value[..., :half, :] + value[..., half:, :]


def prepare_kernel(now_hbm, prev_hbm, rows_hbm, cols_hbm, tiles_hbm, both_ref, rows_ref, cols_ref, tiles_ref, now_ref, prev_ref, sems):
    pairs = (
        (now_hbm, now_ref),
        (prev_hbm, prev_ref),
        (rows_hbm, rows_ref),
        (cols_hbm, cols_ref),
        (tiles_hbm, tiles_ref),
    )
    copies = [pltpu.make_async_copy(source, target, sems.at[k]) for k, (source, target) in enumerate(pairs)]
    for copy in copies:
        copy.start()
    rows_dev = now_ref.shape[0]
    copies[0].wait()
    both_ref[:rows_dev, :] = now_ref[...].astype(BF16)
    copies[1].wait()
    both_ref[rows_dev:, :] = prev_ref[...].astype(BF16)
    for copy in copies[2:]:
        copy.wait()


def tiles_kernel(n_row, n_col, total_rows, me_ref, rows_ref, cols_ref, count_ref, tiles_ref, basis_ref, coupling_ref, *refs):
    half = n_row // 2
    mirror_refs, near_refs, (far_ref, own_ref, total_ref, early_ref) = refs[: half - 1], refs[half - 1 : -4], refs[-4:]
    slots, size, _ = tiles_ref.shape
    width = total_ref.shape[1]
    rows_dev = total_ref.shape[0] // n_row
    piece = early_ref.shape[0] // (n_row * n_col)
    my_row, my_col = me_ref[0], me_ref[1]
    total_ref[...] = jnp.zeros_like(total_ref)
    grams = jnp.zeros((width, 2 * width), F32)
    for slab in range(n_col):
        now = basis_ref[2 * slab * rows_dev : (2 * slab + 1) * rows_dev, :]
        prev = basis_ref[(2 * slab + 1) * rows_dev : (2 * slab + 2) * rows_dev, :]
        grams += lax.dot_general(now, jnp.concatenate([now, prev], axis=1), TN, preferred_element_type=F32)
    square, cross = grams[:, :width], grams[:, width:]
    rows = lax.broadcasted_iota(jnp.int32, square.shape, 0)
    cols = lax.broadcasted_iota(jnp.int32, square.shape, 1)
    if early_ref.shape[0] > 2 * width:
        early_ref[...] = jnp.zeros_like(early_ref)
    early_ref[:width, :] = square - jnp.where(rows == cols, total_rows / n_row, 0.0)
    early_ref[width : 2 * width, :] = dot3(cross, upper_of(coupling_ref[...]), NT)
    used = count_ref[...]
    per_slab = rows_dev // size
    for slot in range(slots):
        col = cols_ref[0, 0, slot]
        start = pl.multiple_of((2 * per_slab * (col // per_slab) + lax.rem(col, per_slab)) * size, size)
        value = jnp.dot(tiles_ref[slot], basis_ref[pl.ds(start, size), :], preferred_element_type=F32)
        value = value * (slot < used).astype(F32)
        place = pl.ds(pl.multiple_of(rows_ref[0, 0, slot] * size, size), size)
        total_ref[place, :] += value

    def parts_of(row):
        slab = total_ref[pl.ds(pl.multiple_of(row * rows_dev, rows_dev), rows_dev), :]
        return slab, early_ref[pl.ds(pl.multiple_of((row * n_col + my_col) * piece, piece), piece), :]

    for step, mirror_ref, near_ref in zip(distances(half), mirror_refs, near_refs):
        write_block(mirror_ref, *parts_of(my_row ^ (step + half)))
        write_block(near_ref, *parts_of(my_row ^ step))
    for row, ref in ((my_row ^ half, far_ref), (my_row, own_ref)):
        ref[:rows_dev, :], ref[rows_dev:, :] = parts_of(row)


def write_block(ref, slab, early):
    rows_dev = slab.shape[0]
    ref[:rows_dev, :] = slab.astype(BF16)
    ref[rows_dev:, :] = early.astype(BF16)


def add_blocks(own_ref, block_refs, rows_dev):
    slab, early = own_ref[:rows_dev, :], own_ref[rows_dev:, :]
    for ref in block_refs:
        slab = slab + ref[:rows_dev, :].astype(F32)
        early = early + ref[rows_dev:, :].astype(F32)
    return slab, early


def mirror_kernel(rows_dev, own_ref, *refs):
    block_refs, out_ref = refs[:-1], refs[-1]
    write_block(out_ref, *add_blocks(own_ref, block_refs, rows_dev))


def shift_kernel(prev_ref, coupling_ref, shift_ref):
    shift_ref[...] = dot3(prev_ref[...], upper_of(coupling_ref[...]), NT)


def grams_kernel(now_ref, shift_ref, own_ref, *refs):
    block_refs, (shifted_ref, grams_ref, early_ref) = refs[:-3], refs[-3:]
    rows_dev, width = now_ref.shape
    product, early_ref[...] = add_blocks(own_ref, block_refs, rows_dev)
    shifted = product - shift_ref[...]
    shifted_ref[...] = shifted
    if grams_ref.shape[0] > 2 * width:
        grams_ref[...] = jnp.zeros_like(grams_ref)
    grams_ref[:width, :] = dot3(now_ref[...], product, TN)
    grams_ref[width : 2 * width, :] = dot3(shifted, shifted, TN)


def spread_kernel(parts_ref, early_ref, out_ref):
    total = parts_ref[0]
    for part in range(1, parts_ref.shape[0]):
        total = total + parts_ref[part]
    value = jnp.concatenate([high_and_low(total), early_ref[...].astype(BF16)], axis=0)
    for part in range(out_ref.shape[0]):
        out_ref[part] = value


def eliminate(gram):
    width = gram.shape[0]
    block, per_group = 16, 2
    lanes = lax.broadcasted_iota(jnp.int32, (block, width), 1)
    subs = lax.broadcasted_iota(jnp.int32, (block, width), 0)

    def column(strip, k):
        return jnp.broadcast_to(strip[:, k : k + 1], (block, width))

    def row(strip, k):
        return jnp.broadcast_to(strip[k : k + 1, :], (block, width))

    strips = [gram[r : r + block, :] for r in range(0, width, block)]
    finished = []
    for begin in range(0, len(strips), per_group):
        group = strips[:per_group]
        for at in range(per_group):
            first = (begin + at) * block
            panel = group[at]
            columns = [column(panel, first + j) for j in range(block)]
            kept = panel
            for j in range(0, block, 2):
                here, there = subs == j, subs == j + 1
                both = here | there
                lane, next_lane = lanes == first + j, lanes == first + j + 1
                left, right = columns[j], columns[j + 1]
                a, b, c = row(left, j), row(right, j), row(right, j + 1)
                scale = 1.0 / (a * c - b * b)
                by_top = jnp.where(here, -c, jnp.where(there, b, left * c - right * b))
                by_bottom = jnp.where(here, b, jnp.where(there, -a, right * a - left * b))
                top, bottom = row(panel, j), row(panel, j + 1)
                ratio = b / a
                kept = jnp.where(here, top, jnp.where(there, bottom - ratio * jnp.where(lane, 1.0, top), kept))
                kept = jnp.where(there & lane, -ratio, kept)
                top = jnp.where(lane, 1.0, jnp.where(next_lane, 0.0, top))
                bottom = jnp.where(lane, 0.0, jnp.where(next_lane, 1.0, bottom))
                panel = jnp.where(both | lane | next_lane, 0.0, panel) - (by_top * top + by_bottom * bottom) * scale
                for m in range(j + 2, block):
                    up, down = row(columns[m], j), row(columns[m], j + 1)
                    columns[m] = jnp.where(both, 0.0, columns[m]) - (by_top * up + by_bottom * down) * scale
            finished.append(kept)
            group[at] = panel
            rows = [row(panel, m) for m in range(block)]
            inside = (lanes >= first) & (lanes < first + block)
            for s in range(per_group):
                if s != at:
                    terms = [column(group[s], first + m) * rows[m] for m in range(block)]
                    while len(terms) > 1:
                        terms = [x + y for x, y in zip(terms[::2], terms[1::2])]
                    group[s] = jnp.where(inside, 0.0, group[s]) - terms[0]
        strips = strips[per_group:]
        if strips:
            first, last = begin * block, (begin + per_group) * block
            below = jnp.concatenate(strips, axis=0)
            solved = [jnp.zeros((first, width), F32)] if first else []
            solved = jnp.concatenate(solved + group + [jnp.zeros((width - last, width), F32)], axis=0)
            cols = lax.broadcasted_iota(jnp.int32, below.shape, 1)
            below = jnp.where((cols >= first) & (cols < last), 0.0, below) - dot3(below, solved)
            strips = [below[r : r + block, :] for r in range(0, below.shape[0], block)]
    return jnp.concatenate(finished, axis=0)


def final_kernel(total_rows, pieces_ref, now_ref, shifted_ref, basis_ref, projection_ref, rfactor_ref):
    width = now_ref.shape[1]
    piece = pieces_ref.shape[1] // 3
    pieces = pieces_ref[...]
    late = sum_high_and_low(pieces[:, : 2 * piece, :]).reshape(-1, width)
    early = pieces[:, 2 * piece :, :].astype(F32).reshape(-1, width)
    now_product, square = late[:width], late[width : 2 * width]
    now_square, shift = early[:width], early[width : 2 * width]
    projection = now_product * total_rows**-0.5
    projection_ref[...] = projection
    scaled = now_product * (1.0 / total_rows)
    half = shift - 0.5 * now_product + 0.5 * dot3(now_square, scaled)
    mixed = dot3(scaled, half, TN)
    gram = square + mixed + mixed.T
    reduced = eliminate(gram * (1.0 / total_rows))
    rows = lax.broadcasted_iota(jnp.int32, reduced.shape, 0)
    cols = lax.broadcasted_iota(jnp.int32, reduced.shape, 1)
    diagonal = jnp.sum(jnp.where(rows == cols, reduced, 0.0), axis=1, keepdims=True)
    root = lax.rsqrt(diagonal)
    rfactor_ref[...] = jnp.where(rows <= cols, reduced, 0.0) * root
    inverse = jnp.where(rows > cols, reduced, jnp.where(rows == cols, 1.0, 0.0)) * root
    residual = shifted_ref[...] - dot3(now_ref[...], scaled)
    basis_ref[...] = dot3(residual, inverse, NT)


def exchange(blocks, axis, steps):
    n = lax.axis_size(axis)
    assert n & (n - 1) == 0
    return [lax.ppermute(block, axis, [(i, i ^ step) for i in range(n)]) for step, block in zip(steps, blocks)]


def on_device(basis_now, basis_prev, coupling, tiles, tile_rows, tile_cols, tile_counts):
    rows_dev, width = basis_now.shape
    n_row, n_col = lax.axis_size("row"), lax.axis_size("col")
    devices = n_row * n_col
    tile_block = tiles[0, 0]
    total_rows = float(rows_dev * devices)
    piece = -(-2 * width // (8 * devices)) * 8
    smem = pl.BlockSpec(memory_space=pltpu.SMEM)
    vmem = pl.BlockSpec(memory_space=pltpu.VMEM)
    params = pltpu.CompilerParams(vmem_limit_bytes=48 * 1024 * 1024)

    in_hbm = [pltpu.with_memory_space_constraint(x, pltpu.HBM) for x in (basis_now, basis_prev, tile_rows, tile_cols, tile_block)]
    both, rows, cols, tile_block = pl.pallas_call(
        prepare_kernel,
        out_shape=(
            jax.ShapeDtypeStruct((2 * rows_dev, width), BF16),
            jax.ShapeDtypeStruct(tile_rows.shape, tile_rows.dtype),
            jax.ShapeDtypeStruct(tile_cols.shape, tile_cols.dtype),
            jax.ShapeDtypeStruct(tile_block.shape, tile_block.dtype),
        ),
        in_specs=[pl.BlockSpec(memory_space=pltpu.HBM)] * 5,
        out_specs=(vmem, vmem, vmem, vmem),
        scratch_shapes=[
            pltpu.VMEM(basis_now.shape, F32),
            pltpu.VMEM(basis_prev.shape, F32),
            pltpu.SemaphoreType.DMA((5,)),
        ],
        compiler_params=params,
        name="prepare",
    )(*in_hbm)
    gathered = lax.all_gather(both, "col", axis=0, tiled=True)
    me = jnp.stack([lax.axis_index("row"), lax.axis_index("col")])
    half = n_row // 2
    block = jax.ShapeDtypeStruct((rows_dev + piece, width), BF16)
    sums = jax.ShapeDtypeStruct((rows_dev + piece, width), F32)
    *blocks, far, own = pl.pallas_call(
        functools.partial(tiles_kernel, n_row, n_col, total_rows),
        out_shape=[block] * (2 * half - 2) + [sums] * 2,
        in_specs=[smem] * 3 + [vmem] * 4,
        out_specs=[vmem] * (2 * half),
        scratch_shapes=[
            pltpu.VMEM((n_row * rows_dev, width), F32),
            pltpu.VMEM((devices * piece, width), F32),
        ],
        compiler_params=params,
        name="tile_products",
    )(me, rows, cols, tile_counts, tile_block, gathered, coupling)
    steps = distances(half)
    mirrors = exchange(blocks[: half - 1], "row", steps)
    near = exchange(blocks[half - 1 :], "row", steps)
    mirror = pl.pallas_call(
        functools.partial(mirror_kernel, rows_dev),
        out_shape=block,
        in_specs=[vmem] * half,
        out_specs=vmem,
        compiler_params=params,
        name="mirror_sum",
    )(far, *mirrors)
    across = exchange([mirror], "row", [half])

    shift = pl.pallas_call(
        shift_kernel,
        out_shape=jax.ShapeDtypeStruct((rows_dev, width), F32),
        in_specs=[vmem] * 2,
        out_specs=vmem,
        compiler_params=params,
        cost_estimate=pl.CostEstimate(flops=12 * rows_dev * width * width, bytes_accessed=12 * rows_dev * width, transcendentals=0),
        name="shift_by_previous",
    )(basis_prev, coupling)
    shifted, grams, early = pl.pallas_call(
        grams_kernel,
        out_shape=(
            jax.ShapeDtypeStruct((rows_dev, width), F32),
            jax.ShapeDtypeStruct((devices * piece, width), F32),
            jax.ShapeDtypeStruct((piece, width), F32),
        ),
        in_specs=[vmem] * (3 + half),
        out_specs=(vmem, vmem, vmem),
        compiler_params=params,
        name="local_grams",
    )(basis_now, shift, own, *near, *across)
    everyone = ("row", "col")
    pieces = lax.all_to_all(grams.reshape(devices, piece, width), everyone, split_axis=0, concat_axis=0, tiled=True)
    copies = pl.pallas_call(
        spread_kernel,
        out_shape=jax.ShapeDtypeStruct((devices, 3 * piece, width), BF16),
        in_specs=[vmem, vmem],
        out_specs=vmem,
        compiler_params=params,
        name="sum_and_spread",
    )(pieces, early)
    gathered_sums = lax.all_to_all(copies, everyone, split_axis=0, concat_axis=0, tiled=True)
    return pl.pallas_call(
        functools.partial(final_kernel, total_rows),
        out_shape=(
            jax.ShapeDtypeStruct((rows_dev, width), F32),
            jax.ShapeDtypeStruct((width, width), F32),
            jax.ShapeDtypeStruct((width, width), F32),
        ),
        in_specs=[vmem] * 3,
        out_specs=(vmem, vmem, vmem),
        compiler_params=params,
        name="factor_and_basis",
    )(gathered_sums, basis_now, shifted)


def solution(mesh):
    placed = (
        P(("row", "col"), None),
        P(("row", "col"), None),
        P(),
        P("row", "col", None, None, None),
        P("row", "col", None),
        P("row", "col", None),
        P("row", "col"),
    )
    return jax.shard_map(
        on_device,
        mesh=mesh,
        in_specs=placed,
        out_specs=(P(("row", "col"), None), P(), P()),
        check_vma=False,
    )
```

```python
import functools

import jax
import jax.numpy as jnp
from jax import lax
from jax.experimental import pallas as pl
from jax.experimental.pallas import tpu as pltpu
from jax.sharding import PartitionSpec as P

F32 = jnp.float32
BF16 = jnp.bfloat16
NN, TN, NT = [(((x,), (y,)), ((), ())) for x, y in ((1, 0), (0, 0), (1, 1))]


def split(x):
    high = x.astype(BF16)
    return high, (x - high.astype(F32)).astype(BF16)


def dot3(a, b, dims=NN):
    (a_high, a_low), (b_high, b_low) = split(a), split(b)

    def one(x, y):
        return lax.dot_general(x, y, dims, preferred_element_type=F32)

    return one(a_high, b_low) + one(a_low, b_high) + one(a_high, b_high)


def upper_of(x):
    rows = lax.broadcasted_iota(jnp.int32, x.shape, 0)
    cols = lax.broadcasted_iota(jnp.int32, x.shape, 1)
    return jnp.where(rows <= cols, x, 0.0)


def distances(n):
    return [1, *range(n - 1, 1, -1)]


def high_and_low(value):
    high = value.astype(BF16)
    low = (value - high.astype(F32)).astype(BF16)
    return jnp.concatenate([high, low], axis=0)


def sum_high_and_low(value):
    half = value.shape[-2] // 2
    value = value.astype(F32)
    return value[..., :half, :] + value[..., half:, :]


def prepare_kernel(now_hbm, prev_hbm, rows_hbm, cols_hbm, tiles_hbm, both_ref, rows_ref, cols_ref, tiles_ref, now_ref, prev_ref, sems):
    pairs = (
        (now_hbm, now_ref),
        (prev_hbm, prev_ref),
        (rows_hbm, rows_ref),
        (cols_hbm, cols_ref),
        (tiles_hbm, tiles_ref),
    )
    copies = [pltpu.make_async_copy(source, target, sems.at[k]) for k, (source, target) in enumerate(pairs)]
    for copy in copies:
        copy.start()
    rows_dev = now_ref.shape[0]
    copies[0].wait()
    both_ref[:rows_dev, :] = now_ref[...].astype(BF16)
    copies[1].wait()
    both_ref[rows_dev:, :] = prev_ref[...].astype(BF16)
    for copy in copies[2:]:
        copy.wait()


def tiles_kernel(n_row, n_col, total_rows, me_ref, rows_ref, cols_ref, count_ref, tiles_ref, basis_ref, coupling_ref, *refs):
    half = n_row // 2
    mirror_refs, near_refs, (far_ref, own_ref, total_ref, early_ref) = refs[: half - 1], refs[half - 1 : -4], refs[-4:]
    slots, size, _ = tiles_ref.shape
    width = total_ref.shape[1]
    rows_dev = total_ref.shape[0] // n_row
    piece = early_ref.shape[0] // (n_row * n_col)
    my_row, my_col = me_ref[0], me_ref[1]
    total_ref[...] = jnp.zeros_like(total_ref)
    grams = jnp.zeros((width, 2 * width), F32)
    for slab in range(n_col):
        now = basis_ref[2 * slab * rows_dev : (2 * slab + 1) * rows_dev, :]
        prev = basis_ref[(2 * slab + 1) * rows_dev : (2 * slab + 2) * rows_dev, :]
        grams += lax.dot_general(now, jnp.concatenate([now, prev], axis=1), TN, preferred_element_type=F32)
    square, cross = grams[:, :width], grams[:, width:]
    rows = lax.broadcasted_iota(jnp.int32, square.shape, 0)
    cols = lax.broadcasted_iota(jnp.int32, square.shape, 1)
    if early_ref.shape[0] > 2 * width:
        early_ref[...] = jnp.zeros_like(early_ref)
    early_ref[:width, :] = square - jnp.where(rows == cols, total_rows / n_row, 0.0)
    early_ref[width : 2 * width, :] = dot3(cross, upper_of(coupling_ref[...]), NT)
    used = count_ref[...]
    per_slab = rows_dev // size
    for slot in range(slots):
        col = cols_ref[0, 0, slot]
        start = pl.multiple_of((2 * per_slab * (col // per_slab) + lax.rem(col, per_slab)) * size, size)
        value = jnp.dot(tiles_ref[slot], basis_ref[pl.ds(start, size), :], preferred_element_type=F32)
        value = value * (slot < used).astype(F32)
        place = pl.ds(pl.multiple_of(rows_ref[0, 0, slot] * size, size), size)
        total_ref[place, :] += value

    def parts_of(row):
        slab = total_ref[pl.ds(pl.multiple_of(row * rows_dev, rows_dev), rows_dev), :]
        return slab, early_ref[pl.ds(pl.multiple_of((row * n_col + my_col) * piece, piece), piece), :]

    for step, mirror_ref, near_ref in zip(distances(half), mirror_refs, near_refs):
        write_block(mirror_ref, *parts_of(my_row ^ (step + half)))
        write_block(near_ref, *parts_of(my_row ^ step))
    for row, ref in ((my_row ^ half, far_ref), (my_row, own_ref)):
        ref[:rows_dev, :], ref[rows_dev:, :] = parts_of(row)


def write_block(ref, slab, early):
    rows_dev = slab.shape[0]
    ref[:rows_dev, :] = slab.astype(BF16)
    ref[rows_dev:, :] = early.astype(BF16)


def add_blocks(own_ref, block_refs, rows_dev):
    slab, early = own_ref[:rows_dev, :], own_ref[rows_dev:, :]
    for ref in block_refs:
        slab = slab + ref[:rows_dev, :].astype(F32)
        early = early + ref[rows_dev:, :].astype(F32)
    return slab, early


def mirror_kernel(rows_dev, own_ref, *refs):
    block_refs, out_ref = refs[:-1], refs[-1]
    write_block(out_ref, *add_blocks(own_ref, block_refs, rows_dev))


def shift_kernel(prev_ref, coupling_ref, shift_ref):
    shift_ref[...] = dot3(prev_ref[...], upper_of(coupling_ref[...]), NT)


def grams_kernel(now_ref, shift_ref, own_ref, *refs):
    block_refs, (shifted_ref, grams_ref, early_ref) = refs[:-3], refs[-3:]
    rows_dev, width = now_ref.shape
    product, early_ref[...] = add_blocks(own_ref, block_refs, rows_dev)
    shifted = product - shift_ref[...]
    shifted_ref[...] = shifted
    if grams_ref.shape[0] > 2 * width:
        grams_ref[...] = jnp.zeros_like(grams_ref)
    grams_ref[:width, :] = dot3(now_ref[...], product, TN)
    grams_ref[width : 2 * width, :] = dot3(shifted, shifted, TN)


def spread_kernel(parts_ref, early_ref, out_ref):
    total = parts_ref[0]
    for part in range(1, parts_ref.shape[0]):
        total = total + parts_ref[part]
    value = jnp.concatenate([high_and_low(total), early_ref[...].astype(BF16)], axis=0)
    for part in range(out_ref.shape[0]):
        out_ref[part] = value


def eliminate(gram):
    width = gram.shape[0]
    block, per_group = 16, 2
    lanes = lax.broadcasted_iota(jnp.int32, (block, width), 1)
    subs = lax.broadcasted_iota(jnp.int32, (block, width), 0)

    def column(strip, k):
        return jnp.broadcast_to(strip[:, k : k + 1], (block, width))

    def row(strip, k):
        return jnp.broadcast_to(strip[k : k + 1, :], (block, width))

    strips = [gram[r : r + block, :] for r in range(0, width, block)]
    finished = []
    for begin in range(0, len(strips), per_group):
        group = strips[:per_group]
        for at in range(per_group):
            first = (begin + at) * block
            panel = group[at]
            columns = [column(panel, first + j) for j in range(block)]
            kept = panel
            for j in range(0, block, 2):
                here, there = subs == j, subs == j + 1
                both = here | there
                lane, next_lane = lanes == first + j, lanes == first + j + 1
                left, right = columns[j], columns[j + 1]
                a, b, c = row(left, j), row(right, j), row(right, j + 1)
                scale = 1.0 / (a * c - b * b)
                by_top = jnp.where(here, -c, jnp.where(there, b, left * c - right * b))
                by_bottom = jnp.where(here, b, jnp.where(there, -a, right * a - left * b))
                top, bottom = row(panel, j), row(panel, j + 1)
                ratio = b / a
                kept = jnp.where(here, top, jnp.where(there, bottom - ratio * jnp.where(lane, 1.0, top), kept))
                kept = jnp.where(there & lane, -ratio, kept)
                top = jnp.where(lane, 1.0, jnp.where(next_lane, 0.0, top))
                bottom = jnp.where(lane, 0.0, jnp.where(next_lane, 1.0, bottom))
                panel = jnp.where(both | lane | next_lane, 0.0, panel) - (by_top * top + by_bottom * bottom) * scale
                for m in range(j + 2, block):
                    up, down = row(columns[m], j), row(columns[m], j + 1)
                    columns[m] = jnp.where(both, 0.0, columns[m]) - (by_top * up + by_bottom * down) * scale
            finished.append(kept)
            group[at] = panel
            rows = [row(panel, m) for m in range(block)]
            inside = (lanes >= first) & (lanes < first + block)
            for s in range(per_group):
                if s != at:
                    terms = [column(group[s], first + m) * rows[m] for m in range(block)]
                    while len(terms) > 1:
                        terms = [x + y for x, y in zip(terms[::2], terms[1::2])]
                    group[s] = jnp.where(inside, 0.0, group[s]) - terms[0]
        strips = strips[per_group:]
        if strips:
            first, last = begin * block, (begin + per_group) * block
            below = jnp.concatenate(strips, axis=0)
            solved = [jnp.zeros((first, width), F32)] if first else []
            solved = jnp.concatenate(solved + group + [jnp.zeros((width - last, width), F32)], axis=0)
            cols = lax.broadcasted_iota(jnp.int32, below.shape, 1)
            below = jnp.where((cols >= first) & (cols < last), 0.0, below) - dot3(below, solved)
            strips = [below[r : r + block, :] for r in range(0, below.shape[0], block)]
    return jnp.concatenate(finished, axis=0)


def final_kernel(total_rows, pieces_ref, now_ref, shifted_ref, basis_ref, projection_ref, rfactor_ref):
    width = now_ref.shape[1]
    piece = pieces_ref.shape[1] // 3
    pieces = pieces_ref[...]
    late = sum_high_and_low(pieces[:, : 2 * piece, :]).reshape(-1, width)
    early = pieces[:, 2 * piece :, :].astype(F32).reshape(-1, width)
    now_product, square = late[:width], late[width : 2 * width]
    now_square, shift = early[:width], early[width : 2 * width]
    projection = now_product * total_rows**-0.5
    projection_ref[...] = projection
    scaled = now_product * (1.0 / total_rows)
    half = shift - 0.5 * now_product + 0.5 * dot3(now_square, scaled)
    mixed = dot3(scaled, half, TN)
    gram = square + mixed + mixed.T
    reduced = eliminate(gram * (1.0 / total_rows))
    rows = lax.broadcasted_iota(jnp.int32, reduced.shape, 0)
    cols = lax.broadcasted_iota(jnp.int32, reduced.shape, 1)
    diagonal = jnp.sum(jnp.where(rows == cols, reduced, 0.0), axis=1, keepdims=True)
    root = lax.rsqrt(diagonal)
    rfactor_ref[...] = jnp.where(rows <= cols, reduced, 0.0) * root
    inverse = jnp.where(rows > cols, reduced, jnp.where(rows == cols, 1.0, 0.0)) * root
    residual = shifted_ref[...] - dot3(now_ref[...], scaled)
    basis_ref[...] = dot3(residual, inverse, NT)


def exchange(blocks, axis, steps):
    n = lax.axis_size(axis)
    assert n & (n - 1) == 0
    return [lax.ppermute(block, axis, [(i, i ^ step) for i in range(n)]) for step, block in zip(steps, blocks)]


def on_device(basis_now, basis_prev, coupling, tiles, tile_rows, tile_cols, tile_counts):
    rows_dev, width = basis_now.shape
    n_row, n_col = lax.axis_size("row"), lax.axis_size("col")
    devices = n_row * n_col
    tile_block = tiles[0, 0]
    total_rows = float(rows_dev * devices)
    piece = -(-2 * width // (8 * devices)) * 8
    smem = pl.BlockSpec(memory_space=pltpu.SMEM)
    vmem = pl.BlockSpec(memory_space=pltpu.VMEM)
    params = pltpu.CompilerParams(vmem_limit_bytes=48 * 1024 * 1024)

    in_hbm = [pltpu.with_memory_space_constraint(x, pltpu.HBM) for x in (basis_now, basis_prev, tile_rows, tile_cols, tile_block)]
    both, rows, cols, tile_block = pl.pallas_call(
        prepare_kernel,
        out_shape=(
            jax.ShapeDtypeStruct((2 * rows_dev, width), BF16),
            jax.ShapeDtypeStruct(tile_rows.shape, tile_rows.dtype),
            jax.ShapeDtypeStruct(tile_cols.shape, tile_cols.dtype),
            jax.ShapeDtypeStruct(tile_block.shape, tile_block.dtype),
        ),
        in_specs=[pl.BlockSpec(memory_space=pltpu.HBM)] * 5,
        out_specs=(vmem, vmem, vmem, vmem),
        scratch_shapes=[
            pltpu.VMEM(basis_now.shape, F32),
            pltpu.VMEM(basis_prev.shape, F32),
            pltpu.SemaphoreType.DMA((5,)),
        ],
        compiler_params=params,
        name="prepare",
    )(*in_hbm)
    gathered = lax.all_gather(both, "col", axis=0, tiled=True)
    me = jnp.stack([lax.axis_index("row"), lax.axis_index("col")])
    half = n_row // 2
    block = jax.ShapeDtypeStruct((rows_dev + piece, width), BF16)
    sums = jax.ShapeDtypeStruct((rows_dev + piece, width), F32)
    *blocks, far, own = pl.pallas_call(
        functools.partial(tiles_kernel, n_row, n_col, total_rows),
        out_shape=[block] * (2 * half - 2) + [sums] * 2,
        in_specs=[smem] * 3 + [vmem] * 4,
        out_specs=[vmem] * (2 * half),
        scratch_shapes=[
            pltpu.VMEM((n_row * rows_dev, width), F32),
            pltpu.VMEM((devices * piece, width), F32),
        ],
        compiler_params=params,
        name="tile_products",
    )(me, rows, cols, tile_counts, tile_block, gathered, coupling)
    steps = distances(half)
    mirrors = exchange(blocks[: half - 1], "row", steps)
    near = exchange(blocks[half - 1 : -1], "row", steps[:-1])
    mirror = pl.pallas_call(
        functools.partial(mirror_kernel, rows_dev),
        out_shape=block,
        in_specs=[vmem] * half,
        out_specs=vmem,
        compiler_params=params,
        name="mirror_sum",
    )(far, *mirrors)
    mirror, last = lax.optimization_barrier((mirror, blocks[-1]))
    across = exchange([mirror], "row", [half])
    near += exchange([last], "row", steps[-1:])

    shift = pl.pallas_call(
        shift_kernel,
        out_shape=jax.ShapeDtypeStruct((rows_dev, width), F32),
        in_specs=[vmem] * 2,
        out_specs=vmem,
        compiler_params=params,
        cost_estimate=pl.CostEstimate(flops=12 * rows_dev * width * width, bytes_accessed=12 * rows_dev * width, transcendentals=0),
        name="shift_by_previous",
    )(basis_prev, coupling)
    shifted, grams, early = pl.pallas_call(
        grams_kernel,
        out_shape=(
            jax.ShapeDtypeStruct((rows_dev, width), F32),
            jax.ShapeDtypeStruct((devices * piece, width), F32),
            jax.ShapeDtypeStruct((piece, width), F32),
        ),
        in_specs=[vmem] * (3 + half),
        out_specs=(vmem, vmem, vmem),
        compiler_params=params,
        name="local_grams",
    )(basis_now, shift, own, *near[:-1], *across, near[-1])
    everyone = ("row", "col")
    pieces = lax.all_to_all(grams.reshape(devices, piece, width), everyone, split_axis=0, concat_axis=0, tiled=True)
    copies = pl.pallas_call(
        spread_kernel,
        out_shape=jax.ShapeDtypeStruct((devices, 3 * piece, width), BF16),
        in_specs=[vmem, vmem],
        out_specs=vmem,
        compiler_params=params,
        name="sum_and_spread",
    )(pieces, early)
    gathered_sums = lax.all_to_all(copies, everyone, split_axis=0, concat_axis=0, tiled=True)
    return pl.pallas_call(
        functools.partial(final_kernel, total_rows),
        out_shape=(
            jax.ShapeDtypeStruct((rows_dev, width), F32),
            jax.ShapeDtypeStruct((width, width), F32),
            jax.ShapeDtypeStruct((width, width), F32),
        ),
        in_specs=[vmem] * 3,
        out_specs=(vmem, vmem, vmem),
        compiler_params=params,
        name="factor_and_basis",
    )(gathered_sums, basis_now, shifted)


def solution(mesh):
    placed = (
        P(("row", "col"), None),
        P(("row", "col"), None),
        P(),
        P("row", "col", None, None, None),
        P("row", "col", None),
        P("row", "col", None),
        P("row", "col"),
    )
    return jax.shard_map(
        on_device,
        mesh=mesh,
        in_specs=placed,
        out_specs=(P(("row", "col"), None), P(), P()),
        check_vma=False,
    )
```

```python
import functools

import jax
import jax.numpy as jnp
from jax import lax
from jax.experimental import pallas as pl
from jax.experimental.pallas import tpu as pltpu
from jax.sharding import PartitionSpec as P

F32 = jnp.float32
BF16 = jnp.bfloat16
NN, TN, NT = [(((x,), (y,)), ((), ())) for x, y in ((1, 0), (0, 0), (1, 1))]


def split(x):
    high = x.astype(BF16)
    return high, (x - high.astype(F32)).astype(BF16)


def dot3(a, b, dims=NN):
    (a_high, a_low), (b_high, b_low) = split(a), split(b)

    def one(x, y):
        return lax.dot_general(x, y, dims, preferred_element_type=F32)

    return one(a_high, b_low) + one(a_low, b_high) + one(a_high, b_high)


def upper_of(x):
    rows = lax.broadcasted_iota(jnp.int32, x.shape, 0)
    cols = lax.broadcasted_iota(jnp.int32, x.shape, 1)
    return jnp.where(rows <= cols, x, 0.0)


def distances(n):
    return [1, *range(n - 1, 1, -1)]


def high_and_low(value):
    high = value.astype(BF16)
    low = (value - high.astype(F32)).astype(BF16)
    return jnp.concatenate([high, low], axis=0)


def sum_high_and_low(value):
    half = value.shape[-2] // 2
    value = value.astype(F32)
    return value[..., :half, :] + value[..., half:, :]


def prepare_kernel(now_hbm, prev_hbm, rows_hbm, cols_hbm, tiles_hbm, both_ref, rows_ref, cols_ref, tiles_ref, now_ref, prev_ref, sems):
    pairs = (
        (now_hbm, now_ref),
        (prev_hbm, prev_ref),
        (rows_hbm, rows_ref),
        (cols_hbm, cols_ref),
        (tiles_hbm, tiles_ref),
    )
    copies = [pltpu.make_async_copy(source, target, sems.at[k]) for k, (source, target) in enumerate(pairs)]
    for copy in copies:
        copy.start()
    rows_dev = now_ref.shape[0]
    copies[0].wait()
    both_ref[:rows_dev, :] = now_ref[...].astype(BF16)
    copies[1].wait()
    both_ref[rows_dev:, :] = prev_ref[...].astype(BF16)
    for copy in copies[2:]:
        copy.wait()


def tiles_kernel(n_row, n_col, total_rows, me_ref, rows_ref, cols_ref, count_ref, tiles_ref, basis_ref, coupling_ref, *refs):
    half = n_row // 2
    mirror_refs, near_refs, (far_ref, own_ref, total_ref, early_ref) = refs[: half - 1], refs[half - 1 : -4], refs[-4:]
    slots, size, _ = tiles_ref.shape
    width = total_ref.shape[1]
    rows_dev = total_ref.shape[0] // n_row
    piece = early_ref.shape[0] // (n_row * n_col)
    my_row, my_col = me_ref[0], me_ref[1]
    total_ref[...] = jnp.zeros_like(total_ref)
    grams = jnp.zeros((width, 2 * width), F32)
    for slab in range(n_col):
        now = basis_ref[2 * slab * rows_dev : (2 * slab + 1) * rows_dev, :]
        prev = basis_ref[(2 * slab + 1) * rows_dev : (2 * slab + 2) * rows_dev, :]
        grams += lax.dot_general(now, jnp.concatenate([now, prev], axis=1), TN, preferred_element_type=F32)
    square, cross = grams[:, :width], grams[:, width:]
    rows = lax.broadcasted_iota(jnp.int32, square.shape, 0)
    cols = lax.broadcasted_iota(jnp.int32, square.shape, 1)
    if early_ref.shape[0] > 2 * width:
        early_ref[...] = jnp.zeros_like(early_ref)
    early_ref[:width, :] = square - jnp.where(rows == cols, total_rows / n_row, 0.0)
    early_ref[width : 2 * width, :] = dot3(cross, upper_of(coupling_ref[...]), NT)
    used = count_ref[...]
    per_slab = rows_dev // size
    for slot in range(slots):
        col = cols_ref[0, 0, slot]
        start = pl.multiple_of((2 * per_slab * (col // per_slab) + lax.rem(col, per_slab)) * size, size)
        value = jnp.dot(tiles_ref[slot], basis_ref[pl.ds(start, size), :], preferred_element_type=F32)
        value = value * (slot < used).astype(F32)
        place = pl.ds(pl.multiple_of(rows_ref[0, 0, slot] * size, size), size)
        total_ref[place, :] += value

    def parts_of(row):
        slab = total_ref[pl.ds(pl.multiple_of(row * rows_dev, rows_dev), rows_dev), :]
        return slab, early_ref[pl.ds(pl.multiple_of((row * n_col + my_col) * piece, piece), piece), :]

    for step, mirror_ref, near_ref in zip(distances(half), mirror_refs, near_refs):
        write_block(mirror_ref, *parts_of(my_row ^ (step + half)))
        write_block(near_ref, *parts_of(my_row ^ step))
    for row, ref in ((my_row ^ half, far_ref), (my_row, own_ref)):
        ref[:rows_dev, :], ref[rows_dev:, :] = parts_of(row)


def write_block(ref, slab, early):
    rows_dev = slab.shape[0]
    ref[:rows_dev, :] = slab.astype(BF16)
    ref[rows_dev:, :] = early.astype(BF16)


def add_blocks(own_ref, block_refs, rows_dev):
    slab, early = own_ref[:rows_dev, :], own_ref[rows_dev:, :]
    for ref in block_refs:
        slab = slab + ref[:rows_dev, :].astype(F32)
        early = early + ref[rows_dev:, :].astype(F32)
    return slab, early


def mirror_kernel(rows_dev, own_ref, *refs):
    block_refs, out_ref = refs[:-1], refs[-1]
    write_block(out_ref, *add_blocks(own_ref, block_refs, rows_dev))


def shift_kernel(prev_ref, coupling_ref, shift_ref):
    shift_ref[...] = dot3(prev_ref[...], upper_of(coupling_ref[...]), NT)


def grams_kernel(now_ref, shift_ref, own_ref, *refs):
    block_refs, (shifted_ref, grams_ref, early_ref) = refs[:-3], refs[-3:]
    rows_dev, width = now_ref.shape
    product, early_ref[...] = add_blocks(own_ref, block_refs, rows_dev)
    shifted = product - shift_ref[...]
    shifted_ref[...] = shifted
    if grams_ref.shape[0] > 2 * width:
        grams_ref[...] = jnp.zeros_like(grams_ref)
    grams_ref[:width, :] = dot3(now_ref[...], product, TN)
    grams_ref[width : 2 * width, :] = dot3(shifted, shifted, TN)


def spread_kernel(parts_ref, early_ref, out_ref):
    total = parts_ref[0]
    for part in range(1, parts_ref.shape[0]):
        total = total + parts_ref[part]
    value = jnp.concatenate([high_and_low(total), early_ref[...].astype(BF16)], axis=0)
    for part in range(out_ref.shape[0]):
        out_ref[part] = value


def eliminate(gram):
    width = gram.shape[0]
    tall, block, per_group = 8, 16, 2
    shape = (tall, width)
    lanes = lax.broadcasted_iota(jnp.int32, shape, 1)
    subs = lax.broadcasted_iota(jnp.int32, shape, 0)

    def cut(strip):
        return [strip[r : r + tall, :] for r in range(0, block, tall)]

    def column(parts, k):
        return [jnp.broadcast_to(part[:, k : k + 1], shape) for part in parts]

    def row(parts, k):
        part, k = parts[k // tall], k % tall
        return jnp.broadcast_to(part[k : k + 1, :], shape)

    strips = [gram[r : r + block, :] for r in range(0, width, block)]
    finished = []
    for begin in range(0, len(strips), per_group):
        group = [cut(strip) for strip in strips[:per_group]]
        for at in range(per_group):
            first = (begin + at) * block
            panel = group[at]
            columns = [column(panel, first + j) for j in range(block)]
            kept = list(panel)
            for j in range(0, block, 2):
                mine = j // tall
                here, there = subs == j % tall, subs == j % tall + 1
                both = here | there
                lane, next_lane = lanes == first + j, lanes == first + j + 1
                left, right = columns[j], columns[j + 1]
                a, b, c = row(left, j), row(right, j), row(right, j + 1)
                scale = 1.0 / (a * c - b * b)
                by_top = [x * c - y * b for x, y in zip(left, right)]
                by_bottom = [y * a - x * b for x, y in zip(left, right)]
                by_top[mine] = jnp.where(here, -c, jnp.where(there, b, by_top[mine]))
                by_bottom[mine] = jnp.where(here, b, jnp.where(there, -a, by_bottom[mine]))

                def update(parts, up, down):
                    rest = [jnp.where(both, 0.0, part) if k == mine else part for k, part in enumerate(parts)]
                    return [x - (t * up + u * down) * scale for x, t, u in zip(rest, by_top, by_bottom)]

                top, bottom = row(panel, j), row(panel, j + 1)
                ratio = b / a
                second = jnp.where(lane, -ratio, bottom - ratio * top)
                kept[mine] = jnp.where(here, top, jnp.where(there, second, kept[mine]))
                pair = lane | next_lane
                top = jnp.where(lane, 1.0, jnp.where(next_lane, 0.0, top))
                bottom = jnp.where(lane, 0.0, jnp.where(next_lane, 1.0, bottom))
                panel = update([jnp.where(pair, 0.0, part) for part in panel], top, bottom)
                for m in range(j + 2, block):
                    columns[m] = update(columns[m], row(columns[m], j), row(columns[m], j + 1))
            finished += kept
            group[at] = panel
            rows = [row(panel, m) for m in range(block)]
            inside = (lanes >= first) & (lanes < first + block)
            for s in range(per_group):
                if s != at:
                    factors = [column(group[s], first + m) for m in range(block)]
                    for k in range(len(group[s])):
                        terms = [factor[k] * value for factor, value in zip(factors, rows)]
                        while len(terms) > 1:
                            terms = [x + y for x, y in zip(terms[::2], terms[1::2])]
                        group[s][k] = jnp.where(inside, 0.0, group[s][k]) - terms[0]
        group = [jnp.concatenate(parts, axis=0) for parts in group]
        strips = strips[per_group:]
        if strips:
            first, last = begin * block, (begin + per_group) * block
            below = jnp.concatenate(strips, axis=0)
            solved = [jnp.zeros((first, width), F32)] if first else []
            solved = jnp.concatenate(solved + group + [jnp.zeros((width - last, width), F32)], axis=0)
            cols = lax.broadcasted_iota(jnp.int32, below.shape, 1)
            below = jnp.where((cols >= first) & (cols < last), 0.0, below) - dot3(below, solved)
            strips = [below[r : r + block, :] for r in range(0, below.shape[0], block)]
    return jnp.concatenate(finished, axis=0)


def final_kernel(total_rows, pieces_ref, now_ref, shifted_ref, basis_ref, projection_ref, rfactor_ref):
    width = now_ref.shape[1]
    piece = pieces_ref.shape[1] // 3
    pieces = pieces_ref[...]
    late = sum_high_and_low(pieces[:, : 2 * piece, :]).reshape(-1, width)
    early = pieces[:, 2 * piece :, :].astype(F32).reshape(-1, width)
    now_product, square = late[:width], late[width : 2 * width]
    now_square, shift = early[:width], early[width : 2 * width]
    projection = now_product * total_rows**-0.5
    projection_ref[...] = projection
    scaled = now_product * (1.0 / total_rows)
    half = shift - 0.5 * now_product + 0.5 * dot3(now_square, scaled)
    mixed = dot3(scaled, half, TN)
    gram = square + mixed + mixed.T
    reduced = eliminate(gram * (1.0 / total_rows))
    rows = lax.broadcasted_iota(jnp.int32, reduced.shape, 0)
    cols = lax.broadcasted_iota(jnp.int32, reduced.shape, 1)
    diagonal = jnp.sum(jnp.where(rows == cols, reduced, 0.0), axis=1, keepdims=True)
    root = lax.rsqrt(diagonal)
    rfactor_ref[...] = jnp.where(rows <= cols, reduced, 0.0) * root
    inverse = jnp.where(rows > cols, reduced, jnp.where(rows == cols, 1.0, 0.0)) * root
    residual = shifted_ref[...] - dot3(now_ref[...], scaled)
    basis_ref[...] = dot3(residual, inverse, NT)


def exchange(blocks, axis, steps):
    n = lax.axis_size(axis)
    assert n & (n - 1) == 0
    return [lax.ppermute(block, axis, [(i, i ^ step) for i in range(n)]) for step, block in zip(steps, blocks)]


def on_device(basis_now, basis_prev, coupling, tiles, tile_rows, tile_cols, tile_counts):
    rows_dev, width = basis_now.shape
    n_row, n_col = lax.axis_size("row"), lax.axis_size("col")
    devices = n_row * n_col
    tile_block = tiles[0, 0]
    total_rows = float(rows_dev * devices)
    piece = -(-2 * width // (8 * devices)) * 8
    smem = pl.BlockSpec(memory_space=pltpu.SMEM)
    vmem = pl.BlockSpec(memory_space=pltpu.VMEM)
    params = pltpu.CompilerParams(vmem_limit_bytes=48 * 1024 * 1024)

    in_hbm = [pltpu.with_memory_space_constraint(x, pltpu.HBM) for x in (basis_now, basis_prev, tile_rows, tile_cols, tile_block)]
    both, rows, cols, tile_block = pl.pallas_call(
        prepare_kernel,
        out_shape=(
            jax.ShapeDtypeStruct((2 * rows_dev, width), BF16),
            jax.ShapeDtypeStruct(tile_rows.shape, tile_rows.dtype),
            jax.ShapeDtypeStruct(tile_cols.shape, tile_cols.dtype),
            jax.ShapeDtypeStruct(tile_block.shape, tile_block.dtype),
        ),
        in_specs=[pl.BlockSpec(memory_space=pltpu.HBM)] * 5,
        out_specs=(vmem, vmem, vmem, vmem),
        scratch_shapes=[
            pltpu.VMEM(basis_now.shape, F32),
            pltpu.VMEM(basis_prev.shape, F32),
            pltpu.SemaphoreType.DMA((5,)),
        ],
        compiler_params=params,
        name="prepare",
    )(*in_hbm)
    gathered = lax.all_gather(both, "col", axis=0, tiled=True)
    me = jnp.stack([lax.axis_index("row"), lax.axis_index("col")])
    half = n_row // 2
    block = jax.ShapeDtypeStruct((rows_dev + piece, width), BF16)
    sums = jax.ShapeDtypeStruct((rows_dev + piece, width), F32)
    *blocks, far, own = pl.pallas_call(
        functools.partial(tiles_kernel, n_row, n_col, total_rows),
        out_shape=[block] * (2 * half - 2) + [sums] * 2,
        in_specs=[smem] * 3 + [vmem] * 4,
        out_specs=[vmem] * (2 * half),
        scratch_shapes=[
            pltpu.VMEM((n_row * rows_dev, width), F32),
            pltpu.VMEM((devices * piece, width), F32),
        ],
        compiler_params=params,
        name="tile_products",
    )(me, rows, cols, tile_counts, tile_block, gathered, coupling)
    steps = distances(half)
    mirrors = exchange(blocks[: half - 1], "row", steps)
    near = exchange(blocks[half - 1 : -1], "row", steps[:-1])
    mirror = pl.pallas_call(
        functools.partial(mirror_kernel, rows_dev),
        out_shape=block,
        in_specs=[vmem] * half,
        out_specs=vmem,
        compiler_params=params,
        name="mirror_sum",
    )(far, *mirrors)
    mirror, last = lax.optimization_barrier((mirror, blocks[-1]))
    across = exchange([mirror], "row", [half])
    near += exchange([last], "row", steps[-1:])

    shift = pl.pallas_call(
        shift_kernel,
        out_shape=jax.ShapeDtypeStruct((rows_dev, width), F32),
        in_specs=[vmem] * 2,
        out_specs=vmem,
        compiler_params=params,
        cost_estimate=pl.CostEstimate(flops=12 * rows_dev * width * width, bytes_accessed=12 * rows_dev * width, transcendentals=0),
        name="shift_by_previous",
    )(basis_prev, coupling)
    shifted, grams, early = pl.pallas_call(
        grams_kernel,
        out_shape=(
            jax.ShapeDtypeStruct((rows_dev, width), F32),
            jax.ShapeDtypeStruct((devices * piece, width), F32),
            jax.ShapeDtypeStruct((piece, width), F32),
        ),
        in_specs=[vmem] * (3 + half),
        out_specs=(vmem, vmem, vmem),
        compiler_params=params,
        name="local_grams",
    )(basis_now, shift, own, *near[:-1], *across, near[-1])
    everyone = ("row", "col")
    pieces = lax.all_to_all(grams.reshape(devices, piece, width), everyone, split_axis=0, concat_axis=0, tiled=True)
    copies = pl.pallas_call(
        spread_kernel,
        out_shape=jax.ShapeDtypeStruct((devices, 3 * piece, width), BF16),
        in_specs=[vmem, vmem],
        out_specs=vmem,
        compiler_params=params,
        name="sum_and_spread",
    )(pieces, early)
    gathered_sums = lax.all_to_all(copies, everyone, split_axis=0, concat_axis=0, tiled=True)
    return pl.pallas_call(
        functools.partial(final_kernel, total_rows),
        out_shape=(
            jax.ShapeDtypeStruct((rows_dev, width), F32),
            jax.ShapeDtypeStruct((width, width), F32),
            jax.ShapeDtypeStruct((width, width), F32),
        ),
        in_specs=[vmem] * 3,
        out_specs=(vmem, vmem, vmem),
        compiler_params=params,
        name="factor_and_basis",
    )(gathered_sums, basis_now, shifted)


def solution(mesh):
    placed = (
        P(("row", "col"), None),
        P(("row", "col"), None),
        P(),
        P("row", "col", None, None, None),
        P("row", "col", None),
        P("row", "col", None),
        P("row", "col"),
    )
    return jax.shard_map(
        on_device,
        mesh=mesh,
        in_specs=placed,
        out_specs=(P(("row", "col"), None), P(), P()),
        check_vma=False,
    )
```

```python
import functools

import jax
import jax.numpy as jnp
from jax import lax
from jax.experimental import pallas as pl
from jax.experimental.pallas import tpu as pltpu
from jax.sharding import PartitionSpec as P

F32 = jnp.float32
BF16 = jnp.bfloat16
NN, TN, NT = [(((x,), (y,)), ((), ())) for x, y in ((1, 0), (0, 0), (1, 1))]


def split(x):
    high = x.astype(BF16)
    return high, (x - high.astype(F32)).astype(BF16)


def dot3(a, b, dims=NN):
    (a_high, a_low), (b_high, b_low) = split(a), split(b)

    def one(x, y):
        return lax.dot_general(x, y, dims, preferred_element_type=F32)

    return one(a_high, b_low) + one(a_low, b_high) + one(a_high, b_high)


def upper_of(x):
    rows = lax.broadcasted_iota(jnp.int32, x.shape, 0)
    cols = lax.broadcasted_iota(jnp.int32, x.shape, 1)
    return jnp.where(rows <= cols, x, 0.0)


def distances(n):
    return [1, *range(n - 1, 1, -1)]


def high_and_low(value):
    high = value.astype(BF16)
    low = (value - high.astype(F32)).astype(BF16)
    return jnp.concatenate([high, low], axis=0)


def sum_high_and_low(value):
    half = value.shape[-2] // 2
    value = value.astype(F32)
    return value[..., :half, :] + value[..., half:, :]


def prepare_kernel(now_hbm, prev_hbm, rows_hbm, cols_hbm, tiles_hbm, both_ref, rows_ref, cols_ref, tiles_ref, now_ref, prev_ref, sems):
    pairs = (
        (now_hbm, now_ref),
        (prev_hbm, prev_ref),
        (rows_hbm, rows_ref),
        (cols_hbm, cols_ref),
        (tiles_hbm, tiles_ref),
    )
    copies = [pltpu.make_async_copy(source, target, sems.at[k]) for k, (source, target) in enumerate(pairs)]
    for copy in copies:
        copy.start()
    rows_dev = now_ref.shape[0]
    copies[0].wait()
    both_ref[:rows_dev, :] = now_ref[...].astype(BF16)
    copies[1].wait()
    both_ref[rows_dev:, :] = prev_ref[...].astype(BF16)
    for copy in copies[2:]:
        copy.wait()


def tiles_kernel(n_row, n_col, total_rows, me_ref, rows_ref, cols_ref, count_ref, tiles_ref, basis_ref, coupling_ref, *refs):
    half = n_row // 2
    mirror_refs, near_refs, (far_ref, own_ref, total_ref, early_ref) = refs[: half - 1], refs[half - 1 : -4], refs[-4:]
    slots, size, _ = tiles_ref.shape
    width = total_ref.shape[1]
    rows_dev = total_ref.shape[0] // n_row
    piece = early_ref.shape[0] // (n_row * n_col)
    my_row, my_col = me_ref[0], me_ref[1]
    total_ref[...] = jnp.zeros_like(total_ref)
    grams = jnp.zeros((width, 2 * width), F32)
    for slab in range(n_col):
        now = basis_ref[2 * slab * rows_dev : (2 * slab + 1) * rows_dev, :]
        prev = basis_ref[(2 * slab + 1) * rows_dev : (2 * slab + 2) * rows_dev, :]
        grams += lax.dot_general(now, jnp.concatenate([now, prev], axis=1), TN, preferred_element_type=F32)
    square, cross = grams[:, :width], grams[:, width:]
    rows = lax.broadcasted_iota(jnp.int32, square.shape, 0)
    cols = lax.broadcasted_iota(jnp.int32, square.shape, 1)
    if early_ref.shape[0] > 2 * width:
        early_ref[...] = jnp.zeros_like(early_ref)
    early_ref[:width, :] = square - jnp.where(rows == cols, total_rows / n_row, 0.0)
    early_ref[width : 2 * width, :] = dot3(cross, upper_of(coupling_ref[...]), NT)
    used = count_ref[...]
    per_slab = rows_dev // size
    for slot in range(slots):
        col = cols_ref[0, 0, slot]
        start = pl.multiple_of((2 * per_slab * (col // per_slab) + lax.rem(col, per_slab)) * size, size)
        value = jnp.dot(tiles_ref[slot], basis_ref[pl.ds(start, size), :], preferred_element_type=F32)
        value = value * (slot < used).astype(F32)
        place = pl.ds(pl.multiple_of(rows_ref[0, 0, slot] * size, size), size)
        total_ref[place, :] += value

    def parts_of(row):
        slab = total_ref[pl.ds(pl.multiple_of(row * rows_dev, rows_dev), rows_dev), :]
        return slab, early_ref[pl.ds(pl.multiple_of((row * n_col + my_col) * piece, piece), piece), :]

    for step, mirror_ref, near_ref in zip(distances(half), mirror_refs, near_refs):
        write_block(mirror_ref, *parts_of(my_row ^ (step + half)))
        write_block(near_ref, *parts_of(my_row ^ step))
    for row, ref in ((my_row ^ half, far_ref), (my_row, own_ref)):
        ref[:rows_dev, :], ref[rows_dev:, :] = parts_of(row)


def write_block(ref, slab, early):
    rows_dev = slab.shape[0]
    ref[:rows_dev, :] = slab.astype(BF16)
    ref[rows_dev:, :] = early.astype(BF16)


def add_blocks(own_ref, block_refs, rows_dev):
    slab, early = own_ref[:rows_dev, :], own_ref[rows_dev:, :]
    for ref in block_refs:
        slab = slab + ref[:rows_dev, :].astype(F32)
        early = early + ref[rows_dev:, :].astype(F32)
    return slab, early


def mirror_kernel(rows_dev, own_ref, *refs):
    block_refs, out_ref = refs[:-1], refs[-1]
    write_block(out_ref, *add_blocks(own_ref, block_refs, rows_dev))


def shift_kernel(prev_ref, coupling_ref, shift_ref):
    shift_ref[...] = dot3(prev_ref[...], upper_of(coupling_ref[...]), NT)


def grams_kernel(now_ref, shift_ref, own_ref, *refs):
    block_refs, (shifted_ref, grams_ref, early_ref) = refs[:-3], refs[-3:]
    rows_dev, width = now_ref.shape
    product, early_ref[...] = add_blocks(own_ref, block_refs, rows_dev)
    shifted = product - shift_ref[...]
    shifted_ref[...] = shifted
    if grams_ref.shape[0] > 2 * width:
        grams_ref[...] = jnp.zeros_like(grams_ref)
    grams_ref[:width, :] = dot3(now_ref[...], product, TN)
    grams_ref[width : 2 * width, :] = dot3(shifted, shifted, TN)


def spread_kernel(parts_ref, early_ref, out_ref):
    total = parts_ref[0]
    for part in range(1, parts_ref.shape[0]):
        total = total + parts_ref[part]
    value = jnp.concatenate([high_and_low(total), early_ref[...].astype(BF16)], axis=0)
    for part in range(out_ref.shape[0]):
        out_ref[part] = value


def eliminate(gram):
    width = gram.shape[0]
    tall, block = 8, 16
    shape = (tall, width)
    lanes = lax.broadcasted_iota(jnp.int32, shape, 1)
    subs = lax.broadcasted_iota(jnp.int32, shape, 0)

    def cut(strip):
        return [strip[r : r + tall, :] for r in range(0, block, tall)]

    def column(parts, k):
        return [jnp.broadcast_to(part[:, k : k + 1], shape) for part in parts]

    def row(parts, k):
        part, k = parts[k // tall], k % tall
        return jnp.broadcast_to(part[k : k + 1, :], shape)

    strips = [cut(gram[r : r + block, :]) for r in range(0, width, block)]
    finished = []
    for first in range(0, width, block):
        panel, *strips = strips
        columns = [column(panel, first + j) for j in range(block)]
        kept = list(panel)
        for j in range(0, block, 2):
            mine = j // tall
            here, there = subs == j % tall, subs == j % tall + 1
            both = here | there
            lane, next_lane = lanes == first + j, lanes == first + j + 1
            left, right = columns[j], columns[j + 1]
            a, b, c = row(left, j), row(right, j), row(right, j + 1)
            scale = 1.0 / (a * c - b * b)
            by_top = [x * c - y * b for x, y in zip(left, right)]
            by_bottom = [y * a - x * b for x, y in zip(left, right)]
            by_top[mine] = jnp.where(here, -c, jnp.where(there, b, by_top[mine]))
            by_bottom[mine] = jnp.where(here, b, jnp.where(there, -a, by_bottom[mine]))

            def update(parts, up, down):
                rest = [jnp.where(both, 0.0, part) if k == mine else part for k, part in enumerate(parts)]
                return [x - (t * up + u * down) * scale for x, t, u in zip(rest, by_top, by_bottom)]

            top, bottom = row(panel, j), row(panel, j + 1)
            ratio = b / a
            second = jnp.where(lane, -ratio, bottom - ratio * top)
            kept[mine] = jnp.where(here, top, jnp.where(there, second, kept[mine]))
            pair = lane | next_lane
            top = jnp.where(lane, 1.0, jnp.where(next_lane, 0.0, top))
            bottom = jnp.where(lane, 0.0, jnp.where(next_lane, 1.0, bottom))
            panel = update([jnp.where(pair, 0.0, part) for part in panel], top, bottom)
            for m in range(j + 2, block):
                columns[m] = update(columns[m], row(columns[m], j), row(columns[m], j + 1))
        finished += kept
        if strips:
            rows = [row(panel, m) for m in range(block)]
            inside = (lanes >= first) & (lanes < first + block)
            factors = [column(strips[0], first + m) for m in range(block)]
            for k in range(len(panel)):
                terms = [factor[k] * value for factor, value in zip(factors, rows)]
                while len(terms) > 1:
                    terms = [x + y for x, y in zip(terms[::2], terms[1::2])]
                strips[0][k] = jnp.where(inside, 0.0, strips[0][k]) - terms[0]
        if len(strips) > 1:
            below = jnp.concatenate([part for strip in strips[1:] for part in strip], axis=0)
            solved = [jnp.zeros((first, width), F32)] if first else []
            solved = jnp.concatenate(solved + panel + [jnp.zeros((width - first - block, width), F32)], axis=0)
            cols = lax.broadcasted_iota(jnp.int32, below.shape, 1)
            below = jnp.where((cols >= first) & (cols < first + block), 0.0, below) - dot3(below, solved)
            strips[1:] = [cut(below[r : r + block, :]) for r in range(0, below.shape[0], block)]
    return jnp.concatenate(finished, axis=0)


def final_kernel(total_rows, pieces_ref, now_ref, shifted_ref, basis_ref, projection_ref, rfactor_ref):
    width = now_ref.shape[1]
    piece = pieces_ref.shape[1] // 3
    pieces = pieces_ref[...]
    late = sum_high_and_low(pieces[:, : 2 * piece, :]).reshape(-1, width)
    early = pieces[:, 2 * piece :, :].astype(F32).reshape(-1, width)
    now_product, square = late[:width], late[width : 2 * width]
    now_square, shift = early[:width], early[width : 2 * width]
    projection = now_product * total_rows**-0.5
    projection_ref[...] = projection
    scaled = now_product * (1.0 / total_rows)
    half = shift - 0.5 * now_product + 0.5 * dot3(now_square, scaled)
    mixed = dot3(scaled, half, TN)
    gram = square + mixed + mixed.T
    reduced = eliminate(gram * (1.0 / total_rows))
    rows = lax.broadcasted_iota(jnp.int32, reduced.shape, 0)
    cols = lax.broadcasted_iota(jnp.int32, reduced.shape, 1)
    diagonal = jnp.sum(jnp.where(rows == cols, reduced, 0.0), axis=1, keepdims=True)
    root = lax.rsqrt(diagonal)
    rfactor_ref[...] = jnp.where(rows <= cols, reduced, 0.0) * root
    inverse = jnp.where(rows > cols, reduced, jnp.where(rows == cols, 1.0, 0.0)) * root
    residual = shifted_ref[...] - dot3(now_ref[...], scaled)
    basis_ref[...] = dot3(residual, inverse, NT)


def exchange(blocks, axis, steps):
    n = lax.axis_size(axis)
    assert n & (n - 1) == 0
    return [lax.ppermute(block, axis, [(i, i ^ step) for i in range(n)]) for step, block in zip(steps, blocks)]


def on_device(basis_now, basis_prev, coupling, tiles, tile_rows, tile_cols, tile_counts):
    rows_dev, width = basis_now.shape
    n_row, n_col = lax.axis_size("row"), lax.axis_size("col")
    devices = n_row * n_col
    tile_block = tiles[0, 0]
    total_rows = float(rows_dev * devices)
    piece = -(-2 * width // (8 * devices)) * 8
    smem = pl.BlockSpec(memory_space=pltpu.SMEM)
    vmem = pl.BlockSpec(memory_space=pltpu.VMEM)
    params = pltpu.CompilerParams(vmem_limit_bytes=48 * 1024 * 1024)

    in_hbm = [pltpu.with_memory_space_constraint(x, pltpu.HBM) for x in (basis_now, basis_prev, tile_rows, tile_cols, tile_block)]
    both, rows, cols, tile_block = pl.pallas_call(
        prepare_kernel,
        out_shape=(
            jax.ShapeDtypeStruct((2 * rows_dev, width), BF16),
            jax.ShapeDtypeStruct(tile_rows.shape, tile_rows.dtype),
            jax.ShapeDtypeStruct(tile_cols.shape, tile_cols.dtype),
            jax.ShapeDtypeStruct(tile_block.shape, tile_block.dtype),
        ),
        in_specs=[pl.BlockSpec(memory_space=pltpu.HBM)] * 5,
        out_specs=(vmem, vmem, vmem, vmem),
        scratch_shapes=[
            pltpu.VMEM(basis_now.shape, F32),
            pltpu.VMEM(basis_prev.shape, F32),
            pltpu.SemaphoreType.DMA((5,)),
        ],
        compiler_params=params,
        name="prepare",
    )(*in_hbm)
    gathered = lax.all_gather(both, "col", axis=0, tiled=True)
    me = jnp.stack([lax.axis_index("row"), lax.axis_index("col")])
    half = n_row // 2
    block = jax.ShapeDtypeStruct((rows_dev + piece, width), BF16)
    sums = jax.ShapeDtypeStruct((rows_dev + piece, width), F32)
    *blocks, far, own = pl.pallas_call(
        functools.partial(tiles_kernel, n_row, n_col, total_rows),
        out_shape=[block] * (2 * half - 2) + [sums] * 2,
        in_specs=[smem] * 3 + [vmem] * 4,
        out_specs=[vmem] * (2 * half),
        scratch_shapes=[
            pltpu.VMEM((n_row * rows_dev, width), F32),
            pltpu.VMEM((devices * piece, width), F32),
        ],
        compiler_params=params,
        name="tile_products",
    )(me, rows, cols, tile_counts, tile_block, gathered, coupling)
    steps = distances(half)
    mirrors = exchange(blocks[: half - 1], "row", steps)
    near = exchange(blocks[half - 1 : -1], "row", steps[:-1])
    mirror = pl.pallas_call(
        functools.partial(mirror_kernel, rows_dev),
        out_shape=block,
        in_specs=[vmem] * half,
        out_specs=vmem,
        compiler_params=params,
        name="mirror_sum",
    )(far, *mirrors)
    mirror, last = lax.optimization_barrier((mirror, blocks[-1]))
    across = exchange([mirror], "row", [half])
    near += exchange([last], "row", steps[-1:])

    shift = pl.pallas_call(
        shift_kernel,
        out_shape=jax.ShapeDtypeStruct((rows_dev, width), F32),
        in_specs=[vmem] * 2,
        out_specs=vmem,
        compiler_params=params,
        cost_estimate=pl.CostEstimate(flops=12 * rows_dev * width * width, bytes_accessed=12 * rows_dev * width, transcendentals=0),
        name="shift_by_previous",
    )(basis_prev, coupling)
    shifted, grams, early = pl.pallas_call(
        grams_kernel,
        out_shape=(
            jax.ShapeDtypeStruct((rows_dev, width), F32),
            jax.ShapeDtypeStruct((devices * piece, width), F32),
            jax.ShapeDtypeStruct((piece, width), F32),
        ),
        in_specs=[vmem] * (3 + half),
        out_specs=(vmem, vmem, vmem),
        compiler_params=params,
        name="local_grams",
    )(basis_now, shift, own, *near[:-1], *across, near[-1])
    everyone = ("row", "col")
    pieces = lax.all_to_all(grams.reshape(devices, piece, width), everyone, split_axis=0, concat_axis=0, tiled=True)
    copies = pl.pallas_call(
        spread_kernel,
        out_shape=jax.ShapeDtypeStruct((devices, 3 * piece, width), BF16),
        in_specs=[vmem, vmem],
        out_specs=vmem,
        compiler_params=params,
        name="sum_and_spread",
    )(pieces, early)
    gathered_sums = lax.all_to_all(copies, everyone, split_axis=0, concat_axis=0, tiled=True)
    return pl.pallas_call(
        functools.partial(final_kernel, total_rows),
        out_shape=(
            jax.ShapeDtypeStruct((rows_dev, width), F32),
            jax.ShapeDtypeStruct((width, width), F32),
            jax.ShapeDtypeStruct((width, width), F32),
        ),
        in_specs=[vmem] * 3,
        out_specs=(vmem, vmem, vmem),
        compiler_params=params,
        name="factor_and_basis",
    )(gathered_sums, basis_now, shifted)


def solution(mesh):
    placed = (
        P(("row", "col"), None),
        P(("row", "col"), None),
        P(),
        P("row", "col", None, None, None),
        P("row", "col", None),
        P("row", "col", None),
        P("row", "col"),
    )
    return jax.shard_map(
        on_device,
        mesh=mesh,
        in_specs=placed,
        out_specs=(P(("row", "col"), None), P(), P()),
        check_vma=False,
    )
```

```python
import functools

import jax
import jax.numpy as jnp
from jax import lax
from jax.experimental import pallas as pl
from jax.experimental.pallas import tpu as pltpu
from jax.sharding import PartitionSpec as P

F32 = jnp.float32
BF16 = jnp.bfloat16
NN, TN, NT = [(((x,), (y,)), ((), ())) for x, y in ((1, 0), (0, 0), (1, 1))]


def split(x):
    high = x.astype(BF16)
    return high, (x - high.astype(F32)).astype(BF16)


def dot3(a, b, dims=NN):
    (a_high, a_low), (b_high, b_low) = split(a), split(b)

    def one(x, y):
        return lax.dot_general(x, y, dims, preferred_element_type=F32)

    return one(a_high, b_low) + one(a_low, b_high) + one(a_high, b_high)


def upper_of(x):
    rows = lax.broadcasted_iota(jnp.int32, x.shape, 0)
    cols = lax.broadcasted_iota(jnp.int32, x.shape, 1)
    return jnp.where(rows <= cols, x, 0.0)


def distances(n):
    return [n - 1, *range(1, n - 1)]


def high_and_low(value):
    high = value.astype(BF16)
    low = (value - high.astype(F32)).astype(BF16)
    return jnp.concatenate([high, low], axis=0)


def sum_high_and_low(value):
    half = value.shape[-2] // 2
    value = value.astype(F32)
    return value[..., :half, :] + value[..., half:, :]


def prepare_kernel(now_hbm, prev_hbm, rows_hbm, cols_hbm, tiles_hbm, both_ref, rows_ref, cols_ref, tiles_ref, now_ref, prev_ref, sems):
    pairs = (
        (now_hbm, now_ref),
        (prev_hbm, prev_ref),
        (rows_hbm, rows_ref),
        (cols_hbm, cols_ref),
        (tiles_hbm, tiles_ref),
    )
    copies = [pltpu.make_async_copy(source, target, sems.at[k]) for k, (source, target) in enumerate(pairs)]
    for copy in copies:
        copy.start()
    rows_dev = now_ref.shape[0]
    copies[0].wait()
    both_ref[:rows_dev, :] = now_ref[...].astype(BF16)
    copies[1].wait()
    both_ref[rows_dev:, :] = prev_ref[...].astype(BF16)
    for copy in copies[2:]:
        copy.wait()


def tiles_kernel(n_row, n_col, total_rows, me_ref, rows_ref, cols_ref, count_ref, tiles_ref, basis_ref, coupling_ref, *refs):
    half = n_row // 2
    mirror_refs, near_refs, (far_ref, own_ref, total_ref, early_ref) = refs[: half - 1], refs[half - 1 : -4], refs[-4:]
    slots, size, _ = tiles_ref.shape
    width = total_ref.shape[1]
    rows_dev = total_ref.shape[0] // n_row
    piece = early_ref.shape[0] // (n_row * n_col)
    my_row, my_col = me_ref[0], me_ref[1]
    total_ref[...] = jnp.zeros_like(total_ref)
    grams = jnp.zeros((width, 2 * width), F32)
    for slab in range(n_col):
        now = basis_ref[2 * slab * rows_dev : (2 * slab + 1) * rows_dev, :]
        prev = basis_ref[(2 * slab + 1) * rows_dev : (2 * slab + 2) * rows_dev, :]
        grams += lax.dot_general(now, jnp.concatenate([now, prev], axis=1), TN, preferred_element_type=F32)
    square, cross = grams[:, :width], grams[:, width:]
    rows = lax.broadcasted_iota(jnp.int32, square.shape, 0)
    cols = lax.broadcasted_iota(jnp.int32, square.shape, 1)
    if early_ref.shape[0] > 2 * width:
        early_ref[...] = jnp.zeros_like(early_ref)
    early_ref[:width, :] = square - jnp.where(rows == cols, total_rows / n_row, 0.0)
    early_ref[width : 2 * width, :] = dot3(cross, upper_of(coupling_ref[...]), NT)
    used = count_ref[...]
    per_slab = rows_dev // size
    for slot in range(slots):
        col = cols_ref[0, 0, slot]
        start = pl.multiple_of((2 * per_slab * (col // per_slab) + lax.rem(col, per_slab)) * size, size)
        value = jnp.dot(tiles_ref[slot], basis_ref[pl.ds(start, size), :], preferred_element_type=F32)
        value = value * (slot < used).astype(F32)
        place = pl.ds(pl.multiple_of(rows_ref[0, 0, slot] * size, size), size)
        total_ref[place, :] += value

    def parts_of(row):
        slab = total_ref[pl.ds(pl.multiple_of(row * rows_dev, rows_dev), rows_dev), :]
        return slab, early_ref[pl.ds(pl.multiple_of((row * n_col + my_col) * piece, piece), piece), :]

    for step, mirror_ref, near_ref in zip(distances(half), mirror_refs, near_refs):
        write_block(mirror_ref, *parts_of(my_row ^ (step + half)))
        write_block(near_ref, *parts_of(my_row ^ step))
    for row, ref in ((my_row ^ half, far_ref), (my_row, own_ref)):
        ref[:rows_dev, :], ref[rows_dev:, :] = parts_of(row)


def write_block(ref, slab, early):
    rows_dev = slab.shape[0]
    ref[:rows_dev, :] = slab.astype(BF16)
    ref[rows_dev:, :] = early.astype(BF16)


def add_blocks(own_ref, block_refs, rows_dev):
    slab, early = own_ref[:rows_dev, :], own_ref[rows_dev:, :]
    for ref in block_refs:
        slab = slab + ref[:rows_dev, :].astype(F32)
        early = early + ref[rows_dev:, :].astype(F32)
    return slab, early


def mirror_kernel(rows_dev, own_ref, *refs):
    block_refs, out_ref = refs[:-1], refs[-1]
    write_block(out_ref, *add_blocks(own_ref, block_refs, rows_dev))


def shift_kernel(prev_ref, coupling_ref, shift_ref):
    shift_ref[...] = dot3(prev_ref[...], upper_of(coupling_ref[...]), NT)


def grams_kernel(now_ref, shift_ref, own_ref, *refs):
    block_refs, (shifted_ref, grams_ref, early_ref) = refs[:-3], refs[-3:]
    rows_dev, width = now_ref.shape
    product, early_ref[...] = add_blocks(own_ref, block_refs, rows_dev)
    shifted = product - shift_ref[...]
    shifted_ref[...] = shifted
    if grams_ref.shape[0] > 2 * width:
        grams_ref[...] = jnp.zeros_like(grams_ref)
    grams_ref[:width, :] = dot3(now_ref[...], product, TN)
    grams_ref[width : 2 * width, :] = dot3(shifted, shifted, TN)


def spread_kernel(parts_ref, early_ref, out_ref):
    total = parts_ref[0]
    for part in range(1, parts_ref.shape[0]):
        total = total + parts_ref[part]
    value = jnp.concatenate([high_and_low(total), early_ref[...].astype(BF16)], axis=0)
    for part in range(out_ref.shape[0]):
        out_ref[part] = value


def eliminate(gram):
    width = gram.shape[0]
    tall, block = 8, 16
    shape = (tall, width)
    lanes = lax.broadcasted_iota(jnp.int32, shape, 1)
    subs = lax.broadcasted_iota(jnp.int32, shape, 0)

    def cut(strip):
        return [strip[r : r + tall, :] for r in range(0, block, tall)]

    def column(parts, k):
        return [jnp.broadcast_to(part[:, k : k + 1], shape) for part in parts]

    def row(parts, k):
        part, k = parts[k // tall], k % tall
        return jnp.broadcast_to(part[k : k + 1, :], shape)

    strips = [cut(gram[r : r + block, :]) for r in range(0, width, block)]
    finished = []
    for first in range(0, width, block):
        panel, *strips = strips
        columns = [column(panel, first + j) for j in range(block)]
        kept = list(panel)
        for j in range(0, block, 2):
            mine = j // tall
            here, there = subs == j % tall, subs == j % tall + 1
            both = here | there
            lane, next_lane = lanes == first + j, lanes == first + j + 1
            left, right = columns[j], columns[j + 1]
            a, b, c = row(left, j), row(right, j), row(right, j + 1)
            scale = 1.0 / (a * c - b * b)
            by_top = [x * c - y * b for x, y in zip(left, right)]
            by_bottom = [y * a - x * b for x, y in zip(left, right)]
            by_top[mine] = jnp.where(here, -c, jnp.where(there, b, by_top[mine]))
            by_bottom[mine] = jnp.where(here, b, jnp.where(there, -a, by_bottom[mine]))

            def update(parts, up, down):
                rest = [jnp.where(both, 0.0, part) if k == mine else part for k, part in enumerate(parts)]
                return [x - (t * up + u * down) * scale for x, t, u in zip(rest, by_top, by_bottom)]

            top, bottom = row(panel, j), row(panel, j + 1)
            ratio = b / a
            second = jnp.where(lane, -ratio, bottom - ratio * top)
            kept[mine] = jnp.where(here, top, jnp.where(there, second, kept[mine]))
            pair = lane | next_lane
            top = jnp.where(lane, 1.0, jnp.where(next_lane, 0.0, top))
            bottom = jnp.where(lane, 0.0, jnp.where(next_lane, 1.0, bottom))
            panel = update([jnp.where(pair, 0.0, part) for part in panel], top, bottom)
            for m in range(j + 2, block):
                columns[m] = update(columns[m], row(columns[m], j), row(columns[m], j + 1))
        finished += kept
        if strips:
            rows = [row(panel, m) for m in range(block)]
            inside = (lanes >= first) & (lanes < first + block)
            factors = [column(strips[0], first + m) for m in range(block)]
            for k in range(len(panel)):
                terms = [factor[k] * value for factor, value in zip(factors, rows)]
                while len(terms) > 1:
                    terms = [x + y for x, y in zip(terms[::2], terms[1::2])]
                strips[0][k] = jnp.where(inside, 0.0, strips[0][k]) - terms[0]
        if len(strips) > 1:
            below = jnp.concatenate([part for strip in strips[1:] for part in strip], axis=0)
            solved = [jnp.zeros((first, width), F32)] if first else []
            solved = jnp.concatenate(solved + panel + [jnp.zeros((width - first - block, width), F32)], axis=0)
            cols = lax.broadcasted_iota(jnp.int32, below.shape, 1)
            below = jnp.where((cols >= first) & (cols < first + block), 0.0, below) - dot3(below, solved)
            strips[1:] = [cut(below[r : r + block, :]) for r in range(0, below.shape[0], block)]
    return jnp.concatenate(finished, axis=0)


def final_kernel(total_rows, pieces_ref, now_ref, shifted_ref, basis_ref, projection_ref, rfactor_ref):
    width = now_ref.shape[1]
    piece = pieces_ref.shape[1] // 3
    pieces = pieces_ref[...]
    late = sum_high_and_low(pieces[:, : 2 * piece, :]).reshape(-1, width)
    early = pieces[:, 2 * piece :, :].reshape(-1, width)
    now_product, square = late[:width], late[width : 2 * width]
    now_square, shift = early[:width], early[width : 2 * width]
    projection = now_product * total_rows**-0.5
    projection_ref[...] = projection
    scaled = now_product * (1.0 / total_rows)
    scaled_high, scaled_low = split(scaled)
    corrected = jnp.dot(now_square, scaled_low, preferred_element_type=F32)
    corrected += jnp.dot(now_square, scaled_high, preferred_element_type=F32)
    half = shift.astype(F32) - 0.5 * now_product + 0.5 * corrected
    mixed = dot3(scaled, half, TN)
    gram = square + mixed + mixed.T
    reduced = eliminate(gram * (1.0 / total_rows))
    rows = lax.broadcasted_iota(jnp.int32, reduced.shape, 0)
    cols = lax.broadcasted_iota(jnp.int32, reduced.shape, 1)
    diagonal = jnp.sum(jnp.where(rows == cols, reduced, 0.0), axis=1, keepdims=True)
    root = lax.rsqrt(diagonal)
    rfactor_ref[...] = jnp.where(rows <= cols, reduced, 0.0) * root
    inverse = jnp.where(rows > cols, reduced, jnp.where(rows == cols, 1.0, 0.0)) * root
    residual = shifted_ref[...] - dot3(now_ref[...], scaled)
    basis_ref[...] = dot3(residual, inverse, NT)


def exchange(blocks, axis, steps):
    n = lax.axis_size(axis)
    assert n & (n - 1) == 0
    return [lax.ppermute(block, axis, [(i, i ^ step) for i in range(n)]) for step, block in zip(steps, blocks)]


def on_device(basis_now, basis_prev, coupling, tiles, tile_rows, tile_cols, tile_counts):
    rows_dev, width = basis_now.shape
    n_row, n_col = lax.axis_size("row"), lax.axis_size("col")
    devices = n_row * n_col
    tile_block = tiles[0, 0]
    total_rows = float(rows_dev * devices)
    piece = -(-2 * width // (8 * devices)) * 8
    smem = pl.BlockSpec(memory_space=pltpu.SMEM)
    vmem = pl.BlockSpec(memory_space=pltpu.VMEM)
    params = pltpu.CompilerParams(vmem_limit_bytes=48 * 1024 * 1024)

    in_hbm = [pltpu.with_memory_space_constraint(x, pltpu.HBM) for x in (basis_now, basis_prev, tile_rows, tile_cols, tile_block)]
    both, rows, cols, tile_block = pl.pallas_call(
        prepare_kernel,
        out_shape=(
            jax.ShapeDtypeStruct((2 * rows_dev, width), BF16),
            jax.ShapeDtypeStruct(tile_rows.shape, tile_rows.dtype),
            jax.ShapeDtypeStruct(tile_cols.shape, tile_cols.dtype),
            jax.ShapeDtypeStruct(tile_block.shape, tile_block.dtype),
        ),
        in_specs=[pl.BlockSpec(memory_space=pltpu.HBM)] * 5,
        out_specs=(vmem, vmem, vmem, vmem),
        scratch_shapes=[
            pltpu.VMEM(basis_now.shape, F32),
            pltpu.VMEM(basis_prev.shape, F32),
            pltpu.SemaphoreType.DMA((5,)),
        ],
        compiler_params=params,
        name="prepare",
    )(*in_hbm)
    gathered = lax.all_gather(both, "col", axis=0, tiled=True)
    me = jnp.stack([lax.axis_index("row"), lax.axis_index("col")])
    half = n_row // 2
    block = jax.ShapeDtypeStruct((rows_dev + piece, width), BF16)
    sums = jax.ShapeDtypeStruct((rows_dev + piece, width), F32)
    *blocks, far, own = pl.pallas_call(
        functools.partial(tiles_kernel, n_row, n_col, total_rows),
        out_shape=[block] * (2 * half - 2) + [sums] * 2,
        in_specs=[smem] * 3 + [vmem] * 4,
        out_specs=[vmem] * (2 * half),
        scratch_shapes=[
            pltpu.VMEM((n_row * rows_dev, width), F32),
            pltpu.VMEM((devices * piece, width), F32),
        ],
        compiler_params=params,
        name="tile_products",
    )(me, rows, cols, tile_counts, tile_block, gathered, coupling)
    steps = distances(half)
    mirrors = exchange(blocks[: half - 1], "row", steps)
    near = exchange(blocks[half - 1 : -1], "row", steps[:-1])
    mirror = pl.pallas_call(
        functools.partial(mirror_kernel, rows_dev),
        out_shape=block,
        in_specs=[vmem] * half,
        out_specs=vmem,
        compiler_params=params,
        name="mirror_sum",
    )(far, *mirrors)
    mirror, last = lax.optimization_barrier((mirror, blocks[-1]))
    across = exchange([mirror], "row", [half])
    near += exchange([last], "row", steps[-1:])

    shift = pl.pallas_call(
        shift_kernel,
        out_shape=jax.ShapeDtypeStruct((rows_dev, width), F32),
        in_specs=[vmem] * 2,
        out_specs=vmem,
        compiler_params=params,
        cost_estimate=pl.CostEstimate(flops=12 * rows_dev * width * width, bytes_accessed=12 * rows_dev * width, transcendentals=0),
        name="shift_by_previous",
    )(basis_prev, coupling)
    shifted, grams, early = pl.pallas_call(
        grams_kernel,
        out_shape=(
            jax.ShapeDtypeStruct((rows_dev, width), F32),
            jax.ShapeDtypeStruct((devices * piece, width), F32),
            jax.ShapeDtypeStruct((piece, width), F32),
        ),
        in_specs=[vmem] * (3 + half),
        out_specs=(vmem, vmem, vmem),
        compiler_params=params,
        name="local_grams",
    )(basis_now, shift, own, *near[:-1], *across, near[-1])
    everyone = ("row", "col")
    pieces = lax.all_to_all(grams.reshape(devices, piece, width), everyone, split_axis=0, concat_axis=0, tiled=True)
    copies = pl.pallas_call(
        spread_kernel,
        out_shape=jax.ShapeDtypeStruct((devices, 3 * piece, width), BF16),
        in_specs=[vmem, vmem],
        out_specs=vmem,
        compiler_params=params,
        name="sum_and_spread",
    )(pieces, early)
    gathered_sums = lax.all_to_all(copies, everyone, split_axis=0, concat_axis=0, tiled=True)
    return pl.pallas_call(
        functools.partial(final_kernel, total_rows),
        out_shape=(
            jax.ShapeDtypeStruct((rows_dev, width), F32),
            jax.ShapeDtypeStruct((width, width), F32),
            jax.ShapeDtypeStruct((width, width), F32),
        ),
        in_specs=[vmem] * 3,
        out_specs=(vmem, vmem, vmem),
        compiler_params=params,
        name="factor_and_basis",
    )(gathered_sums, basis_now, shifted)


def solution(mesh):
    placed = (
        P(("row", "col"), None),
        P(("row", "col"), None),
        P(),
        P("row", "col", None, None, None),
        P("row", "col", None),
        P("row", "col", None),
        P("row", "col"),
    )
    return jax.shard_map(
        on_device,
        mesh=mesh,
        in_specs=placed,
        out_specs=(P(("row", "col"), None), P(), P()),
        check_vma=False,
    )
```

```python
import functools

import jax
import jax.numpy as jnp
from jax import lax
from jax.experimental import pallas as pl
from jax.experimental.pallas import tpu as pltpu
from jax.sharding import PartitionSpec as P

F32 = jnp.float32
BF16 = jnp.bfloat16
NN, TN, NT = [(((x,), (y,)), ((), ())) for x, y in ((1, 0), (0, 0), (1, 1))]


def split(x):
    high = x.astype(BF16)
    return high, (x - high.astype(F32)).astype(BF16)


def dot3(a, b, dims=NN):
    (a_high, a_low), (b_high, b_low) = split(a), split(b)

    def one(x, y):
        return lax.dot_general(x, y, dims, preferred_element_type=F32)

    return one(a_high, b_low) + one(a_low, b_high) + one(a_high, b_high)


def upper_of(x):
    rows = lax.broadcasted_iota(jnp.int32, x.shape, 0)
    cols = lax.broadcasted_iota(jnp.int32, x.shape, 1)
    return jnp.where(rows <= cols, x, 0.0)


def distances(n):
    return [n - 1, *range(1, n - 1)]


def near_distances(n):
    return [*range(2, n), 1]


def high_and_low(value):
    high = value.astype(BF16)
    low = (value - high.astype(F32)).astype(BF16)
    return jnp.concatenate([high, low], axis=0)


def sum_high_and_low(value):
    half = value.shape[-2] // 2
    value = value.astype(F32)
    return value[..., :half, :] + value[..., half:, :]


def prepare_kernel(now_hbm, prev_hbm, rows_hbm, cols_hbm, tiles_hbm, both_ref, rows_ref, cols_ref, tiles_ref, now_ref, prev_ref, sems):
    pairs = (
        (now_hbm, now_ref),
        (prev_hbm, prev_ref),
        (rows_hbm, rows_ref),
        (cols_hbm, cols_ref),
        (tiles_hbm, tiles_ref),
    )
    copies = [pltpu.make_async_copy(source, target, sems.at[k]) for k, (source, target) in enumerate(pairs)]
    for copy in copies:
        copy.start()
    rows_dev = now_ref.shape[0]
    copies[0].wait()
    both_ref[:rows_dev, :] = now_ref[...].astype(BF16)
    copies[1].wait()
    both_ref[rows_dev:, :] = prev_ref[...].astype(BF16)
    for copy in copies[2:]:
        copy.wait()


def tiles_kernel(n_row, n_col, total_rows, me_ref, rows_ref, cols_ref, count_ref, tiles_ref, basis_ref, coupling_ref, *refs):
    half = n_row // 2
    mirror_refs, near_refs, (far_ref, own_ref, total_ref, early_ref) = refs[: half - 1], refs[half - 1 : -4], refs[-4:]
    slots, size, _ = tiles_ref.shape
    width = total_ref.shape[1]
    rows_dev = total_ref.shape[0] // n_row
    piece = early_ref.shape[0] // (n_row * n_col)
    my_row, my_col = me_ref[0], me_ref[1]
    total_ref[...] = jnp.zeros_like(total_ref)
    grams = jnp.zeros((width, 2 * width), F32)
    for slab in range(n_col):
        now = basis_ref[2 * slab * rows_dev : (2 * slab + 1) * rows_dev, :]
        prev = basis_ref[(2 * slab + 1) * rows_dev : (2 * slab + 2) * rows_dev, :]
        grams += lax.dot_general(now, jnp.concatenate([now, prev], axis=1), TN, preferred_element_type=F32)
    square, cross = grams[:, :width], grams[:, width:]
    rows = lax.broadcasted_iota(jnp.int32, square.shape, 0)
    cols = lax.broadcasted_iota(jnp.int32, square.shape, 1)
    if early_ref.shape[0] > 2 * width:
        early_ref[...] = jnp.zeros_like(early_ref)
    early_ref[:width, :] = square - jnp.where(rows == cols, total_rows / n_row, 0.0)
    early_ref[width : 2 * width, :] = dot3(cross, upper_of(coupling_ref[...]), NT)
    used = count_ref[...]
    per_slab = rows_dev // size
    for slot in range(slots):
        col = cols_ref[0, 0, slot]
        start = pl.multiple_of((2 * per_slab * (col // per_slab) + lax.rem(col, per_slab)) * size, size)
        value = jnp.dot(tiles_ref[slot], basis_ref[pl.ds(start, size), :], preferred_element_type=F32)
        value = value * (slot < used).astype(F32)
        place = pl.ds(pl.multiple_of(rows_ref[0, 0, slot] * size, size), size)
        total_ref[place, :] += value

    def parts_of(row):
        slab = total_ref[pl.ds(pl.multiple_of(row * rows_dev, rows_dev), rows_dev), :]
        return slab, early_ref[pl.ds(pl.multiple_of((row * n_col + my_col) * piece, piece), piece), :]

    for step, ref in zip(distances(half), mirror_refs):
        write_block(ref, *parts_of(my_row ^ (step + half)))
    for step, ref in zip(near_distances(half), near_refs):
        write_block(ref, *parts_of(my_row ^ step))
    for row, ref in ((my_row ^ half, far_ref), (my_row, own_ref)):
        ref[:rows_dev, :], ref[rows_dev:, :] = parts_of(row)


def write_block(ref, slab, early):
    rows_dev = slab.shape[0]
    ref[:rows_dev, :] = slab.astype(BF16)
    ref[rows_dev:, :] = early.astype(BF16)


def add_blocks(own_ref, block_refs, rows_dev):
    slab, early = own_ref[:rows_dev, :], own_ref[rows_dev:, :]
    for ref in block_refs:
        slab = slab + ref[:rows_dev, :].astype(F32)
        early = early + ref[rows_dev:, :].astype(F32)
    return slab, early


def mirror_kernel(rows_dev, own_ref, *refs):
    block_refs, out_ref = refs[:-1], refs[-1]
    write_block(out_ref, *add_blocks(own_ref, block_refs, rows_dev))


def shift_kernel(prev_ref, coupling_ref, shift_ref):
    shift_ref[...] = dot3(prev_ref[...], upper_of(coupling_ref[...]), NT)


def grams_kernel(now_ref, shift_ref, own_ref, *refs):
    block_refs, (shifted_ref, grams_ref, early_ref) = refs[:-3], refs[-3:]
    rows_dev, width = now_ref.shape
    product, early_ref[...] = add_blocks(own_ref, block_refs, rows_dev)
    shifted = product - shift_ref[...]
    shifted_ref[...] = shifted
    if grams_ref.shape[0] > 2 * width:
        grams_ref[...] = jnp.zeros_like(grams_ref)
    grams_ref[:width, :] = dot3(now_ref[...], product, TN)
    grams_ref[width : 2 * width, :] = dot3(shifted, shifted, TN)


def spread_kernel(parts_ref, early_ref, out_ref):
    total = parts_ref[0]
    for part in range(1, parts_ref.shape[0]):
        total = total + parts_ref[part]
    value = jnp.concatenate([high_and_low(total), early_ref[...].astype(BF16)], axis=0)
    for part in range(out_ref.shape[0]):
        out_ref[part] = value


def eliminate(gram):
    width = gram.shape[0]
    tall, block = 8, 16
    shape = (tall, width)
    lanes = lax.broadcasted_iota(jnp.int32, shape, 1)
    subs = lax.broadcasted_iota(jnp.int32, shape, 0)

    def cut(strip):
        return [strip[r : r + tall, :] for r in range(0, block, tall)]

    def column(parts, k):
        return [jnp.broadcast_to(part[:, k : k + 1], shape) for part in parts]

    def row(parts, k):
        part, k = parts[k // tall], k % tall
        return jnp.broadcast_to(part[k : k + 1, :], shape)

    strips = [cut(gram[r : r + block, :]) for r in range(0, width, block)]
    finished = []
    for first in range(0, width, block):
        panel, *strips = strips
        columns = [column(panel, first + j) for j in range(block)]
        kept = list(panel)
        for j in range(0, block, 2):
            mine = j // tall
            here, there = subs == j % tall, subs == j % tall + 1
            both = here | there
            lane, next_lane = lanes == first + j, lanes == first + j + 1
            left, right = columns[j], columns[j + 1]
            a, b, c = row(left, j), row(right, j), row(right, j + 1)
            scale = 1.0 / (a * c - b * b)
            by_top = [x * c - y * b for x, y in zip(left, right)]
            by_bottom = [y * a - x * b for x, y in zip(left, right)]
            by_top[mine] = jnp.where(here, -c, jnp.where(there, b, by_top[mine]))
            by_bottom[mine] = jnp.where(here, b, jnp.where(there, -a, by_bottom[mine]))

            def update(parts, up, down):
                rest = [jnp.where(both, 0.0, part) if k == mine else part for k, part in enumerate(parts)]
                return [x - (t * up + u * down) * scale for x, t, u in zip(rest, by_top, by_bottom)]

            top, bottom = row(panel, j), row(panel, j + 1)
            ratio = b / a
            second = jnp.where(lane, -ratio, bottom - ratio * top)
            kept[mine] = jnp.where(here, top, jnp.where(there, second, kept[mine]))
            pair = lane | next_lane
            top = jnp.where(lane, 1.0, jnp.where(next_lane, 0.0, top))
            bottom = jnp.where(lane, 0.0, jnp.where(next_lane, 1.0, bottom))
            panel = update([jnp.where(pair, 0.0, part) for part in panel], top, bottom)
            for m in range(j + 2, block):
                columns[m] = update(columns[m], row(columns[m], j), row(columns[m], j + 1))
        finished += kept
        if strips:
            rows = [row(panel, m) for m in range(block)]
            inside = (lanes >= first) & (lanes < first + block)
            factors = [column(strips[0], first + m) for m in range(block)]
            for k in range(len(panel)):
                terms = [factor[k] * value for factor, value in zip(factors, rows)]
                while len(terms) > 1:
                    terms = [x + y for x, y in zip(terms[::2], terms[1::2])]
                strips[0][k] = jnp.where(inside, 0.0, strips[0][k]) - terms[0]
        if len(strips) > 1:
            below = jnp.concatenate([part for strip in strips[1:] for part in strip], axis=0)
            solved = [jnp.zeros((first, width), F32)] if first else []
            solved = jnp.concatenate(solved + panel + [jnp.zeros((width - first - block, width), F32)], axis=0)
            cols = lax.broadcasted_iota(jnp.int32, below.shape, 1)
            below = jnp.where((cols >= first) & (cols < first + block), 0.0, below) - dot3(below, solved)
            strips[1:] = [cut(below[r : r + block, :]) for r in range(0, below.shape[0], block)]
    return jnp.concatenate(finished, axis=0)


def final_kernel(total_rows, pieces_ref, now_ref, shifted_ref, basis_ref, projection_ref, rfactor_ref):
    width = now_ref.shape[1]
    piece = pieces_ref.shape[1] // 3
    pieces = pieces_ref[...]
    late = sum_high_and_low(pieces[:, : 2 * piece, :]).reshape(-1, width)
    early = pieces[:, 2 * piece :, :].reshape(-1, width)
    now_product, square = late[:width], late[width : 2 * width]
    now_square, shift = early[:width], early[width : 2 * width]
    projection = now_product * total_rows**-0.5
    projection_ref[...] = projection
    scaled = now_product * (1.0 / total_rows)
    scaled_high, scaled_low = split(scaled)
    corrected = jnp.dot(now_square, scaled_low, preferred_element_type=F32)
    corrected += jnp.dot(now_square, scaled_high, preferred_element_type=F32)
    half = shift.astype(F32) - 0.5 * now_product + 0.5 * corrected
    mixed = dot3(scaled, half, TN)
    gram = square + mixed + mixed.T
    reduced = eliminate(gram * (1.0 / total_rows))
    rows = lax.broadcasted_iota(jnp.int32, reduced.shape, 0)
    cols = lax.broadcasted_iota(jnp.int32, reduced.shape, 1)
    diagonal = jnp.sum(jnp.where(rows == cols, reduced, 0.0), axis=1, keepdims=True)
    root = lax.rsqrt(diagonal)
    rfactor_ref[...] = jnp.where(rows <= cols, reduced, 0.0) * root
    inverse = jnp.where(rows > cols, reduced, jnp.where(rows == cols, 1.0, 0.0)) * root
    residual = shifted_ref[...] - dot3(now_ref[...], scaled)
    basis_ref[...] = dot3(residual, inverse, NT)


def exchange(blocks, axis, steps):
    n = lax.axis_size(axis)
    assert n & (n - 1) == 0
    return [lax.ppermute(block, axis, [(i, i ^ step) for i in range(n)]) for step, block in zip(steps, blocks)]


def on_device(basis_now, basis_prev, coupling, tiles, tile_rows, tile_cols, tile_counts):
    rows_dev, width = basis_now.shape
    n_row, n_col = lax.axis_size("row"), lax.axis_size("col")
    devices = n_row * n_col
    tile_block = tiles[0, 0]
    total_rows = float(rows_dev * devices)
    piece = -(-2 * width // (8 * devices)) * 8
    smem = pl.BlockSpec(memory_space=pltpu.SMEM)
    vmem = pl.BlockSpec(memory_space=pltpu.VMEM)
    params = pltpu.CompilerParams(vmem_limit_bytes=48 * 1024 * 1024)

    in_hbm = [pltpu.with_memory_space_constraint(x, pltpu.HBM) for x in (basis_now, basis_prev, tile_rows, tile_cols, tile_block)]
    both, rows, cols, tile_block = pl.pallas_call(
        prepare_kernel,
        out_shape=(
            jax.ShapeDtypeStruct((2 * rows_dev, width), BF16),
            jax.ShapeDtypeStruct(tile_rows.shape, tile_rows.dtype),
            jax.ShapeDtypeStruct(tile_cols.shape, tile_cols.dtype),
            jax.ShapeDtypeStruct(tile_block.shape, tile_block.dtype),
        ),
        in_specs=[pl.BlockSpec(memory_space=pltpu.HBM)] * 5,
        out_specs=(vmem, vmem, vmem, vmem),
        scratch_shapes=[
            pltpu.VMEM(basis_now.shape, F32),
            pltpu.VMEM(basis_prev.shape, F32),
            pltpu.SemaphoreType.DMA((5,)),
        ],
        compiler_params=params,
        name="prepare",
    )(*in_hbm)
    gathered = lax.all_gather(both, "col", axis=0, tiled=True)
    me = jnp.stack([lax.axis_index("row"), lax.axis_index("col")])
    half = n_row // 2
    block = jax.ShapeDtypeStruct((rows_dev + piece, width), BF16)
    sums = jax.ShapeDtypeStruct((rows_dev + piece, width), F32)
    *blocks, far, own = pl.pallas_call(
        functools.partial(tiles_kernel, n_row, n_col, total_rows),
        out_shape=[block] * (2 * half - 2) + [sums] * 2,
        in_specs=[smem] * 3 + [vmem] * 4,
        out_specs=[vmem] * (2 * half),
        scratch_shapes=[
            pltpu.VMEM((n_row * rows_dev, width), F32),
            pltpu.VMEM((devices * piece, width), F32),
        ],
        compiler_params=params,
        name="tile_products",
    )(me, rows, cols, tile_counts, tile_block, gathered, coupling)
    mirrors = exchange(blocks[: half - 1], "row", distances(half))
    steps = near_distances(half)
    near = exchange(blocks[half - 1 : -1], "row", steps[:-1])
    mirror = pl.pallas_call(
        functools.partial(mirror_kernel, rows_dev),
        out_shape=block,
        in_specs=[vmem] * half,
        out_specs=vmem,
        compiler_params=params,
        name="mirror_sum",
    )(far, *mirrors)
    mirror, last = lax.optimization_barrier((mirror, blocks[-1]))
    across = exchange([mirror], "row", [half])
    near += exchange([last], "row", steps[-1:])

    shift = pl.pallas_call(
        shift_kernel,
        out_shape=jax.ShapeDtypeStruct((rows_dev, width), F32),
        in_specs=[vmem] * 2,
        out_specs=vmem,
        compiler_params=params,
        cost_estimate=pl.CostEstimate(flops=12 * rows_dev * width * width, bytes_accessed=12 * rows_dev * width, transcendentals=0),
        name="shift_by_previous",
    )(basis_prev, coupling)
    shifted, grams, early = pl.pallas_call(
        grams_kernel,
        out_shape=(
            jax.ShapeDtypeStruct((rows_dev, width), F32),
            jax.ShapeDtypeStruct((devices * piece, width), F32),
            jax.ShapeDtypeStruct((piece, width), F32),
        ),
        in_specs=[vmem] * (3 + half),
        out_specs=(vmem, vmem, vmem),
        compiler_params=params,
        name="local_grams",
    )(basis_now, shift, own, *near[:-1], *across, near[-1])
    everyone = ("row", "col")
    pieces = lax.all_to_all(grams.reshape(devices, piece, width), everyone, split_axis=0, concat_axis=0, tiled=True)
    copies = pl.pallas_call(
        spread_kernel,
        out_shape=jax.ShapeDtypeStruct((devices, 3 * piece, width), BF16),
        in_specs=[vmem, vmem],
        out_specs=vmem,
        compiler_params=params,
        name="sum_and_spread",
    )(pieces, early)
    gathered_sums = lax.all_to_all(copies, everyone, split_axis=0, concat_axis=0, tiled=True)
    return pl.pallas_call(
        functools.partial(final_kernel, total_rows),
        out_shape=(
            jax.ShapeDtypeStruct((rows_dev, width), F32),
            jax.ShapeDtypeStruct((width, width), F32),
            jax.ShapeDtypeStruct((width, width), F32),
        ),
        in_specs=[vmem] * 3,
        out_specs=(vmem, vmem, vmem),
        compiler_params=params,
        name="factor_and_basis",
    )(gathered_sums, basis_now, shifted)


def solution(mesh):
    placed = (
        P(("row", "col"), None),
        P(("row", "col"), None),
        P(),
        P("row", "col", None, None, None),
        P("row", "col", None),
        P("row", "col", None),
        P("row", "col"),
    )
    return jax.shard_map(
        on_device,
        mesh=mesh,
        in_specs=placed,
        out_specs=(P(("row", "col"), None), P(), P()),
        check_vma=False,
    )
```

```python
import functools

import jax
import jax.numpy as jnp
from jax import lax
from jax.experimental import pallas as pl
from jax.experimental.pallas import tpu as pltpu
from jax.sharding import PartitionSpec as P

F32 = jnp.float32
BF16 = jnp.bfloat16
NN, TN, NT = [(((x,), (y,)), ((), ())) for x, y in ((1, 0), (0, 0), (1, 1))]


def split(x):
    high = x.astype(BF16)
    return high, (x - high.astype(F32)).astype(BF16)


def dot3(a, b, dims=NN):
    (a_high, a_low), (b_high, b_low) = split(a), split(b)

    def one(x, y):
        return lax.dot_general(x, y, dims, preferred_element_type=F32)

    return one(a_high, b_low) + one(a_low, b_high) + one(a_high, b_high)


def upper_of(x):
    rows = lax.broadcasted_iota(jnp.int32, x.shape, 0)
    cols = lax.broadcasted_iota(jnp.int32, x.shape, 1)
    return jnp.where(rows <= cols, x, 0.0)


def distances(n):
    return [n - 1, *range(1, n - 1)]


def high_and_low(value):
    high = value.astype(BF16)
    low = (value - high.astype(F32)).astype(BF16)
    return jnp.concatenate([high, low], axis=0)


def sum_high_and_low(value):
    half = value.shape[-2] // 2
    value = value.astype(F32)
    return value[..., :half, :] + value[..., half:, :]


def prepare_kernel(now_hbm, prev_hbm, rows_hbm, cols_hbm, tiles_hbm, both_ref, rows_ref, cols_ref, tiles_ref, now_ref, prev_ref, sems):
    pairs = (
        (now_hbm, now_ref),
        (prev_hbm, prev_ref),
        (rows_hbm, rows_ref),
        (cols_hbm, cols_ref),
        (tiles_hbm, tiles_ref),
    )
    copies = [pltpu.make_async_copy(source, target, sems.at[k]) for k, (source, target) in enumerate(pairs)]
    for copy in copies:
        copy.start()
    rows_dev = now_ref.shape[0]
    copies[0].wait()
    both_ref[:rows_dev, :] = now_ref[...].astype(BF16)
    copies[1].wait()
    both_ref[rows_dev:, :] = prev_ref[...].astype(BF16)
    for copy in copies[2:]:
        copy.wait()


def tiles_kernel(n_row, n_col, total_rows, me_ref, rows_ref, cols_ref, count_ref, tiles_ref, basis_ref, coupling_ref, *refs):
    half = n_row // 2
    mirror_refs, near_refs, (far_ref, own_ref, total_ref, early_ref) = refs[: half - 1], refs[half - 1 : -4], refs[-4:]
    slots, size, _ = tiles_ref.shape
    width = total_ref.shape[1]
    rows_dev = total_ref.shape[0] // n_row
    piece = early_ref.shape[0] // (n_row * n_col)
    my_row, my_col = me_ref[0], me_ref[1]
    total_ref[...] = jnp.zeros_like(total_ref)
    grams = jnp.zeros((width, 2 * width), F32)
    for slab in range(n_col):
        now = basis_ref[2 * slab * rows_dev : (2 * slab + 1) * rows_dev, :]
        prev = basis_ref[(2 * slab + 1) * rows_dev : (2 * slab + 2) * rows_dev, :]
        grams += lax.dot_general(now, jnp.concatenate([now, prev], axis=1), TN, preferred_element_type=F32)
    square, cross = grams[:, :width], grams[:, width:]
    rows = lax.broadcasted_iota(jnp.int32, square.shape, 0)
    cols = lax.broadcasted_iota(jnp.int32, square.shape, 1)
    if early_ref.shape[0] > 2 * width:
        early_ref[...] = jnp.zeros_like(early_ref)
    early_ref[:width, :] = square - jnp.where(rows == cols, total_rows / n_row, 0.0)
    early_ref[width : 2 * width, :] = dot3(cross, upper_of(coupling_ref[...]), NT)
    used = count_ref[...]
    per_slab = rows_dev // size
    for slot in range(slots):
        col = cols_ref[0, 0, slot]
        start = pl.multiple_of((2 * per_slab * (col // per_slab) + lax.rem(col, per_slab)) * size, size)
        value = jnp.dot(tiles_ref[slot], basis_ref[pl.ds(start, size), :], preferred_element_type=F32)
        value = value * (slot < used).astype(F32)
        place = pl.ds(pl.multiple_of(rows_ref[0, 0, slot] * size, size), size)
        total_ref[place, :] += value

    def parts_of(row):
        slab = total_ref[pl.ds(pl.multiple_of(row * rows_dev, rows_dev), rows_dev), :]
        return slab, early_ref[pl.ds(pl.multiple_of((row * n_col + my_col) * piece, piece), piece), :]

    for step, mirror_ref, near_ref in zip(distances(half), mirror_refs, near_refs):
        write_block(mirror_ref, *parts_of(my_row ^ (step + half)))
        write_block(near_ref, *parts_of(my_row ^ step))
    for row, ref in ((my_row ^ half, far_ref), (my_row, own_ref)):
        ref[:rows_dev, :], ref[rows_dev:, :] = parts_of(row)


def write_block(ref, slab, early):
    rows_dev = slab.shape[0]
    ref[:rows_dev, :] = slab.astype(BF16)
    ref[rows_dev:, :] = early.astype(BF16)


def add_blocks(own_ref, block_refs, rows_dev):
    slab, early = own_ref[:rows_dev, :], own_ref[rows_dev:, :]
    for ref in block_refs:
        slab = slab + ref[:rows_dev, :].astype(F32)
        early = early + ref[rows_dev:, :].astype(F32)
    return slab, early


def mirror_kernel(rows_dev, own_ref, *refs):
    block_refs, out_ref = refs[:-1], refs[-1]
    write_block(out_ref, *add_blocks(own_ref, block_refs, rows_dev))


def shift_kernel(prev_ref, coupling_ref, shift_ref):
    shift_ref[...] = dot3(prev_ref[...], upper_of(coupling_ref[...]), NT)


def grams_kernel(now_ref, shift_ref, own_ref, *refs):
    block_refs, (shifted_ref, grams_ref, early_ref) = refs[:-3], refs[-3:]
    rows_dev, width = now_ref.shape
    product, early_ref[...] = add_blocks(own_ref, block_refs, rows_dev)
    shifted = product - shift_ref[...]
    shifted_ref[...] = shifted
    if grams_ref.shape[0] > 2 * width:
        grams_ref[...] = jnp.zeros_like(grams_ref)
    grams_ref[:width, :] = dot3(now_ref[...], product, TN)
    grams_ref[width : 2 * width, :] = dot3(shifted, shifted, TN)


def spread_kernel(parts_ref, early_ref, out_ref):
    total = parts_ref[0]
    for part in range(1, parts_ref.shape[0]):
        total = total + parts_ref[part]
    value = jnp.concatenate([high_and_low(total), early_ref[...].astype(BF16)], axis=0)
    for part in range(out_ref.shape[0]):
        out_ref[part] = value


def eliminate(gram):
    width = gram.shape[0]
    tall, block = 8, 16
    shape = (tall, width)
    lanes = lax.broadcasted_iota(jnp.int32, shape, 1)
    subs = lax.broadcasted_iota(jnp.int32, shape, 0)

    def cut(strip):
        return [strip[r : r + tall, :] for r in range(0, block, tall)]

    def column(parts, k):
        return [jnp.broadcast_to(part[:, k : k + 1], shape) for part in parts]

    def row(parts, k):
        part, k = parts[k // tall], k % tall
        return jnp.broadcast_to(part[k : k + 1, :], shape)

    strips = [cut(gram[r : r + block, :]) for r in range(0, width, block)]
    finished = []
    for first in range(0, width, block):
        panel, *strips = strips
        columns = [column(panel, first + j) for j in range(block)]
        kept = list(panel)
        for j in range(0, block, 2):
            mine = j // tall
            here, there = subs == j % tall, subs == j % tall + 1
            both = here | there
            lane, next_lane = lanes == first + j, lanes == first + j + 1
            left, right = columns[j], columns[j + 1]
            a, b, c = row(left, j), row(right, j), row(right, j + 1)
            scale = 1.0 / (a * c - b * b)
            by_top = [x * c - y * b for x, y in zip(left, right)]
            by_bottom = [y * a - x * b for x, y in zip(left, right)]
            by_top[mine] = jnp.where(here, -c, jnp.where(there, b, by_top[mine]))
            by_bottom[mine] = jnp.where(here, b, jnp.where(there, -a, by_bottom[mine]))

            def update(parts, up, down):
                rest = [jnp.where(both, 0.0, part) if k == mine else part for k, part in enumerate(parts)]
                return [x - (t * up + u * down) * scale for x, t, u in zip(rest, by_top, by_bottom)]

            top, bottom = row(panel, j), row(panel, j + 1)
            ratio = b / a
            second = jnp.where(lane, -ratio, bottom - ratio * top)
            kept[mine] = jnp.where(here, top, jnp.where(there, second, kept[mine]))
            pair = lane | next_lane
            top = jnp.where(lane, 1.0, jnp.where(next_lane, 0.0, top))
            bottom = jnp.where(lane, 0.0, jnp.where(next_lane, 1.0, bottom))
            panel = update([jnp.where(pair, 0.0, part) for part in panel], top, bottom)
            for m in range(j + 2, block):
                columns[m] = update(columns[m], row(columns[m], j), row(columns[m], j + 1))
        finished += kept
        if strips:
            rows = [row(panel, m) for m in range(block)]
            inside = (lanes >= first) & (lanes < first + block)
            factors = [column(strips[0], first + m) for m in range(block)]
            for k in range(len(panel)):
                terms = [factor[k] * value for factor, value in zip(factors, rows)]
                while len(terms) > 1:
                    terms = [x + y for x, y in zip(terms[::2], terms[1::2])]
                strips[0][k] = jnp.where(inside, 0.0, strips[0][k]) - terms[0]
        if len(strips) > 1:
            below = jnp.concatenate([part for strip in strips[1:] for part in strip], axis=0)
            solved = [jnp.zeros((first, width), F32)] if first else []
            solved = jnp.concatenate(solved + panel + [jnp.zeros((width - first - block, width), F32)], axis=0)
            cols = lax.broadcasted_iota(jnp.int32, below.shape, 1)
            below = jnp.where((cols >= first) & (cols < first + block), 0.0, below) - dot3(below, solved)
            strips[1:] = [cut(below[r : r + block, :]) for r in range(0, below.shape[0], block)]
    return jnp.concatenate(finished, axis=0)


def final_kernel(total_rows, pieces_ref, now_ref, shifted_ref, basis_out, projection_out, rfactor_out, basis_ref, projection_ref, rfactor_ref, sems):
    width = now_ref.shape[1]
    piece = pieces_ref.shape[1] // 3
    pieces = pieces_ref[...]
    late = sum_high_and_low(pieces[:, : 2 * piece, :]).reshape(-1, width)
    early = pieces[:, 2 * piece :, :].reshape(-1, width)
    now_product, square = late[:width], late[width : 2 * width]
    now_square, shift = early[:width], early[width : 2 * width]
    projection = now_product * total_rows**-0.5
    projection_ref[...] = projection
    copies = [pltpu.make_async_copy(projection_ref, projection_out, sems.at[0])]
    copies[0].start()
    scaled = now_product * (1.0 / total_rows)
    scaled_high, scaled_low = split(scaled)
    corrected = jnp.dot(now_square, scaled_low, preferred_element_type=F32)
    corrected += jnp.dot(now_square, scaled_high, preferred_element_type=F32)
    half = shift.astype(F32) - 0.5 * now_product + 0.5 * corrected
    mixed = dot3(scaled, half, TN)
    gram = square + mixed + mixed.T
    reduced = eliminate(gram * (1.0 / total_rows))
    rows = lax.broadcasted_iota(jnp.int32, reduced.shape, 0)
    cols = lax.broadcasted_iota(jnp.int32, reduced.shape, 1)
    diagonal = jnp.sum(jnp.where(rows == cols, reduced, 0.0), axis=1, keepdims=True)
    root = lax.rsqrt(diagonal)
    rfactor_ref[...] = jnp.where(rows <= cols, reduced, 0.0) * root
    copies.append(pltpu.make_async_copy(rfactor_ref, rfactor_out, sems.at[1]))
    copies[1].start()
    inverse = jnp.where(rows > cols, reduced, jnp.where(rows == cols, 1.0, 0.0)) * root
    residual = shifted_ref[...] - dot3(now_ref[...], scaled)
    part = residual.shape[0] // 2
    for k in range(2):
        place = pl.ds(k * part, part)
        basis_ref[place, :] = dot3(residual[k * part : (k + 1) * part], inverse, NT)
        copies.append(pltpu.make_async_copy(basis_ref.at[place], basis_out.at[place], sems.at[2 + k]))
        copies[-1].start()
    for copy in copies:
        copy.wait()


def exchange(blocks, axis, steps):
    n = lax.axis_size(axis)
    assert n & (n - 1) == 0
    return [lax.ppermute(block, axis, [(i, i ^ step) for i in range(n)]) for step, block in zip(steps, blocks)]


def on_device(basis_now, basis_prev, coupling, tiles, tile_rows, tile_cols, tile_counts):
    rows_dev, width = basis_now.shape
    n_row, n_col = lax.axis_size("row"), lax.axis_size("col")
    devices = n_row * n_col
    tile_block = tiles[0, 0]
    total_rows = float(rows_dev * devices)
    piece = -(-2 * width // (8 * devices)) * 8
    smem = pl.BlockSpec(memory_space=pltpu.SMEM)
    vmem = pl.BlockSpec(memory_space=pltpu.VMEM)
    params = pltpu.CompilerParams(vmem_limit_bytes=48 * 1024 * 1024)

    in_hbm = [pltpu.with_memory_space_constraint(x, pltpu.HBM) for x in (basis_now, basis_prev, tile_rows, tile_cols, tile_block)]
    both, rows, cols, tile_block = pl.pallas_call(
        prepare_kernel,
        out_shape=(
            jax.ShapeDtypeStruct((2 * rows_dev, width), BF16),
            jax.ShapeDtypeStruct(tile_rows.shape, tile_rows.dtype),
            jax.ShapeDtypeStruct(tile_cols.shape, tile_cols.dtype),
            jax.ShapeDtypeStruct(tile_block.shape, tile_block.dtype),
        ),
        in_specs=[pl.BlockSpec(memory_space=pltpu.HBM)] * 5,
        out_specs=(vmem, vmem, vmem, vmem),
        scratch_shapes=[
            pltpu.VMEM(basis_now.shape, F32),
            pltpu.VMEM(basis_prev.shape, F32),
            pltpu.SemaphoreType.DMA((5,)),
        ],
        compiler_params=params,
        name="prepare",
    )(*in_hbm)
    gathered = lax.all_gather(both, "col", axis=0, tiled=True)
    me = jnp.stack([lax.axis_index("row"), lax.axis_index("col")])
    half = n_row // 2
    block = jax.ShapeDtypeStruct((rows_dev + piece, width), BF16)
    sums = jax.ShapeDtypeStruct((rows_dev + piece, width), F32)
    *blocks, far, own = pl.pallas_call(
        functools.partial(tiles_kernel, n_row, n_col, total_rows),
        out_shape=[block] * (2 * half - 2) + [sums] * 2,
        in_specs=[smem] * 3 + [vmem] * 4,
        out_specs=[vmem] * (2 * half),
        scratch_shapes=[
            pltpu.VMEM((n_row * rows_dev, width), F32),
            pltpu.VMEM((devices * piece, width), F32),
        ],
        compiler_params=params,
        name="tile_products",
    )(me, rows, cols, tile_counts, tile_block, gathered, coupling)
    steps = distances(half)
    mirrors = exchange(blocks[: half - 1], "row", steps)
    near = exchange(blocks[half - 1 : -1], "row", steps[:-1])
    mirror = pl.pallas_call(
        functools.partial(mirror_kernel, rows_dev),
        out_shape=block,
        in_specs=[vmem] * half,
        out_specs=vmem,
        compiler_params=params,
        name="mirror_sum",
    )(far, *mirrors)
    mirror, last = lax.optimization_barrier((mirror, blocks[-1]))
    across = exchange([mirror], "row", [half])
    near += exchange([last], "row", steps[-1:])

    shift = pl.pallas_call(
        shift_kernel,
        out_shape=jax.ShapeDtypeStruct((rows_dev, width), F32),
        in_specs=[vmem] * 2,
        out_specs=vmem,
        compiler_params=params,
        cost_estimate=pl.CostEstimate(flops=12 * rows_dev * width * width, bytes_accessed=12 * rows_dev * width, transcendentals=0),
        name="shift_by_previous",
    )(basis_prev, coupling)
    shifted, grams, early = pl.pallas_call(
        grams_kernel,
        out_shape=(
            jax.ShapeDtypeStruct((rows_dev, width), F32),
            jax.ShapeDtypeStruct((devices * piece, width), F32),
            jax.ShapeDtypeStruct((piece, width), F32),
        ),
        in_specs=[vmem] * (3 + half),
        out_specs=(vmem, vmem, vmem),
        compiler_params=params,
        name="local_grams",
    )(basis_now, shift, own, *near[:-1], *across, near[-1])
    everyone = ("row", "col")
    pieces = lax.all_to_all(grams.reshape(devices, piece, width), everyone, split_axis=0, concat_axis=0, tiled=True)
    copies = pl.pallas_call(
        spread_kernel,
        out_shape=jax.ShapeDtypeStruct((devices, 3 * piece, width), BF16),
        in_specs=[vmem, vmem],
        out_specs=vmem,
        compiler_params=params,
        name="sum_and_spread",
    )(pieces, early)
    gathered_sums = lax.all_to_all(copies, everyone, split_axis=0, concat_axis=0, tiled=True)
    return pl.pallas_call(
        functools.partial(final_kernel, total_rows),
        out_shape=(
            jax.ShapeDtypeStruct((rows_dev, width), F32),
            jax.ShapeDtypeStruct((width, width), F32),
            jax.ShapeDtypeStruct((width, width), F32),
        ),
        in_specs=[vmem] * 3,
        out_specs=[pl.BlockSpec(memory_space=pl.ANY)] * 3,
        scratch_shapes=[
            pltpu.VMEM((rows_dev, width), F32),
            pltpu.VMEM((width, width), F32),
            pltpu.VMEM((width, width), F32),
            pltpu.SemaphoreType.DMA((4,)),
        ],
        compiler_params=params,
        name="factor_and_basis",
    )(gathered_sums, basis_now, shifted)


def solution(mesh):
    placed = (
        P(("row", "col"), None),
        P(("row", "col"), None),
        P(),
        P("row", "col", None, None, None),
        P("row", "col", None),
        P("row", "col", None),
        P("row", "col"),
    )
    return jax.shard_map(
        on_device,
        mesh=mesh,
        in_specs=placed,
        out_specs=(P(("row", "col"), None), P(), P()),
        check_vma=False,
    )
```
